32 devices in a mesh: rep: 16 (over z, x, core), head: 2 (over y).
Axes of the slice: x: 2, y: 2, z: 4, core: 2. Of those that a mesh axis runs over, the one named last changes fastest.
Arguments:
- states: float32 [32, 8, 128, 128], P('rep', 'head'), may hold values from -4 to 4
- conv_states: bfloat16 [32, 3, 3, 1024], P('rep', None, None, 'head'), may hold values from -6 to 6
- projected: bfloat16 [6, 32, 3, 1024], P(None, 'rep', None, 'head'), may hold values from -6 to 6
- conv_weight: float32 [4, 3, 1024], P(None, None, 'head'), may hold values from -3 to 3
- decay_input: float32 [6, 32, 1024], P(None, 'rep', 'head'), may hold values from -6 to 6
- decay_rate: float32 [8], P('head'), may hold values from 0.05 to 2
- beta_logit: float32 [6, 32, 8], P(None, 'rep', 'head'), may hold values from -6 to 6
- out_gate: bfloat16 [6, 32, 1024], P(None, 'rep', 'head'), may hold values from -6 to 6
- norm_gain: float32 [128], replicated, may hold values from 0.25 to 1.75
- out_weight: bfloat16 [1024, 2304], P('head'), may hold values from -0.25 to 0.25
- destinations: int32 [6, 32], replicated, may hold values from 0 to 31, as said below
- live_counts: int32 [6, 16], P(None, 'rep'), may hold values from 1 to 2
Outputs:
- layer_out: bfloat16 [6, 32, 2304], P(None, 'rep', 'head')
- states_out: float32 [32, 8, 128, 128], P('rep', 'head')
- conv_out: bfloat16 [32, 3, 3, 1024], P('rep', None, None, 'head')
The draws below stay inside these ranges and needn't reach their ends.
Inputs may be any that keep to these rules, and one draw needn't show every extreme that they name: For each step t, destinations[t] is a permutation of the 32 slots; slot g belongs to replica group g // 2. In every step, the number of slots g of each group with destinations[t, g] != g is exactly 1.
All inputs are finite; a program needn't handle non-finite values.
Results may differ from the reference program's by a relative error of at most 0.015.
Values may be sent and summed in bfloat16 or wider, within the bound.
No kernel may reach another device: no remote copies, remote signals or barrier semaphores. Data moves between devices by JAX's collectives and lax.ppermute only.
A program may use at most 128 MiB of HBM per device.

```python
import math
import jax
import jax.numpy as jnp
from jax import lax

D = 2304
DK = 128
TAPS = 4
ROWS_DEV = 2
MOVE = 1
STEPS = 6
HEADS = 8
GROUPS = 16
ROWS_TOTAL = 32


def group_movers(key, group_total):
    keys = jax.random.split(key, group_total)
    picked = jax.vmap(lambda single: jax.random.permutation(single, ROWS_DEV)[:MOVE])(keys)
    return (jnp.arange(group_total, dtype=jnp.int32)[:, None] * ROWS_DEV + picked.astype(jnp.int32)).reshape(-1)


def draw_destinations(key, part):
    key = jax.random.fold_in(key, 7)
    group_total = ROWS_TOTAL // ROWS_DEV
    stacked = []
    for step_id in range(STEPS):
        step_key = jax.random.fold_in(key, step_id)
        first_key, second_key = jax.random.split(step_key)
        movers = group_movers(first_key, group_total)
        ordering = movers[jax.random.permutation(second_key, group_total * MOVE)]
        mapping = jnp.arange(ROWS_TOTAL, dtype=jnp.int32).at[ordering].set(jnp.roll(ordering, -1))
        stacked.append(mapping.astype(jnp.int32))
    return jnp.stack(stacked)


def with_ends(drawn, rng, least, largest):
    shape = drawn.shape
    index_at = [jax.random.randint(jax.random.fold_in(rng, axis), (), 0, shape[axis]) for axis in range(len(shape))]
    drawn = drawn.at[tuple(index_at)].set(least)
    longest = shape.index(max(shape))
    index_at[longest] = (index_at[longest] + 1) % shape[longest]
    return drawn.at[tuple(index_at)].set(largest)


def raised(result, rng, source, target, blocks, factor):
    def block_of(position):
        return (jnp.arange(result.shape[position]) // (result.shape[position] // blocks)).reshape((-1,) + (1,) * (result.ndim - 1 - position))

    first = jax.random.permutation(rng, blocks)[block_of(target)]
    second = (block_of(target) + blocks // 2) % blocks
    return jnp.where((block_of(source) == first) | (block_of(source) == second), factor * result, result)


def block_levels(stream_key, shape, pieces, least, largest):
    loudness, own = 1.0, jax.random.fold_in(stream_key, 6)
    for axis_at, blocks in pieces:
        draws = jnp.exp(jax.random.uniform(jax.random.fold_in(own, axis_at), (blocks,), jnp.float32, least / len(pieces), largest / len(pieces)))
        loudness = loudness * jnp.repeat(draws, shape[axis_at] // blocks).reshape([-1 if axis == axis_at else 1 for axis in range(len(shape))])
    return loudness


def bell_draw(rng, shape, width, reach, shards=(), kind=jnp.bfloat16):
    result = width * jax.random.normal(rng, shape, jnp.float32)
    if shards:
        result = result * block_levels(rng, shape, shards, -0.22, 0.18)
    return jnp.clip(result, -reach, reach).astype(kind)


def heavy_noise(rng, extent, width, reach, shards, heavy, kind=jnp.bfloat16):
    array = width * jax.random.normal(rng, extent, jnp.float32)
    if shards:
        array = array * block_levels(rng, extent, shards, -0.22, 0.18)
    return jnp.clip(raised(array, jax.random.fold_in(rng, 3), *heavy), -reach, reach).astype(kind)


def setup_inputs(seed: int = 0) -> dict:
    splits = jax.random.split(jax.random.key(seed), 13)
    return {
        "states": bell_draw(splits[0], (ROWS_TOTAL, HEADS, DK, DK), 0.5, 4.0, ((0, 16), (1, 2)), jnp.float32),
        "conv_states": bell_draw(splits[1], (ROWS_TOTAL, TAPS - 1, 3, HEADS * DK), 1.0, 6.0, ((0, 16), (3, 2))),
        "projected": bell_draw(splits[2], (STEPS, ROWS_TOTAL, 3, HEADS * DK), 1.0, 6.0, ((1, 16), (3, 2))),
        "conv_weight": bell_draw(splits[3], (TAPS, 3, HEADS * DK), 0.6, 3.0, ((2, 2),), jnp.float32),
        "decay_input": bell_draw(splits[4], (STEPS, ROWS_TOTAL, HEADS * DK), 1.5, 6.0, ((1, 16), (2, 2)), jnp.float32),
        "decay_rate": jnp.clip(jnp.exp(math.log(2.0) - 3.6888794 * jax.random.uniform(splits[5], (HEADS,), jnp.float32) ** block_levels(splits[5], (HEADS,), ((0, 2),), -0.2, 0.2)), 0.05, 2.0),
        "beta_logit": bell_draw(splits[6], (STEPS, ROWS_TOTAL, HEADS), 1.5, 6.0, ((1, 16), (2, 2)), jnp.float32),
        "out_gate": bell_draw(splits[7], (STEPS, ROWS_TOTAL, HEADS * DK), 1.5, 6.0, ((1, 16), (2, 2))),
        "norm_gain": jnp.clip(1.0 + 0.15 * jax.random.normal(splits[8], (DK,), jnp.float32), 0.25, 1.75),
        "out_weight": heavy_noise(splits[9], (HEADS * DK, D), (HEADS * DK) ** -0.5, 0.25, ((0, 2),), (0, 1, 2, 2.0)),
        "destinations": draw_destinations(jax.random.fold_in(splits[12], 71), 0),
        "live_counts": with_ends(jax.random.randint(splits[11], (STEPS, GROUPS), 1, ROWS_DEV + 1), jax.random.fold_in(splits[11], 1), 1, ROWS_DEV).astype(jnp.int32),
    }


EPSILON = 1e-06

def unit_rows(vectors):
    return vectors / jnp.sqrt(lax.optimization_barrier(jnp.sum(vectors * vectors, axis=-1, keepdims=True)) + EPSILON)

def head_update(carried):
    memory, query, key_vec, value_vec, retain, strength = carried
    decayed = retain[:, :, None] * memory
    recalled = lax.optimization_barrier(jnp.sum(key_vec[:, :, None] * decayed, axis=1))
    updated = decayed + strength[:, None, None] * key_vec[:, :, None] * (value_vec - recalled)[:, None, :]
    readout = lax.optimization_barrier(jnp.sum(query[:, :, None] * updated, axis=1)) * DK ** (-0.5)
    return (updated, readout)

def reference(states, conv_states, projected, conv_weight, decay_input, decay_rate, beta_logit, out_gate, norm_gain, out_weight, destinations, live_counts):
    memory = jnp.moveaxis(states, 1, 0)
    history = conv_states
    slot_ids = jnp.arange(ROWS_TOTAL, dtype=jnp.int32)
    results = []
    for step_id in range(STEPS):
        source = jnp.zeros((ROWS_TOTAL,), jnp.int32).at[destinations[step_id]].set(slot_ids)
        memory = memory[:, source]
        history = history[source]
        alive = slot_ids % ROWS_DEV < jnp.repeat(live_counts[step_id], ROWS_DEV)
        window = jnp.concatenate([history.astype(jnp.float32), projected[step_id][:, None].astype(jnp.float32)], axis=1)
        summed = window[:, 0] * conv_weight[0]
        for tap_id in range(1, TAPS):
            summed = summed + window[:, tap_id] * conv_weight[tap_id]
        activated = jax.nn.silu(summed)
        shifted = window[:, 1:].astype(jnp.bfloat16)
        query = unit_rows(activated[:, 0].reshape(ROWS_TOTAL, HEADS, DK))
        key_vec = unit_rows(activated[:, 1].reshape(ROWS_TOTAL, HEADS, DK))
        value_vec = activated[:, 2].reshape(ROWS_TOTAL, HEADS, DK)
        retain = jnp.exp(-decay_rate[None, :, None] * jax.nn.softplus(decay_input[step_id].reshape(ROWS_TOTAL, HEADS, DK)))
        strength = jax.nn.sigmoid(beta_logit[step_id])
        updated, readout = lax.map(head_update, (memory, jnp.moveaxis(query, 1, 0), jnp.moveaxis(key_vec, 1, 0), jnp.moveaxis(value_vec, 1, 0), jnp.moveaxis(retain, 1, 0), jnp.moveaxis(strength, 1, 0)))
        memory = jnp.where(alive[None, :, None, None], updated, memory)
        history = jnp.where(alive[:, None, None, None], shifted, history)
        readout = jnp.moveaxis(readout, 0, 1)
        scaling = lax.rsqrt(lax.optimization_barrier(jnp.mean(readout * readout, axis=-1, keepdims=True)) + EPSILON)
        gates = jax.nn.sigmoid(out_gate[step_id].astype(jnp.float32).reshape(ROWS_TOTAL, HEADS, DK))
        gated = readout * scaling * norm_gain * gates
        gated = jnp.where(alive[:, None, None], gated, jnp.zeros_like(gated)).astype(jnp.bfloat16).reshape(ROWS_TOTAL, HEADS * DK)
        results.append(jnp.dot(gated, out_weight, preferred_element_type=jnp.float32).astype(jnp.bfloat16))
    return (jnp.stack(results), jnp.moveaxis(memory, 0, 1), history)
```

```python
import functools

import jax
import jax.numpy as jnp
from jax import lax
from jax.experimental import pallas as pl
from jax.experimental.pallas import tpu as pltpu
from jax.sharding import PartitionSpec as P

EPSILON = 1e-06
LANES = 128
VMEM_LIMIT = 32 * 1024 * 1024
F32 = jnp.float32
BF16 = jnp.bfloat16


def round_up(value, multiple):
    return -(-value // multiple) * multiple


class Sizes:
    def __init__(self, group_total, states, conv_states, projected):
        self.groups = n = group_total
        self.rows, self.heads, self.dk, _ = states.shape
        self.taps, self.parts = conv_states.shape[1:3]
        self.steps = projected.shape[0]
        self.slots = n * self.rows
        self.cuts = n // self.heads
        far = [*range(0, self.heads, 2), *range(1, self.heads, 2)]
        self.order = [h * self.cuts + cut for cut in range(self.cuts) for h in far]
        self.place_of = [self.order.index(p) for p in range(n)]
        self.cols = self.dk // self.cuts
        self.state_rows = self.rows * self.cols
        self.quarter = self.dk // 4
        self.decay_at = self.steps * 2 * self.rows
        self.hist_at = self.decay_at + self.steps * self.rows
        self.value_at = self.hist_at + self.taps * 2 * self.rows
        self.value_depth = -(-(self.steps + self.taps) // 4)
        self.flag_at = self.value_depth * self.rows
        self.tail_rows = round_up(self.flag_at + self.rows, 8)
        self.info_rows = self.value_at + self.tail_rows
        self.back_sets = self.steps + self.taps * self.parts
        self.back_depth = -(-self.back_sets // 4)
        self.back_rows = round_up(self.back_depth * self.rows, 8)
        self.whole_tiles = self.cols % 16 == 0
        self.width = max(LANES, 8 * self.cols)
        self.tile = self.width // self.cols


def mod(value, size):
    return value & (size - 1) if size & (size - 1) == 0 else lax.rem(value, size)


def quotient(value, size):
    if size & (size - 1) == 0:
        return lax.shift_right_logical(value, jnp.int32(size.bit_length() - 1))
    return lax.div(value, jnp.int32(size))


def in_block(sz, shape, cut, shift):
    start = cut * sz.cols + shift * sz.quarter
    return mod(iota(shape, len(shape) - 1) + (2 * sz.dk - start), sz.dk) < sz.cols


def iota(shape, dim):
    return lax.broadcasted_iota(jnp.int32, shape, dim)


def one_hot(condition):
    return jnp.where(condition, 1.0, 0.0).astype(BF16)


def dot(lhs, rhs, lhs_dim=1, rhs_dim=0):
    return lax.dot_general(
        lhs, rhs, (((lhs_dim,), (rhs_dim,)), ((), ())), preferred_element_type=F32
    )


def pack_kernel(sz, *refs):
    count = 8
    sources, states_hbm = refs[:count], refs[count]
    pieces, pick, place, final, taps = refs[count + 1 : count + 6]
    scratch = refs[count + 6 :]
    targets, live, rate, beta, proj, hist, decay, filters, states = scratch[: count + 1]
    info, tails, strengths, in_sems = scratch[count + 1 :]
    copies = []

    def start(source, target):
        copies.append(pltpu.make_async_copy(source, target, in_sems.at[len(copies)]))
        copies[-1].start()

    for source, target in zip(sources, scratch):
        start(source, target)
    for r in range(sz.rows):
        for h in range(sz.heads):
            start(states_hbm.at[r, h], states.at[r, h])
    for copy in copies:
        copy.wait()
    route(sz, targets, pick, place, final)
    own_head = lax.axis_index("rep") // sz.cuts
    head_lanes = pl.ds(pl.multiple_of(own_head * sz.dk, sz.dk), sz.dk)
    for part in range(sz.parts):
        taps[part] = filters[part, :, head_lanes]
    channels, dk = sz.heads * sz.dk, sz.dk
    lane_head = quotient(iota((1, channels), 1), dk)
    rates = jnp.zeros((1, channels), F32)
    for h in range(sz.heads):
        rates = jnp.where(lane_head == h, rate[:, h : h + 1], rates)
    row_ids = iota((sz.rows, channels), 0)

    def keep(target, at, value):
        for h in range(sz.heads):
            target[h, at : at + sz.rows, :] = value[:, h * dk : (h + 1) * dk]

    tails[...] = jnp.zeros(tails.shape, F32)

    def keep_value(index, value):
        shift = index // sz.value_depth
        at = index % sz.value_depth * sz.rows
        for h in range(sz.heads):
            own = value[:, h * dk : (h + 1) * dk]
            if shift:
                own = pltpu.roll(own, shift * sz.quarter, 1)
            tails[shift, h, at : at + sz.rows, :] = own

    for t in range(sz.steps):
        for part in range(2):
            keep(info, (t * 2 + part) * sz.rows, proj[t, part].astype(F32))
        keep_value(t, proj[t, 2].astype(F32))
        x = decay[t]
        softplus = jnp.maximum(x, 0.0) + jnp.log1p(jnp.exp(-jnp.abs(x)))
        keep(
            info,
            sz.decay_at + t * sz.rows,
            jnp.where(row_ids < live[:, t : t + 1], rates * softplus, 0.0),
        )
    for tap in range(sz.taps):
        for part in range(2):
            keep(info, sz.hist_at + (tap * 2 + part) * sz.rows, hist[tap, part].astype(F32))
        keep_value(sz.steps + tap, hist[tap, 2].astype(F32))
    lane = iota((sz.heads, dk), 1)
    strengths[...] = jnp.zeros(strengths.shape, F32)
    for r in range(sz.rows):
        strengths[:, : sz.steps] = beta[r]
        lives = jnp.zeros((sz.heads, dk), F32)
        for t in range(sz.steps):
            lives = jnp.where((lane == t) & (r < live[:, t : t + 1]), 1.0, lives)
        strength = lives / (1.0 + jnp.exp(-strengths[...]))
        high = strength.astype(BF16).astype(F32)
        flags = high + pltpu.roll(lives, 16, 1) + pltpu.roll(strength - high, 32, 1)
        for h in range(sz.heads):
            at = sz.flag_at + r
            for shift in range(4):
                tails[shift, h, at : at + 1, :] = flags[h : h + 1]
    blocks = [
        [in_block(sz, (sz.tail_rows, dk), cut, shift) for shift in range(1, 4)]
        for cut in range(sz.cuts)
    ]
    for h in range(sz.heads):
        head = info[h].astype(BF16)
        across = [states[r, h].T for r in range(sz.rows)]
        for cut in range(sz.cuts):
            p, at = h * sz.cuts + cut, cut * sz.cols
            own = [a[at : at + sz.cols] for a in across]
            pieces[p, : sz.state_rows, :] = jnp.concatenate(own, axis=0).astype(BF16)
            pieces[p, sz.state_rows : sz.state_rows + sz.value_at, :] = head
            tail = tails[0, h]
            for shift in range(1, 4):
                tail = jnp.where(blocks[cut][shift - 1], tails[shift, h], tail)
            pieces[p, sz.state_rows + sz.value_at :, :] = tail.astype(BF16)


def route(sz, targets, pick, place, final):
    n, T = sz.slots, sz.steps

    def label(slot):
        return mod(slot, sz.rows) * sz.groups + quotient(slot, sz.rows)

    to_label = one_hot(label(iota((n, n), 0)) == iota((n, n), 1))
    ordered = dot(targets[...].astype(F32).astype(BF16), to_label)
    ordered = label((ordered + 0.5).astype(jnp.int32))
    steps = [one_hot(iota((n, n), 0) == ordered[t : t + 1]) for t in range(T)]
    chain = [steps[0]]
    for t in range(1, T):
        if t % 2:
            pair = dot(steps[t], steps[t - 1]).astype(BF16)
            chain.append(dot(pair, chain[t - 2]).astype(BF16) if t > 1 else pair)
        else:
            chain.append(dot(steps[t], chain[t - 1]).astype(BF16))
    for t in range(T):
        place[t] = chain[t]
        pick[t] = chain[t].astype(F32).T.astype(BF16)
    slot = iota((8, n), 1)
    row, group = quotient(slot, sz.groups), mod(slot, sz.groups)
    head, cut = quotient(group, sz.cuts), mod(group, sz.cuts)
    far = quotient(head, 2) + mod(head, 2) * ((sz.heads + 1) // 2)
    weights = (cut * sz.heads + far) * sz.rows + row
    places = dot(weights.astype(F32).astype(BF16), chain[T - 1])
    final[...] = (places + 0.5).astype(jnp.int32)


def gate_factor(sz, live, gain, gate, factor):
    channels = sz.heads * sz.dk
    gains = jnp.concatenate([gain[...]] * sz.heads, axis=1)
    row = iota((sz.rows, channels), 0)
    factor[...] = jnp.zeros(factor.shape, F32)
    for t in range(sz.steps):
        gates = gains / (1.0 + jnp.exp(-gate[t].astype(F32)))
        factor[t * sz.rows : (t + 1) * sz.rows, :] = jnp.where(
            row < live[:, t : t + 1], gates, 0.0
        )


def step_kernel(sz, filters, pick, place, came, *refs):
    count = sz.groups
    sources, sent, factor, scratch = refs[:4], refs[4], refs[5], refs[6:]
    scalars, live, gain, gate, info, later, back, sems = scratch
    copies = []
    for i, (source, target) in enumerate(zip(sources, scratch)):
        copies.append(pltpu.make_async_copy(source, target, sems.at[i]))
        copies[-1].start()
    n, dk, T = sz.slots, sz.dk, sz.steps
    mine = lax.axis_index("rep")
    cut = lax.rem(mine, sz.cuts)
    stride = sz.info_rows
    for g in range(count):
        info[g * stride : (g + 1) * stride, :] = came[g, sz.state_rows :, :].astype(F32)

    def gather(at):
        return jnp.concatenate(
            [info[pl.ds(at + r, count, stride=stride), :] for r in range(sz.rows)], axis=0
        )

    def gather_value(index):
        value = gather(sz.value_at + index % sz.value_depth * sz.rows)
        shift = index // sz.value_depth
        return pltpu.roll(value, sz.dk - shift * sz.quarter, 1) if shift else value

    weights = [filters[part] for part in range(sz.parts)]
    flags = gather(sz.value_at + sz.flag_at)
    window = [
        [gather(sz.hist_at + (tap * 2 + part) * sz.rows) for part in range(2)]
        + [gather_value(T + tap)]
        for tap in range(sz.taps)
    ]
    reach = jnp.ones((n, dk), F32)
    keys = []
    from_state, values, strengths, key_mix, read_mix = [], [], [], [], []
    for t in range(T):
        slots = [gather((t * 2 + part) * sz.rows) for part in range(2)]
        slots += [gather_value(t), gather(sz.decay_at + t * sz.rows), flags]
        moved = dot(pick[t], jnp.concatenate(slots, axis=1).astype(BF16))
        inputs = [moved[:, i * dk : (i + 1) * dk] for i in range(sz.parts + 2)]
        moved_flags = inputs[sz.parts + 1]
        strength = moved_flags[:, t : t + 1] + moved_flags[:, 32 + t : 33 + t]
        alive = moved_flags[:, 16 + t : 17 + t] > 0.5
        active = []
        for part in range(sz.parts):
            frames = [window[tap][part] for tap in range(sz.taps)] + [inputs[part]]
            total = frames[0] * weights[part][:1]
            for j in range(1, sz.taps + 1):
                total = total + frames[j] * weights[part][j : j + 1]
            active.append(total / (1.0 + jnp.exp(-total)))
            for tap in range(sz.taps):
                window[tap][part] = jnp.where(alive, frames[tap + 1], frames[tap])
        query, key = (
            x * lax.rsqrt(jnp.sum(x * x, axis=1, keepdims=True) + EPSILON) for x in active[:2]
        )
        retain = jnp.exp(-inputs[sz.parts])
        reach = reach * retain
        keys = [k * retain for k in keys]
        key_mix.append([jnp.sum(key * k, axis=1, keepdims=True) for k in keys])
        keys.append(key)
        read_mix.append([jnp.sum(query * k, axis=1, keepdims=True) for k in keys])
        from_state += [reach * key, reach * query]
        values.append(active[2])
        strengths.append(strength)

    spread = one_hot(
        iota((dk, sz.width), 0) == cut * sz.cols + mod(iota((dk, sz.width), 1), sz.cols)
    )
    value_cols = dot(jnp.concatenate(values, axis=0).astype(BF16), spread)
    for copy in copies:
        copy.wait()
    gate_factor(sz, live, gain, gate, factor)
    lane_row = quotient(iota((sz.tile, sz.width), 1), sz.cols)
    own = iota((sz.tile, sz.width), 0) == lane_row
    readouts = [[] for _ in range(T)]
    for at in range(0, n, sz.tile):
        r, g = at // count, at % count
        rows = slice(at, at + sz.tile)
        if sz.whole_tiles:
            block = [
                came[g + i, r * sz.cols : (r + 1) * sz.cols, :] for i in range(sz.tile)
            ]
        else:
            block = [
                came[g + i, : sz.state_rows, :].astype(F32)[r * sz.cols : (r + 1) * sz.cols]
                for i in range(sz.tile)
            ]
        seen = dot(
            jnp.concatenate([x[rows] for x in from_state], axis=0).astype(BF16),
            jnp.concatenate(block, axis=0).astype(BF16),
            1,
            1,
        )
        seen = [seen[i * sz.tile : (i + 1) * sz.tile] for i in range(2 * T)]
        writes = []
        for t in range(T):
            target = value_cols[t * n + at : t * n + at + sz.tile] - seen[2 * t]
            target = jnp.where(own, target, 0.0)
            for s in range(t):
                target = target - key_mix[t][s][rows] * writes[s]
            writes.append(strengths[t][rows] * target)
            read = jnp.where(own, seen[2 * t + 1], 0.0)
            for s in range(t + 1):
                read = read + read_mix[t][s][rows] * writes[s]
            readouts[t].append(read * dk ** (-0.5))
        added = dot(
            jnp.concatenate(writes, axis=0).astype(BF16),
            jnp.concatenate([k[rows] for k in keys], axis=0).astype(BF16),
            0,
            0,
        )
        for i in range(sz.tile):
            part = block[i].astype(F32) * reach[at + i : at + i + 1]
            part = part + added[i * sz.cols : (i + 1) * sz.cols]
            to = scalars[0, at + i]
            if sz.whole_tiles:
                start = pl.multiple_of(mod(to, sz.rows) * sz.cols, sz.cols)
                sent[quotient(to, sz.rows), pl.ds(start, sz.cols), :] = part.astype(BF16)
            else:
                later[pl.ds(pl.multiple_of(to * sz.cols, sz.cols), sz.cols), :] = part
    blocks = [in_block(sz, (n, dk), cut, shift) for shift in range(4)]
    lanes = cut * sz.cols + mod(iota((sz.width, dk), 0), sz.cols)
    fold = [
        one_hot(iota((sz.width, dk), 1) == mod(lanes + shift * sz.quarter, dk))
        for shift in range(-(-T // sz.back_depth))
    ]
    placed = [None] * sz.back_depth
    kept = [None] * sz.back_depth
    for index in range(sz.back_sets):
        shift, slot = index // sz.back_depth, index % sz.back_depth
        if index < T:
            folded = dot(jnp.concatenate(readouts[index], axis=0).astype(BF16), fold[shift])
            value = dot(place[index], folded.astype(BF16))
            placed[slot] = value if placed[slot] is None else placed[slot] + value
        else:
            value = window[(index - T) // sz.parts][(index - T) % sz.parts]
            if shift:
                value = pltpu.roll(value, shift * sz.quarter, 1)
            rest = jnp.zeros((n, dk), F32) if kept[slot] is None else kept[slot]
            kept[slot] = jnp.where(blocks[shift], value, rest)
    held = dot(place[T - 1], jnp.concatenate(kept, axis=1).astype(BF16))
    for slot in range(sz.back_depth):
        value = placed[slot] + held[:, slot * dk : (slot + 1) * dk]
        for r in range(sz.rows):
            at = slot * sz.rows + r
            back[pl.ds(at, count, stride=sz.back_rows), :] = value[r * count : (r + 1) * count]
    for g in range(count):
        p = sz.place_of[g]
        if not sz.whole_tiles:
            sent[p, : sz.state_rows, :] = later[
                p * sz.state_rows : (p + 1) * sz.state_rows, :
            ].astype(BF16)
        sent[p, sz.state_rows :, :] = back[
            g * sz.back_rows : (g + 1) * sz.back_rows, :
        ].astype(BF16)


def unpacker(sz, came, h, wanted):
    shape = (sz.back_rows, sz.dk)
    pieces = [
        came[sz.place_of[h * sz.cuts + cut], sz.state_rows :, :].astype(F32)
        for cut in range(sz.cuts)
    ]
    narrow = {}
    for shift in sorted({index // sz.back_depth for index in wanted}):
        value = pieces[0]
        for cut in range(1, sz.cuts):
            value = jnp.where(in_block(sz, shape, cut, shift), pieces[cut], value)
        if shift:
            value = pltpu.roll(value, sz.dk - shift * sz.quarter, 1)
        narrow[shift] = value

    def unpacked(index):
        at = index % sz.back_depth * sz.rows
        return narrow[index // sz.back_depth][at : at + sz.rows]

    return unpacked


def project_kernel(sz, blocks, factor, weight, came, *refs):
    dk = sz.dk
    partials, kept = refs[: blocks - 1], refs[blocks - 1]
    entries = sz.steps * sz.rows
    padded = factor.shape[0]
    gated = []
    for h in range(sz.heads):
        lanes = slice(h * dk, (h + 1) * dk)
        unpacked = unpacker(sz, came, h, range(sz.steps))
        total = jnp.concatenate(
            [unpacked(t) for t in range(sz.steps)]
            + [jnp.zeros((padded - entries, dk), F32)],
            axis=0,
        )
        scaling = lax.rsqrt(jnp.mean(total * total, axis=1, keepdims=True) + EPSILON)
        gated.append(total * scaling * factor[:, lanes])
    gated = jnp.concatenate(gated, axis=1).astype(BF16)
    kept[...] = gated
    for shift in range(1, blocks):
        project(sz, blocks, shift, gated, weight, partials[shift - 1])


def project(sz, blocks, shift, gated, weight, partial):
    columns = weight.shape[1] // blocks
    lanes = slice(None)
    if blocks > 1:
        at = lax.rem(lax.axis_index("head") + shift, blocks) * columns
        lanes = pl.ds(pl.multiple_of(at, LANES), columns)
    result = dot(gated, weight[:, lanes])
    for t in range(sz.steps):
        partial[t] = result[t * sz.rows : (t + 1) * sz.rows].astype(partial.dtype)


def restore_kernel(sz, blocks, gated, weight, came, states, partial, hist):
    project(sz, blocks, 0, gated[...], weight, partial)
    for h in range(sz.heads):
        unpacked = unpacker(sz, came, h, range(sz.steps, sz.back_sets))
        for tap in range(sz.taps):
            for part in range(sz.parts):
                value = unpacked(sz.steps + tap * sz.parts + part)
                hist[tap, part, :, h * sz.dk : (h + 1) * sz.dk] = value.astype(BF16)
    kind = BF16 if sz.whole_tiles else F32
    for r in range(sz.rows):
        for h in range(sz.heads):
            cuts = [
                came[sz.place_of[h * sz.cuts + cut], : sz.state_rows, :].astype(kind)[
                    r * sz.cols : (r + 1) * sz.cols
                ]
                for cut in range(sz.cuts)
            ]
            states[r, h] = jnp.concatenate(cuts, axis=0).T.astype(F32)


def vmem():
    return pl.BlockSpec(memory_space=pltpu.VMEM)


def smem():
    return pl.BlockSpec(memory_space=pltpu.SMEM)


def anywhere():
    return pl.BlockSpec(memory_space=pl.ANY)


def in_hbm(value):
    return pltpu.with_memory_space_constraint(value, pltpu.HBM)


def call(body, outs, ins, out_specs, scratch, name):
    return pl.pallas_call(
        body,
        out_shape=outs,
        in_specs=ins,
        out_specs=out_specs,
        scratch_shapes=scratch,
        compiler_params=pltpu.CompilerParams(vmem_limit_bytes=VMEM_LIMIT),
        name=name,
    )


def exchange(pieces, groups=None):
    return lax.all_to_all(
        pieces, "rep", split_axis=0, concat_axis=0, axis_index_groups=groups, tiled=True
    )


def local(
    group_total,
    head_total,
    states,
    conv_states,
    projected,
    conv_weight,
    decay_input,
    decay_rate,
    beta_logit,
    out_gate,
    norm_gain,
    out_weight,
    destinations,
    live_counts,
):
    sz = Sizes(group_total, states, conv_states, projected)
    n, channels = sz.groups, sz.heads * sz.dk
    shape = jax.ShapeDtypeStruct
    lives = live_counts.T
    arguments = (
        destinations,
        lives,
        decay_rate.reshape(1, sz.heads),
        beta_logit.transpose(1, 2, 0),
        projected.transpose(0, 2, 1, 3),
        conv_states.transpose(1, 2, 0, 3),
        decay_input,
        conv_weight.transpose(1, 0, 2),
        states,
    )
    routes = shape((sz.steps, sz.slots, sz.slots), BF16)
    pieces, pick, place, final, taps = call(
        functools.partial(pack_kernel, sz),
        (
            shape((n, sz.state_rows + sz.info_rows, sz.dk), BF16),
            routes,
            routes,
            shape((8, sz.slots), jnp.int32),
            shape((sz.parts, sz.taps + 1, sz.dk), F32),
        ),
        [anywhere()] * len(arguments),
        (vmem(),) * 5,
        [pltpu.VMEM(x.shape, x.dtype) for x in arguments]
        + [
            pltpu.VMEM((sz.heads, sz.value_at, sz.dk), F32),
            pltpu.VMEM((4, sz.heads, sz.tail_rows, sz.dk), F32),
            pltpu.VMEM((sz.heads, sz.dk), F32),
            pltpu.SemaphoreType.DMA((len(arguments) - 1 + sz.rows * sz.heads,)),
        ],
        "pack",
    )(*[in_hbm(x) for x in arguments])
    came = exchange(pieces)
    padded = round_up(sz.steps * sz.rows, 16)
    gain = norm_gain.reshape(1, sz.dk)
    stepped, factor = call(
        functools.partial(step_kernel, sz),
        (
            shape((n, sz.state_rows + sz.back_rows, sz.dk), BF16),
            shape((padded, channels), F32),
        ),
        [vmem()] * 4 + [anywhere()] * 4,
        (vmem(), vmem()),
        [
            pltpu.SMEM((8, sz.slots), jnp.int32),
            pltpu.VMEM(lives.shape, lives.dtype),
            pltpu.VMEM(gain.shape, F32),
            pltpu.VMEM(out_gate.shape, BF16),
            pltpu.VMEM((n * sz.info_rows, sz.dk), F32),
            pltpu.VMEM((8 if sz.whole_tiles else n * sz.state_rows, sz.dk), F32),
            pltpu.VMEM((n * sz.back_rows, sz.dk), F32),
            pltpu.SemaphoreType.DMA((4,)),
        ],
        "steps",
    )(taps, pick, place, came, final, in_hbm(lives), in_hbm(gain), in_hbm(out_gate))
    back = exchange(stepped, [sz.order])
    width = out_weight.shape[1]
    columns = width // head_total
    blocks = head_total if columns % LANES == 0 else 1
    *partials, gated = call(
        functools.partial(project_kernel, sz, blocks),
        tuple(shape((sz.steps, sz.rows, columns), BF16) for _ in range(1, blocks))
        + (shape((padded, channels), BF16),),
        [vmem()] * 3,
        tuple([vmem()] * blocks),
        [],
        "project",
    )(factor, out_weight, back)
    states_out, own, conv_out = call(
        functools.partial(restore_kernel, sz, blocks),
        (
            shape(states.shape, F32),
            shape((sz.steps, sz.rows, width // blocks), F32),
            shape((sz.taps, sz.parts, sz.rows, channels), BF16),
        ),
        [vmem()] * 3,
        (vmem(),) * 3,
        [],
        "restore",
    )(gated, out_weight, back)
    partials = [own, *partials]
    if blocks != head_total:
        mine = lax.axis_index("head")
        partials = [
            lax.dynamic_slice_in_dim(
                partials[0], lax.rem(mine + shift, head_total) * columns, columns, 2
            )
            for shift in range(head_total)
        ]
    total = partials[0]
    for shift in range(1, head_total):
        pairs = [(i, (i + shift) % head_total) for i in range(head_total)]
        passed = lax.ppermute(partials[shift].astype(BF16), "head", pairs)
        total = total + passed.astype(F32)
    return (total.astype(BF16), states_out, conv_out.transpose(2, 0, 1, 3))


def solution(mesh):
    placed = (
        P("rep", "head", None, None),
        P("rep", None, None, "head"),
        P(None, "rep", None, "head"),
        P(None, None, "head"),
        P(None, "rep", "head"),
        P("head"),
        P(None, "rep", "head"),
        P(None, "rep", "head"),
        P(),
        P("head", None),
        P(),
        P(None, "rep"),
    )
    return jax.shard_map(
        functools.partial(local, mesh.shape["rep"], mesh.shape["head"]),
        mesh=mesh,
        in_specs=placed,
        out_specs=(
            P(None, "rep", "head"),
            P("rep", "head", None, None),
            P("rep", None, None, "head"),
        ),
        check_vma=False,
    )
```

```python
import functools

import jax
import jax.numpy as jnp
from jax import lax
from jax.experimental import pallas as pl
from jax.experimental.pallas import tpu as pltpu
from jax.sharding import PartitionSpec as P

EPSILON = 1e-06
LANES = 128
VMEM_LIMIT = 32 * 1024 * 1024
F32 = jnp.float32
BF16 = jnp.bfloat16


def round_up(value, multiple):
    return -(-value // multiple) * multiple


class Sizes:
    def __init__(self, group_total, states, conv_states, projected):
        self.groups = n = group_total
        self.rows, self.heads, self.dk, _ = states.shape
        self.taps, self.parts = conv_states.shape[1:3]
        self.steps = projected.shape[0]
        self.slots = n * self.rows
        self.cuts = n // self.heads
        far = [*range(0, self.heads, 2), *range(1, self.heads, 2)]
        self.order = [h * self.cuts + cut for cut in range(self.cuts) for h in far]
        self.place_of = [self.order.index(p) for p in range(n)]
        self.cols = self.dk // self.cuts
        self.state_rows = self.rows * self.cols
        self.quarter = self.dk // 4
        self.decay_at = self.steps * 2
        self.hist_at = self.decay_at + self.steps
        self.value_at = self.hist_at + self.taps * 2
        self.value_depth = -(-(self.steps + self.taps) // 4)
        self.flag_at = self.value_at + self.value_depth
        self.info_sets = self.padded(self.flag_at + 1)
        self.info_rows = self.rows * self.info_sets
        self.back_sets = self.steps + self.taps * self.parts
        self.back_depth = self.padded(-(-self.back_sets // 4))
        self.back_rows = self.rows * self.back_depth
        self.read_rows = round_up(-(-self.steps // self.back_depth) * self.back_rows, 16)
        self.whole_tiles = self.cols % 16 == 0
        self.width = max(LANES, 8 * self.cols)
        self.tile = self.width // self.cols

    def padded(self, sets):
        while sets * self.rows % 8:
            sets += 1
        return sets

    def read_at(self, t, r):
        return t // self.back_depth * self.back_rows + r * self.back_depth + t % self.back_depth


def mod(value, size):
    return value & (size - 1) if size & (size - 1) == 0 else lax.rem(value, size)


def quotient(value, size):
    if size & (size - 1) == 0:
        return lax.shift_right_logical(value, jnp.int32(size.bit_length() - 1))
    return lax.div(value, jnp.int32(size))


def in_block(sz, shape, cut, shift):
    start = cut * sz.cols + shift * sz.quarter
    return mod(iota(shape, len(shape) - 1) + (2 * sz.dk - start), sz.dk) < sz.cols


def iota(shape, dim):
    return lax.broadcasted_iota(jnp.int32, shape, dim)


def one_hot(condition):
    return jnp.where(condition, 1.0, 0.0).astype(BF16)


def dot(lhs, rhs, lhs_dim=1, rhs_dim=0):
    return lax.dot_general(
        lhs, rhs, (((lhs_dim,), (rhs_dim,)), ((), ())), preferred_element_type=F32
    )


def pack_kernel(sz, *refs):
    count = 8
    sources, states_hbm = refs[:count], refs[count]
    pieces, pick, place, final, taps = refs[count + 1 : count + 6]
    scratch = refs[count + 6 :]
    targets, live, rate, beta, proj, hist, decay, filters, states = scratch[: count + 1]
    info, tails, strengths, in_sems = scratch[count + 1 :]
    copies = []

    def start(source, target):
        copies.append(pltpu.make_async_copy(source, target, in_sems.at[len(copies)]))
        copies[-1].start()

    for source, target in zip(sources, scratch):
        start(source, target)
    for r in range(sz.rows):
        for h in range(sz.heads):
            start(states_hbm.at[r, h], states.at[r, h])
    for copy in copies:
        copy.wait()
    route(sz, targets, pick, place, final)
    own_head = lax.axis_index("rep") // sz.cuts
    head_lanes = pl.ds(pl.multiple_of(own_head * sz.dk, sz.dk), sz.dk)
    for part in range(sz.parts):
        taps[part] = filters[part, :, head_lanes]
    channels, dk = sz.heads * sz.dk, sz.dk
    lane_head = quotient(iota((1, channels), 1), dk)
    rates = jnp.zeros((1, channels), F32)
    for h in range(sz.heads):
        rates = jnp.where(lane_head == h, rate[:, h : h + 1], rates)
    row_ids = iota((sz.rows, channels), 0)

    def keep(target, index, value):
        for h in range(sz.heads):
            rows = pl.ds(index, sz.rows, stride=sz.info_sets)
            target[h, rows, :] = value[:, h * dk : (h + 1) * dk]

    def keep_value(index, value):
        shift = index // sz.value_depth
        at = sz.value_at + index % sz.value_depth
        if shift:
            heads = [value[:, h * dk : (h + 1) * dk] for h in range(sz.heads)]
            heads = [pltpu.roll(head, shift * sz.quarter, 1) for head in heads]
            keep(tails.at[shift - 1], at, jnp.concatenate(heads, axis=1))
        else:
            keep(info, at, value)

    for t in range(sz.steps):
        for part in range(2):
            keep(info, t * 2 + part, proj[t, part].astype(F32))
        keep_value(t, proj[t, 2].astype(F32))
        x = decay[t]
        softplus = jnp.maximum(x, 0.0) + jnp.log1p(jnp.exp(-jnp.abs(x)))
        keep(
            info,
            sz.decay_at + t,
            jnp.where(row_ids < live[:, t : t + 1], rates * softplus, 0.0),
        )
    for tap in range(sz.taps):
        for part in range(2):
            keep(info, sz.hist_at + tap * 2 + part, hist[tap, part].astype(F32))
        keep_value(sz.steps + tap, hist[tap, 2].astype(F32))
    lane = iota((sz.heads, dk), 1)
    strengths[...] = jnp.zeros(strengths.shape, F32)
    for r in range(sz.rows):
        strengths[:, : sz.steps] = beta[r]
        lives = jnp.zeros((sz.heads, dk), F32)
        for t in range(sz.steps):
            lives = jnp.where((lane == t) & (r < live[:, t : t + 1]), 1.0, lives)
        strength = lives / (1.0 + jnp.exp(-strengths[...]))
        high = strength.astype(BF16).astype(F32)
        flags = high + pltpu.roll(lives, 16, 1) + pltpu.roll(strength - high, 32, 1)
        for h in range(sz.heads):
            at = r * sz.info_sets + sz.flag_at
            info[h, at : at + 1, :] = flags[h : h + 1]
    wide = [
        r * sz.info_sets + sz.value_at + i for r in range(sz.rows) for i in range(sz.value_depth)
    ]
    masks = {}
    for tile in sorted({at // 8 for at in wide}):
        row = iota((8, dk), 0) + tile * 8
        narrow = functools.reduce(jnp.logical_or, [row == at for at in wide if at // 8 == tile])
        masks[tile] = [
            [narrow & in_block(sz, (8, dk), cut, shift) for shift in range(1, 4)]
            for cut in range(sz.cuts)
        ]
    for h in range(sz.heads):
        across = [states[r, h].T for r in range(sz.rows)]
        base = [info[h, at : at + 8, :] for at in range(0, sz.info_rows, 8)]
        others = {
            tile: [tails[shift, h, tile * 8 : tile * 8 + 8, :] for shift in range(3)]
            for tile in masks
        }
        for cut in range(sz.cuts):
            p, at = h * sz.cuts + cut, cut * sz.cols
            own = [a[at : at + sz.cols] for a in across]
            pieces[p, : sz.state_rows, :] = jnp.concatenate(own, axis=0).astype(BF16)
            rest = list(base)
            for tile in masks:
                for shift in range(3):
                    rest[tile] = jnp.where(
                        masks[tile][cut][shift], others[tile][shift], rest[tile]
                    )
            pieces[p, sz.state_rows :, :] = jnp.concatenate(rest, axis=0).astype(BF16)


def route(sz, targets, pick, place, final):
    n, T = sz.slots, sz.steps
    steps = [one_hot(iota((n, n), 0) == targets[t : t + 1, :]) for t in range(T)]
    chain = [steps[0]]
    for t in range(1, T):
        if t % 2:
            pair = dot(steps[t], steps[t - 1]).astype(BF16)
            chain.append(dot(pair, chain[t - 2]).astype(BF16) if t > 1 else pair)
        else:
            chain.append(dot(steps[t], chain[t - 1]).astype(BF16))
    for t in range(T):
        place[t] = chain[t]
        pick[t] = chain[t].astype(F32).T.astype(BF16)
    slot = iota((8, n), 1)
    row, group = mod(slot, sz.rows), quotient(slot, sz.rows)
    head, cut = quotient(group, sz.cuts), mod(group, sz.cuts)
    far = quotient(head, 2) + mod(head, 2) * ((sz.heads + 1) // 2)
    weights = (cut * sz.heads + far) * sz.rows + row
    places = dot(weights.astype(F32).astype(BF16), chain[T - 1])
    final[...] = (places + 0.5).astype(jnp.int32)


def gate_factor(sz, live, gain, gate, factor):
    channels = sz.heads * sz.dk
    gains = jnp.concatenate([gain[...]] * sz.heads, axis=1)
    row = iota((sz.rows, channels), 0)
    factor[...] = jnp.zeros(factor.shape, F32)
    for t in range(sz.steps):
        gates = gains / (1.0 + jnp.exp(-gate[t].astype(F32)))
        gates = jnp.where(row < live[:, t : t + 1], gates, 0.0)
        for r in range(sz.rows):
            at = sz.read_at(t, r)
            factor[at : at + 1, :] = gates[r : r + 1]


def step_kernel(sz, filters, pick, place, came, *refs):
    count = sz.groups
    sources, sent, factor, scratch = refs[:4], refs[4], refs[5], refs[6:]
    scalars, live, gain, gate, info, later, back, sems = scratch
    copies = []
    for i, (source, target) in enumerate(zip(sources, scratch)):
        copies.append(pltpu.make_async_copy(source, target, sems.at[i]))
        copies[-1].start()
    n, dk, T = sz.slots, sz.dk, sz.steps
    mine = lax.axis_index("rep")
    cut = lax.rem(mine, sz.cuts)
    stride = sz.info_rows
    for g in range(count):
        info[g * stride : (g + 1) * stride, :] = came[g, sz.state_rows :, :].astype(F32)

    def gather(index):
        return info[pl.ds(index, n, stride=sz.info_sets), :]

    def gather_value(index):
        value = gather(sz.value_at + index % sz.value_depth)
        shift = index // sz.value_depth
        return pltpu.roll(value, dk - shift * sz.quarter, 1) if shift else value

    weights = [filters[part] for part in range(sz.parts)]
    flags = gather(sz.flag_at)
    window = [
        [gather(sz.hist_at + tap * 2 + part) for part in range(2)]
        + [gather_value(T + tap)]
        for tap in range(sz.taps)
    ]
    reach = jnp.ones((n, dk), F32)
    keys = []
    from_state, values, strengths, key_mix, read_mix = [], [], [], [], []
    for t in range(T):
        slots = [gather(t * 2 + part) for part in range(2)]
        slots += [gather_value(t), gather(sz.decay_at + t), flags]
        moved = dot(pick[t], jnp.concatenate(slots, axis=1).astype(BF16))
        inputs = [moved[:, i * dk : (i + 1) * dk] for i in range(sz.parts + 2)]
        moved_flags = inputs[sz.parts + 1]
        strength = moved_flags[:, t : t + 1] + moved_flags[:, 32 + t : 33 + t]
        alive = moved_flags[:, 16 + t : 17 + t] > 0.5
        active = []
        for part in range(sz.parts):
            frames = [window[tap][part] for tap in range(sz.taps)] + [inputs[part]]
            total = frames[0] * weights[part][:1]
            for j in range(1, sz.taps + 1):
                total = total + frames[j] * weights[part][j : j + 1]
            active.append(total / (1.0 + jnp.exp(-total)))
            for tap in range(sz.taps):
                window[tap][part] = jnp.where(alive, frames[tap + 1], frames[tap])
        query, key = (
            x * lax.rsqrt(jnp.sum(x * x, axis=1, keepdims=True) + EPSILON) for x in active[:2]
        )
        retain = jnp.exp(-inputs[sz.parts])
        reach = reach * retain
        keys = [k * retain for k in keys]
        key_mix.append([jnp.sum(key * k, axis=1, keepdims=True) for k in keys])
        keys.append(key)
        read_mix.append([jnp.sum(query * k, axis=1, keepdims=True) for k in keys])
        from_state += [reach * key, reach * query]
        values.append(active[2])
        strengths.append(strength)

    spread = one_hot(
        iota((dk, sz.width), 0) == cut * sz.cols + mod(iota((dk, sz.width), 1), sz.cols)
    )
    value_cols = dot(jnp.concatenate(values, axis=0).astype(BF16), spread)
    for copy in copies:
        copy.wait()
    gate_factor(sz, live, gain, gate, factor)
    lane_row = quotient(iota((sz.tile, sz.width), 1), sz.cols)
    own = iota((sz.tile, sz.width), 0) == lane_row
    readouts = [[] for _ in range(T)]
    for at in range(0, n, sz.tile):
        rows = slice(at, at + sz.tile)
        block = []
        for g in range(at // sz.rows, (at + sz.tile) // sz.rows):
            for r in range(sz.rows):
                if sz.whole_tiles:
                    block.append(came[g, r * sz.cols : (r + 1) * sz.cols, :])
                else:
                    piece = came[g, : sz.state_rows, :].astype(F32)
                    block.append(piece[r * sz.cols : (r + 1) * sz.cols])
        seen = dot(
            jnp.concatenate([x[rows] for x in from_state], axis=0).astype(BF16),
            jnp.concatenate(block, axis=0).astype(BF16),
            1,
            1,
        )
        seen = [seen[i * sz.tile : (i + 1) * sz.tile] for i in range(2 * T)]
        writes = []
        for t in range(T):
            target = value_cols[t * n + at : t * n + at + sz.tile] - seen[2 * t]
            target = jnp.where(own, target, 0.0)
            for s in range(t):
                target = target - key_mix[t][s][rows] * writes[s]
            writes.append(strengths[t][rows] * target)
            read = jnp.where(own, seen[2 * t + 1], 0.0)
            for s in range(t + 1):
                read = read + read_mix[t][s][rows] * writes[s]
            readouts[t].append(read * dk ** (-0.5))
        added = dot(
            jnp.concatenate(writes, axis=0).astype(BF16),
            jnp.concatenate([k[rows] for k in keys], axis=0).astype(BF16),
            0,
            0,
        )
        for i in range(sz.tile):
            part = block[i].astype(F32) * reach[at + i : at + i + 1]
            part = part + added[i * sz.cols : (i + 1) * sz.cols]
            to = scalars[0, at + i]
            if sz.whole_tiles:
                start = pl.multiple_of(mod(to, sz.rows) * sz.cols, sz.cols)
                sent[quotient(to, sz.rows), pl.ds(start, sz.cols), :] = part.astype(BF16)
            else:
                later[pl.ds(pl.multiple_of(to * sz.cols, sz.cols), sz.cols), :] = part
    blocks = [in_block(sz, (n, dk), cut, shift) for shift in range(4)]
    lanes = cut * sz.cols + mod(iota((sz.width, dk), 0), sz.cols)
    fold = [
        one_hot(iota((sz.width, dk), 1) == mod(lanes + shift * sz.quarter, dk))
        for shift in range(-(-T // sz.back_depth))
    ]
    placed = [None] * sz.back_depth
    kept = [None] * sz.back_depth
    for index in range(sz.back_sets):
        shift, slot = index // sz.back_depth, index % sz.back_depth
        if index < T:
            folded = dot(jnp.concatenate(readouts[index], axis=0).astype(BF16), fold[shift])
            value = dot(place[index], folded.astype(BF16))
            placed[slot] = value if placed[slot] is None else placed[slot] + value
        else:
            value = window[(index - T) // sz.parts][(index - T) % sz.parts]
            if shift:
                value = pltpu.roll(value, shift * sz.quarter, 1)
            rest = jnp.zeros((n, dk), F32) if kept[slot] is None else kept[slot]
            kept[slot] = jnp.where(blocks[shift], value, rest)
    kept = [jnp.zeros((n, dk), F32) if value is None else value for value in kept]
    held = dot(place[T - 1], jnp.concatenate(kept, axis=1).astype(BF16))
    for slot in range(sz.back_depth):
        value = held[:, slot * dk : (slot + 1) * dk]
        if placed[slot] is not None:
            value = value + placed[slot]
        back[pl.ds(slot, n, stride=sz.back_depth), :] = value
    for g in range(count):
        p = sz.place_of[g]
        if not sz.whole_tiles:
            sent[p, : sz.state_rows, :] = later[
                p * sz.state_rows : (p + 1) * sz.state_rows, :
            ].astype(BF16)
        sent[p, sz.state_rows :, :] = back[
            g * sz.back_rows : (g + 1) * sz.back_rows, :
        ].astype(BF16)


def unpack(sz, came, h, wanted):
    shape = (sz.back_rows, sz.dk)
    pieces = [
        came[sz.place_of[h * sz.cuts + cut], sz.state_rows :, :].astype(F32)
        for cut in range(sz.cuts)
    ]
    narrow = {}
    for shift in sorted({index // sz.back_depth for index in wanted}):
        value = pieces[0]
        for cut in range(1, sz.cuts):
            value = jnp.where(in_block(sz, shape, cut, shift), pieces[cut], value)
        if shift:
            value = pltpu.roll(value, sz.dk - shift * sz.quarter, 1)
        narrow[shift] = value

    return narrow


def project_kernel(sz, blocks, factor, weight, came, *refs):
    dk = sz.dk
    partials, kept = refs[: blocks - 1], refs[blocks - 1]
    gated = []
    for h in range(sz.heads):
        lanes = slice(h * dk, (h + 1) * dk)
        narrow = unpack(sz, came, h, range(sz.steps))
        total = [narrow[quarter] for quarter in sorted(narrow)]
        spare = sz.read_rows - len(total) * sz.back_rows
        if spare:
            total.append(jnp.zeros((spare, dk), F32))
        total = jnp.concatenate(total, axis=0)
        scaling = lax.rsqrt(jnp.mean(total * total, axis=1, keepdims=True) + EPSILON)
        gated.append(total * scaling * factor[:, lanes])
    gated = jnp.concatenate(gated, axis=1).astype(BF16)
    kept[...] = gated
    for shift in range(1, blocks):
        project(sz, blocks, shift, gated, weight, partials[shift - 1])


def project(sz, blocks, shift, gated, weight, partial):
    columns = weight.shape[1] // blocks
    lanes = slice(None)
    if blocks > 1:
        at = lax.rem(lax.axis_index("head") + shift, blocks) * columns
        lanes = pl.ds(pl.multiple_of(at, LANES), columns)
    result = dot(gated, weight[:, lanes])
    for t in range(sz.steps):
        rows = [result[at : at + 1] for at in (sz.read_at(t, r) for r in range(sz.rows))]
        partial[t] = jnp.concatenate(rows, axis=0).astype(partial.dtype)


def restore_kernel(sz, blocks, gated, weight, came, states, partial, hist):
    project(sz, blocks, 0, gated[...], weight, partial)
    for h in range(sz.heads):
        narrow = unpack(sz, came, h, range(sz.steps, sz.back_sets))
        for tap in range(sz.taps):
            for part in range(sz.parts):
                index = sz.steps + tap * sz.parts + part
                held = narrow[index // sz.back_depth]
                at = index % sz.back_depth
                rows = [held[at + r * sz.back_depth :][:1] for r in range(sz.rows)]
                value = jnp.concatenate(rows, axis=0)
                hist[tap, part, :, h * sz.dk : (h + 1) * sz.dk] = value.astype(BF16)
    kind = BF16 if sz.whole_tiles else F32
    for r in range(sz.rows):
        for h in range(sz.heads):
            cuts = [
                came[sz.place_of[h * sz.cuts + cut], : sz.state_rows, :].astype(kind)[
                    r * sz.cols : (r + 1) * sz.cols
                ]
                for cut in range(sz.cuts)
            ]
            states[r, h] = jnp.concatenate(cuts, axis=0).T.astype(F32)


def vmem():
    return pl.BlockSpec(memory_space=pltpu.VMEM)


def smem():
    return pl.BlockSpec(memory_space=pltpu.SMEM)


def anywhere():
    return pl.BlockSpec(memory_space=pl.ANY)


def in_hbm(value):
    return pltpu.with_memory_space_constraint(value, pltpu.HBM)


def call(body, outs, ins, out_specs, scratch, name):
    return pl.pallas_call(
        body,
        out_shape=outs,
        in_specs=ins,
        out_specs=out_specs,
        scratch_shapes=scratch,
        compiler_params=pltpu.CompilerParams(vmem_limit_bytes=VMEM_LIMIT),
        name=name,
    )


def exchange(pieces, groups=None):
    return lax.all_to_all(
        pieces, "rep", split_axis=0, concat_axis=0, axis_index_groups=groups, tiled=True
    )


def local(
    group_total,
    head_total,
    states,
    conv_states,
    projected,
    conv_weight,
    decay_input,
    decay_rate,
    beta_logit,
    out_gate,
    norm_gain,
    out_weight,
    destinations,
    live_counts,
):
    sz = Sizes(group_total, states, conv_states, projected)
    n, channels = sz.groups, sz.heads * sz.dk
    shape = jax.ShapeDtypeStruct
    lives = live_counts.T
    arguments = (
        destinations,
        lives,
        decay_rate.reshape(1, sz.heads),
        beta_logit.transpose(1, 2, 0),
        projected.transpose(0, 2, 1, 3),
        conv_states.transpose(1, 2, 0, 3),
        decay_input,
        conv_weight.transpose(1, 0, 2),
        states,
    )
    routes = shape((sz.steps, sz.slots, sz.slots), BF16)
    pieces, pick, place, final, taps = call(
        functools.partial(pack_kernel, sz),
        (
            shape((n, sz.state_rows + sz.info_rows, sz.dk), BF16),
            routes,
            routes,
            shape((8, sz.slots), jnp.int32),
            shape((sz.parts, sz.taps + 1, sz.dk), F32),
        ),
        [anywhere()] * len(arguments),
        (vmem(),) * 5,
        [pltpu.VMEM(x.shape, x.dtype) for x in arguments]
        + [
            pltpu.VMEM((sz.heads, sz.info_rows, sz.dk), F32),
            pltpu.VMEM((3, sz.heads, sz.info_rows, sz.dk), F32),
            pltpu.VMEM((sz.heads, sz.dk), F32),
            pltpu.SemaphoreType.DMA((len(arguments) - 1 + sz.rows * sz.heads,)),
        ],
        "pack",
    )(*[in_hbm(x) for x in arguments])
    came = exchange(pieces)
    gain = norm_gain.reshape(1, sz.dk)
    stepped, factor = call(
        functools.partial(step_kernel, sz),
        (
            shape((n, sz.state_rows + sz.back_rows, sz.dk), BF16),
            shape((sz.read_rows, channels), F32),
        ),
        [vmem()] * 4 + [anywhere()] * 4,
        (vmem(), vmem()),
        [
            pltpu.SMEM((8, sz.slots), jnp.int32),
            pltpu.VMEM(lives.shape, lives.dtype),
            pltpu.VMEM(gain.shape, F32),
            pltpu.VMEM(out_gate.shape, BF16),
            pltpu.VMEM((n * sz.info_rows, sz.dk), F32),
            pltpu.VMEM((8 if sz.whole_tiles else n * sz.state_rows, sz.dk), F32),
            pltpu.VMEM((n * sz.back_rows, sz.dk), F32),
            pltpu.SemaphoreType.DMA((4,)),
        ],
        "steps",
    )(taps, pick, place, came, final, in_hbm(lives), in_hbm(gain), in_hbm(out_gate))
    back = exchange(stepped, [sz.order])
    width = out_weight.shape[1]
    columns = width // head_total
    blocks = head_total if columns % LANES == 0 else 1
    *partials, gated = call(
        functools.partial(project_kernel, sz, blocks),
        tuple(shape((sz.steps, sz.rows, columns), BF16) for _ in range(1, blocks))
        + (shape((sz.read_rows, channels), BF16),),
        [vmem()] * 3,
        tuple([vmem()] * blocks),
        [],
        "project",
    )(factor, out_weight, back)
    states_out, own, conv_out = call(
        functools.partial(restore_kernel, sz, blocks),
        (
            shape(states.shape, F32),
            shape((sz.steps, sz.rows, width // blocks), F32),
            shape((sz.taps, sz.parts, sz.rows, channels), BF16),
        ),
        [vmem()] * 3,
        (vmem(),) * 3,
        [],
        "restore",
    )(gated, out_weight, back)
    partials = [own, *partials]
    if blocks != head_total:
        mine = lax.axis_index("head")
        partials = [
            lax.dynamic_slice_in_dim(
                partials[0], lax.rem(mine + shift, head_total) * columns, columns, 2
            )
            for shift in range(head_total)
        ]
    total = partials[0]
    for shift in range(1, head_total):
        pairs = [(i, (i + shift) % head_total) for i in range(head_total)]
        passed = lax.ppermute(partials[shift].astype(BF16), "head", pairs)
        total = total + passed.astype(F32)
    return (total.astype(BF16), states_out, conv_out.transpose(2, 0, 1, 3))


def solution(mesh):
    placed = (
        P("rep", "head", None, None),
        P("rep", None, None, "head"),
        P(None, "rep", None, "head"),
        P(None, None, "head"),
        P(None, "rep", "head"),
        P("head"),
        P(None, "rep", "head"),
        P(None, "rep", "head"),
        P(),
        P("head", None),
        P(),
        P(None, "rep"),
    )
    return jax.shard_map(
        functools.partial(local, mesh.shape["rep"], mesh.shape["head"]),
        mesh=mesh,
        in_specs=placed,
        out_specs=(
            P(None, "rep", "head"),
            P("rep", "head", None, None),
            P("rep", None, None, "head"),
        ),
        check_vma=False,
    )
```

```python
import functools

import jax
import jax.numpy as jnp
from jax import lax
from jax.experimental import pallas as pl
from jax.experimental.pallas import tpu as pltpu
from jax.sharding import PartitionSpec as P

EPSILON = 1e-06
LANES = 128
VMEM_LIMIT = 32 * 1024 * 1024
F32 = jnp.float32
BF16 = jnp.bfloat16


def round_up(value, multiple):
    return -(-value // multiple) * multiple


class Sizes:
    def __init__(self, group_total, states, conv_states, projected):
        self.groups = n = group_total
        self.rows, self.heads, self.dk, _ = states.shape
        self.taps, self.parts = conv_states.shape[1:3]
        self.steps = projected.shape[0]
        self.slots = n * self.rows
        self.cuts = n // self.heads
        far = [*range(0, self.heads, 2), *range(1, self.heads, 2)]
        self.order = [h * self.cuts + cut for cut in range(self.cuts) for h in far]
        self.place_of = [self.order.index(p) for p in range(n)]
        self.cols = self.dk // self.cuts
        self.state_rows = self.rows * self.cols
        self.quarter = self.dk // 4
        self.decay_at = self.steps * 2
        self.hist_at = self.decay_at + self.steps
        self.value_at = self.hist_at + self.taps * 2
        self.value_depth = -(-(self.steps + self.taps) // 4)
        self.flag_at = self.value_at + self.value_depth
        self.info_sets = self.padded(self.flag_at + 1)
        self.info_rows = self.rows * self.info_sets
        self.back_sets = self.steps + self.taps * self.parts
        self.back_depth = self.padded(-(-self.back_sets // 4))
        self.back_rows = self.rows * self.back_depth
        self.read_rows = round_up(-(-self.steps // self.back_depth) * self.back_rows, 16)
        self.whole_tiles = self.cols % 16 == 0
        self.width = max(LANES, 8 * self.cols)
        self.tile = self.width // self.cols

    def padded(self, sets):
        while sets * self.rows % 8:
            sets += 1
        return sets

    def read_at(self, t, r):
        return t // self.back_depth * self.back_rows + r * self.back_depth + t % self.back_depth


def mod(value, size):
    return value & (size - 1) if size & (size - 1) == 0 else lax.rem(value, size)


def quotient(value, size):
    if size & (size - 1) == 0:
        return lax.shift_right_logical(value, jnp.int32(size.bit_length() - 1))
    return lax.div(value, jnp.int32(size))


def in_block(sz, shape, cut, shift):
    start = cut * sz.cols + shift * sz.quarter
    return mod(iota(shape, len(shape) - 1) + (2 * sz.dk - start), sz.dk) < sz.cols


def iota(shape, dim):
    return lax.broadcasted_iota(jnp.int32, shape, dim)


def one_hot(condition):
    return jnp.where(condition, 1.0, 0.0).astype(BF16)


def dot(lhs, rhs, lhs_dim=1, rhs_dim=0):
    return lax.dot_general(
        lhs, rhs, (((lhs_dim,), (rhs_dim,)), ((), ())), preferred_element_type=F32
    )


def pack_kernel(sz, *refs):
    count = 8
    sources, states_hbm = refs[:count], refs[count]
    pieces, pick, place, final, taps = refs[count + 1 : count + 6]
    scratch = refs[count + 6 :]
    targets, live, rate, beta, proj, hist, decay, filters, states = scratch[: count + 1]
    info, tails, strengths, in_sems = scratch[count + 1 :]
    copies = []

    def start(source, target):
        copies.append(pltpu.make_async_copy(source, target, in_sems.at[len(copies)]))
        copies[-1].start()

    for source, target in zip(sources, scratch):
        start(source, target)
    for r in range(sz.rows):
        for h in range(sz.heads):
            start(states_hbm.at[r, h], states.at[r, h])
    for copy in copies[:count]:
        copy.wait()
    route(sz, targets, pick, place, final)
    own_head = lax.axis_index("rep") // sz.cuts
    head_lanes = pl.ds(pl.multiple_of(own_head * sz.dk, sz.dk), sz.dk)
    for part in range(sz.parts):
        taps[part] = filters[part, :, head_lanes]
    channels, dk = sz.heads * sz.dk, sz.dk
    lane_head = quotient(iota((1, channels), 1), dk)
    rates = jnp.zeros((1, channels), F32)
    for h in range(sz.heads):
        rates = jnp.where(lane_head == h, rate[:, h : h + 1], rates)
    row_ids = iota((sz.rows, channels), 0)

    def keep(target, index, value):
        for h in range(sz.heads):
            rows = pl.ds(index, sz.rows, stride=sz.info_sets)
            target[h, rows, :] = value[:, h * dk : (h + 1) * dk]

    def keep_value(index, value):
        shift = index // sz.value_depth
        at = sz.value_at + index % sz.value_depth
        if shift:
            heads = [value[:, h * dk : (h + 1) * dk] for h in range(sz.heads)]
            heads = [pltpu.roll(head, shift * sz.quarter, 1) for head in heads]
            keep(tails.at[shift - 1], at, jnp.concatenate(heads, axis=1))
        else:
            keep(info, at, value)

    for t in range(sz.steps):
        for part in range(2):
            keep(info, t * 2 + part, proj[t, part].astype(F32))
        keep_value(t, proj[t, 2].astype(F32))
        x = decay[t]
        softplus = jnp.maximum(x, 0.0) + jnp.log1p(jnp.exp(-jnp.abs(x)))
        keep(
            info,
            sz.decay_at + t,
            jnp.where(row_ids < live[:, t : t + 1], rates * softplus, 0.0),
        )
    for tap in range(sz.taps):
        for part in range(2):
            keep(info, sz.hist_at + tap * 2 + part, hist[tap, part].astype(F32))
        keep_value(sz.steps + tap, hist[tap, 2].astype(F32))
    lane = iota((sz.heads, dk), 1)
    strengths[...] = jnp.zeros(strengths.shape, F32)
    for r in range(sz.rows):
        strengths[:, : sz.steps] = beta[r]
        lives = jnp.zeros((sz.heads, dk), F32)
        for t in range(sz.steps):
            lives = jnp.where((lane == t) & (r < live[:, t : t + 1]), 1.0, lives)
        strength = lives / (1.0 + jnp.exp(-strengths[...]))
        high = strength.astype(BF16).astype(F32)
        flags = high + pltpu.roll(lives, 16, 1) + pltpu.roll(strength - high, 32, 1)
        for h in range(sz.heads):
            at = r * sz.info_sets + sz.flag_at
            info[h, at : at + 1, :] = flags[h : h + 1]
    wide = [
        r * sz.info_sets + sz.value_at + i for r in range(sz.rows) for i in range(sz.value_depth)
    ]
    masks = {}
    for tile in sorted({at // 8 for at in wide}):
        row = iota((8, dk), 0) + tile * 8
        narrow = functools.reduce(jnp.logical_or, [row == at for at in wide if at // 8 == tile])
        masks[tile] = [
            [narrow & in_block(sz, (8, dk), cut, shift) for shift in range(1, 4)]
            for cut in range(sz.cuts)
        ]
    shared = [
        at for at in range(0, sz.info_rows, 16) if at // 8 not in masks and at // 8 + 1 not in masks
    ]
    held = [[info[h, at : at + 16, :].astype(BF16) for at in shared] for h in range(sz.heads)]
    for copy in copies[count:]:
        copy.wait()
    for h in range(sz.heads):
        across = [states[r, h].T for r in range(sz.rows)]
        for cut in range(sz.cuts):
            p, at = h * sz.cuts + cut, cut * sz.cols
            own = [a[at : at + sz.cols] for a in across]
            pieces[p, : sz.state_rows, :] = jnp.concatenate(own, axis=0).astype(BF16)
            for at, value in zip(shared, held[h]):
                to = sz.state_rows + at
                pieces[p, to : to + value.shape[0], :] = value
            for at in range(0, sz.info_rows, 16):
                if at in shared:
                    continue
                rest = []
                for tile in range(at // 8, min(at + 16, sz.info_rows) // 8):
                    rows = slice(tile * 8, tile * 8 + 8)
                    value = info[h, rows, :]
                    for shift in range(3 if tile in masks else 0):
                        value = jnp.where(masks[tile][cut][shift], tails[shift, h, rows, :], value)
                    rest.append(value)
                rest = jnp.concatenate(rest, axis=0)
                to = sz.state_rows + at
                pieces[p, to : to + rest.shape[0], :] = rest.astype(BF16)


def route(sz, targets, pick, place, final):
    n, T = sz.slots, sz.steps
    steps = [one_hot(iota((n, n), 0) == targets[t : t + 1, :]) for t in range(T)]
    chain = [steps[0]]
    for t in range(1, T):
        if t % 2:
            pair = dot(steps[t], steps[t - 1]).astype(BF16)
            chain.append(dot(pair, chain[t - 2]).astype(BF16) if t > 1 else pair)
        else:
            chain.append(dot(steps[t], chain[t - 1]).astype(BF16))
    for t in range(T):
        place[t] = chain[t]
        pick[t] = chain[t].astype(F32).T.astype(BF16)
    slot = iota((8, n), 1)
    row, group = mod(slot, sz.rows), quotient(slot, sz.rows)
    head, cut = quotient(group, sz.cuts), mod(group, sz.cuts)
    far = quotient(head, 2) + mod(head, 2) * ((sz.heads + 1) // 2)
    weights = (cut * sz.heads + far) * sz.rows + row
    places = dot(weights.astype(F32).astype(BF16), chain[T - 1])
    final[...] = (places + 0.5).astype(jnp.int32)


def gate_factor(sz, live, gain, gate, factor):
    channels = sz.heads * sz.dk
    gains = jnp.concatenate([gain[...]] * sz.heads, axis=1)
    row = iota((sz.rows, channels), 0)
    factor[...] = jnp.zeros(factor.shape, F32)
    for t in range(sz.steps):
        gates = gains / (1.0 + jnp.exp(-gate[t].astype(F32)))
        gates = jnp.where(row < live[:, t : t + 1], gates, 0.0)
        for r in range(sz.rows):
            at = sz.read_at(t, r)
            factor[at : at + 1, :] = gates[r : r + 1]


def step_kernel(sz, filters, pick, place, came, *refs):
    count = sz.groups
    sources, sent, factor, scratch = refs[:4], refs[4], refs[5], refs[6:]
    scalars, live, gain, gate, info, later, back, sems = scratch
    copies = []
    for i, (source, target) in enumerate(zip(sources, scratch)):
        copies.append(pltpu.make_async_copy(source, target, sems.at[i]))
        copies[-1].start()
    n, dk, T = sz.slots, sz.dk, sz.steps
    mine = lax.axis_index("rep")
    cut = lax.rem(mine, sz.cuts)
    stride = sz.info_rows
    for g in range(count):
        info[g * stride : (g + 1) * stride, :] = came[g, sz.state_rows :, :].astype(F32)

    def gather(index):
        return info[pl.ds(index, n, stride=sz.info_sets), :]

    def gather_value(index):
        value = gather(sz.value_at + index % sz.value_depth)
        shift = index // sz.value_depth
        return pltpu.roll(value, dk - shift * sz.quarter, 1) if shift else value

    weights = [filters[part] for part in range(sz.parts)]
    flags = gather(sz.flag_at)
    window = [
        [gather(sz.hist_at + tap * 2 + part) for part in range(2)]
        + [gather_value(T + tap)]
        for tap in range(sz.taps)
    ]
    reach = jnp.ones((n, dk), F32)
    keys = []
    from_state, values, strengths, key_mix, read_mix = [], [], [], [], []
    for t in range(T):
        slots = [gather(t * 2 + part) for part in range(2)]
        slots += [gather_value(t), gather(sz.decay_at + t), flags]
        moved = dot(pick[t], jnp.concatenate(slots, axis=1).astype(BF16))
        inputs = [moved[:, i * dk : (i + 1) * dk] for i in range(sz.parts + 2)]
        moved_flags = inputs[sz.parts + 1]
        strength = moved_flags[:, t : t + 1] + moved_flags[:, 32 + t : 33 + t]
        alive = moved_flags[:, 16 + t : 17 + t] > 0.5
        active = []
        for part in range(sz.parts):
            frames = [window[tap][part] for tap in range(sz.taps)] + [inputs[part]]
            total = frames[0] * weights[part][:1]
            for j in range(1, sz.taps + 1):
                total = total + frames[j] * weights[part][j : j + 1]
            active.append(total / (1.0 + jnp.exp(-total)))
            for tap in range(sz.taps):
                window[tap][part] = jnp.where(alive, frames[tap + 1], frames[tap])
        query, key = (
            x * lax.rsqrt(jnp.sum(x * x, axis=1, keepdims=True) + EPSILON) for x in active[:2]
        )
        retain = jnp.exp(-inputs[sz.parts])
        reach = reach * retain
        keys = [k * retain for k in keys]
        key_mix.append([jnp.sum(key * k, axis=1, keepdims=True) for k in keys])
        keys.append(key)
        read_mix.append([jnp.sum(query * k, axis=1, keepdims=True) for k in keys])
        from_state += [reach * key, reach * query]
        values.append(active[2])
        strengths.append(strength)

    spread = one_hot(
        iota((dk, sz.width), 0) == cut * sz.cols + mod(iota((dk, sz.width), 1), sz.cols)
    )
    value_cols = dot(jnp.concatenate(values, axis=0).astype(BF16), spread)
    for copy in copies:
        copy.wait()
    gate_factor(sz, live, gain, gate, factor)
    lane_row = quotient(iota((sz.tile, sz.width), 1), sz.cols)
    own = iota((sz.tile, sz.width), 0) == lane_row
    readouts = [[] for _ in range(T)]
    for at in range(0, n, sz.tile):
        rows = slice(at, at + sz.tile)
        block = []
        for g in range(at // sz.rows, (at + sz.tile) // sz.rows):
            for r in range(sz.rows):
                if sz.whole_tiles:
                    block.append(came[g, r * sz.cols : (r + 1) * sz.cols, :])
                else:
                    piece = came[g, : sz.state_rows, :].astype(F32)
                    block.append(piece[r * sz.cols : (r + 1) * sz.cols])
        seen = dot(
            jnp.concatenate([x[rows] for x in from_state], axis=0).astype(BF16),
            jnp.concatenate(block, axis=0).astype(BF16),
            1,
            1,
        )
        seen = [seen[i * sz.tile : (i + 1) * sz.tile] for i in range(2 * T)]
        writes = []
        for t in range(T):
            target = value_cols[t * n + at : t * n + at + sz.tile] - seen[2 * t]
            target = jnp.where(own, target, 0.0)
            for s in range(t):
                target = target - key_mix[t][s][rows] * writes[s]
            writes.append(strengths[t][rows] * target)
            read = jnp.where(own, seen[2 * t + 1], 0.0)
            for s in range(t + 1):
                read = read + read_mix[t][s][rows] * writes[s]
            readouts[t].append(read * dk ** (-0.5))
        added = dot(
            jnp.concatenate(writes, axis=0).astype(BF16),
            jnp.concatenate([k[rows] for k in keys], axis=0).astype(BF16),
            0,
            0,
        )
        for i in range(sz.tile):
            part = block[i].astype(F32) * reach[at + i : at + i + 1]
            part = part + added[i * sz.cols : (i + 1) * sz.cols]
            to = scalars[0, at + i]
            if sz.whole_tiles:
                start = pl.multiple_of(mod(to, sz.rows) * sz.cols, sz.cols)
                sent[quotient(to, sz.rows), pl.ds(start, sz.cols), :] = part.astype(BF16)
            else:
                later[pl.ds(pl.multiple_of(to * sz.cols, sz.cols), sz.cols), :] = part
    blocks = [in_block(sz, (n, dk), cut, shift) for shift in range(4)]
    lanes = cut * sz.cols + mod(iota((sz.width, dk), 0), sz.cols)
    fold = [
        one_hot(iota((sz.width, dk), 1) == mod(lanes + shift * sz.quarter, dk))
        for shift in range(-(-T // sz.back_depth))
    ]
    placed = [None] * sz.back_depth
    kept = [None] * sz.back_depth
    for index in range(sz.back_sets):
        shift, slot = index // sz.back_depth, index % sz.back_depth
        if index < T:
            folded = dot(jnp.concatenate(readouts[index], axis=0).astype(BF16), fold[shift])
            value = dot(place[index], folded.astype(BF16))
            placed[slot] = value if placed[slot] is None else placed[slot] + value
        else:
            value = window[(index - T) // sz.parts][(index - T) % sz.parts]
            if shift:
                value = pltpu.roll(value, shift * sz.quarter, 1)
            rest = jnp.zeros((n, dk), F32) if kept[slot] is None else kept[slot]
            kept[slot] = jnp.where(blocks[shift], value, rest)
    kept = [jnp.zeros((n, dk), F32) if value is None else value for value in kept]
    held = dot(place[T - 1], jnp.concatenate(kept, axis=1).astype(BF16))
    for slot in range(sz.back_depth):
        value = held[:, slot * dk : (slot + 1) * dk]
        if placed[slot] is not None:
            value = value + placed[slot]
        back[pl.ds(slot, n, stride=sz.back_depth), :] = value
    for g in range(count):
        p = sz.place_of[g]
        if not sz.whole_tiles:
            sent[p, : sz.state_rows, :] = later[
                p * sz.state_rows : (p + 1) * sz.state_rows, :
            ].astype(BF16)
        sent[p, sz.state_rows :, :] = back[
            g * sz.back_rows : (g + 1) * sz.back_rows, :
        ].astype(BF16)


def unpack(sz, came, h, wanted):
    shape = (sz.back_rows, sz.dk)
    pieces = [
        came[sz.place_of[h * sz.cuts + cut], sz.state_rows :, :].astype(F32)
        for cut in range(sz.cuts)
    ]
    narrow = {}
    for shift in sorted({index // sz.back_depth for index in wanted}):
        value = pieces[0]
        for cut in range(1, sz.cuts):
            value = jnp.where(in_block(sz, shape, cut, shift), pieces[cut], value)
        if shift:
            value = pltpu.roll(value, sz.dk - shift * sz.quarter, 1)
        narrow[shift] = value

    return narrow


def project_kernel(sz, blocks, factor, weight, came, *refs):
    dk = sz.dk
    partials, kept = refs[: blocks - 1], refs[blocks - 1]
    gated = []
    for h in range(sz.heads):
        lanes = slice(h * dk, (h + 1) * dk)
        narrow = unpack(sz, came, h, range(sz.steps))
        total = [narrow[quarter] for quarter in sorted(narrow)]
        spare = sz.read_rows - len(total) * sz.back_rows
        if spare:
            total.append(jnp.zeros((spare, dk), F32))
        total = jnp.concatenate(total, axis=0)
        scaling = lax.rsqrt(jnp.mean(total * total, axis=1, keepdims=True) + EPSILON)
        gated.append(total * scaling * factor[:, lanes])
    gated = jnp.concatenate(gated, axis=1).astype(BF16)
    kept[...] = gated
    for shift in range(1, blocks):
        project(sz, blocks, shift, gated, weight, partials[shift - 1])


def project(sz, blocks, shift, gated, weight, partial):
    columns = weight.shape[1] // blocks
    lanes = slice(None)
    if blocks > 1:
        at = lax.rem(lax.axis_index("head") + shift, blocks) * columns
        lanes = pl.ds(pl.multiple_of(at, LANES), columns)
    result = dot(gated, weight[:, lanes])
    for t in range(sz.steps):
        rows = [result[at : at + 1] for at in (sz.read_at(t, r) for r in range(sz.rows))]
        partial[t] = jnp.concatenate(rows, axis=0).astype(partial.dtype)


def restore_kernel(sz, blocks, gated, weight, came, states, partial, hist):
    project(sz, blocks, 0, gated[...], weight, partial)
    for h in range(sz.heads):
        narrow = unpack(sz, came, h, range(sz.steps, sz.back_sets))
        for tap in range(sz.taps):
            for part in range(sz.parts):
                index = sz.steps + tap * sz.parts + part
                held = narrow[index // sz.back_depth]
                at = index % sz.back_depth
                rows = [held[at + r * sz.back_depth :][:1] for r in range(sz.rows)]
                value = jnp.concatenate(rows, axis=0)
                hist[tap, part, :, h * sz.dk : (h + 1) * sz.dk] = value.astype(BF16)
    kind = BF16 if sz.whole_tiles else F32
    for r in range(sz.rows):
        for h in range(sz.heads):
            cuts = [
                came[sz.place_of[h * sz.cuts + cut], : sz.state_rows, :].astype(kind)[
                    r * sz.cols : (r + 1) * sz.cols
                ]
                for cut in range(sz.cuts)
            ]
            states[r, h] = jnp.concatenate(cuts, axis=0).T.astype(F32)


def vmem():
    return pl.BlockSpec(memory_space=pltpu.VMEM)


def smem():
    return pl.BlockSpec(memory_space=pltpu.SMEM)


def anywhere():
    return pl.BlockSpec(memory_space=pl.ANY)


def in_hbm(value):
    return pltpu.with_memory_space_constraint(value, pltpu.HBM)


def call(body, outs, ins, out_specs, scratch, name):
    return pl.pallas_call(
        body,
        out_shape=outs,
        in_specs=ins,
        out_specs=out_specs,
        scratch_shapes=scratch,
        compiler_params=pltpu.CompilerParams(vmem_limit_bytes=VMEM_LIMIT),
        name=name,
    )


def exchange(pieces, groups=None):
    return lax.all_to_all(
        pieces, "rep", split_axis=0, concat_axis=0, axis_index_groups=groups, tiled=True
    )


def local(
    group_total,
    head_total,
    states,
    conv_states,
    projected,
    conv_weight,
    decay_input,
    decay_rate,
    beta_logit,
    out_gate,
    norm_gain,
    out_weight,
    destinations,
    live_counts,
):
    sz = Sizes(group_total, states, conv_states, projected)
    n, channels = sz.groups, sz.heads * sz.dk
    shape = jax.ShapeDtypeStruct
    lives = live_counts.T
    arguments = (
        destinations,
        lives,
        decay_rate.reshape(1, sz.heads),
        beta_logit.transpose(1, 2, 0),
        projected.transpose(0, 2, 1, 3),
        conv_states.transpose(1, 2, 0, 3),
        decay_input,
        conv_weight.transpose(1, 0, 2),
        states,
    )
    routes = shape((sz.steps, sz.slots, sz.slots), BF16)
    pieces, pick, place, final, taps = call(
        functools.partial(pack_kernel, sz),
        (
            shape((n, sz.state_rows + sz.info_rows, sz.dk), BF16),
            routes,
            routes,
            shape((8, sz.slots), jnp.int32),
            shape((sz.parts, sz.taps + 1, sz.dk), F32),
        ),
        [anywhere()] * len(arguments),
        (vmem(),) * 5,
        [pltpu.VMEM(x.shape, x.dtype) for x in arguments]
        + [
            pltpu.VMEM((sz.heads, sz.info_rows, sz.dk), F32),
            pltpu.VMEM((3, sz.heads, sz.info_rows, sz.dk), F32),
            pltpu.VMEM((sz.heads, sz.dk), F32),
            pltpu.SemaphoreType.DMA((len(arguments) - 1 + sz.rows * sz.heads,)),
        ],
        "pack",
    )(*[in_hbm(x) for x in arguments])
    came = exchange(pieces)
    gain = norm_gain.reshape(1, sz.dk)
    stepped, factor = call(
        functools.partial(step_kernel, sz),
        (
            shape((n, sz.state_rows + sz.back_rows, sz.dk), BF16),
            shape((sz.read_rows, channels), F32),
        ),
        [vmem()] * 4 + [anywhere()] * 4,
        (vmem(), vmem()),
        [
            pltpu.SMEM((8, sz.slots), jnp.int32),
            pltpu.VMEM(lives.shape, lives.dtype),
            pltpu.VMEM(gain.shape, F32),
            pltpu.VMEM(out_gate.shape, BF16),
            pltpu.VMEM((n * sz.info_rows, sz.dk), F32),
            pltpu.VMEM((8 if sz.whole_tiles else n * sz.state_rows, sz.dk), F32),
            pltpu.VMEM((n * sz.back_rows, sz.dk), F32),
            pltpu.SemaphoreType.DMA((4,)),
        ],
        "steps",
    )(taps, pick, place, came, final, in_hbm(lives), in_hbm(gain), in_hbm(out_gate))
    back = exchange(stepped, [sz.order])
    width = out_weight.shape[1]
    columns = width // head_total
    blocks = head_total if columns % LANES == 0 else 1
    *partials, gated = call(
        functools.partial(project_kernel, sz, blocks),
        tuple(shape((sz.steps, sz.rows, columns), BF16) for _ in range(1, blocks))
        + (shape((sz.read_rows, channels), BF16),),
        [vmem()] * 3,
        tuple([vmem()] * blocks),
        [],
        "project",
    )(factor, out_weight, back)
    states_out, own, conv_out = call(
        functools.partial(restore_kernel, sz, blocks),
        (
            shape(states.shape, F32),
            shape((sz.steps, sz.rows, width // blocks), F32),
            shape((sz.taps, sz.parts, sz.rows, channels), BF16),
        ),
        [vmem()] * 3,
        (vmem(),) * 3,
        [],
        "restore",
    )(gated, out_weight, back)
    partials = [own, *partials]
    if blocks != head_total:
        mine = lax.axis_index("head")
        partials = [
            lax.dynamic_slice_in_dim(
                partials[0], lax.rem(mine + shift, head_total) * columns, columns, 2
            )
            for shift in range(head_total)
        ]
    total = partials[0]
    for shift in range(1, head_total):
        pairs = [(i, (i + shift) % head_total) for i in range(head_total)]
        passed = lax.ppermute(partials[shift].astype(BF16), "head", pairs)
        total = total + passed.astype(F32)
    return (total.astype(BF16), states_out, conv_out.transpose(2, 0, 1, 3))


def solution(mesh):
    placed = (
        P("rep", "head", None, None),
        P("rep", None, None, "head"),
        P(None, "rep", None, "head"),
        P(None, None, "head"),
        P(None, "rep", "head"),
        P("head"),
        P(None, "rep", "head"),
        P(None, "rep", "head"),
        P(),
        P("head", None),
        P(),
        P(None, "rep"),
    )
    return jax.shard_map(
        functools.partial(local, mesh.shape["rep"], mesh.shape["head"]),
        mesh=mesh,
        in_specs=placed,
        out_specs=(
            P(None, "rep", "head"),
            P("rep", "head", None, None),
            P("rep", None, None, "head"),
        ),
        check_vma=False,
    )
```

```python
import functools

import jax
import jax.numpy as jnp
from jax import lax
from jax.experimental import pallas as pl
from jax.experimental.pallas import tpu as pltpu
from jax.sharding import PartitionSpec as P

EPSILON = 1e-06
LANES = 128
VMEM_LIMIT = 32 * 1024 * 1024
F32 = jnp.float32
BF16 = jnp.bfloat16


def round_up(value, multiple):
    return -(-value // multiple) * multiple


class Sizes:
    def __init__(self, group_total, states, conv_states, projected):
        self.groups = n = group_total
        self.rows, self.heads, self.dk, _ = states.shape
        self.taps, self.parts = conv_states.shape[1:3]
        self.steps = projected.shape[0]
        self.slots = n * self.rows
        self.cuts = n // self.heads
        far = [*range(0, self.heads, 2), *range(1, self.heads, 2)]
        self.order = [h * self.cuts + cut for cut in range(self.cuts) for h in far]
        self.place_of = [self.order.index(p) for p in range(n)]
        self.cols = self.dk // self.cuts
        self.state_rows = self.rows * self.cols
        self.quarter = self.dk // 4
        self.decay_at = self.steps * 2
        self.hist_at = self.decay_at + self.steps
        self.value_at = self.hist_at + self.taps * 2
        self.value_depth = -(-(self.steps + self.taps) // 4)
        self.flag_at = self.value_at + self.value_depth
        self.info_sets = self.padded(self.flag_at + 1)
        self.info_rows = self.rows * self.info_sets
        self.back_sets = self.steps + self.taps * self.parts
        self.back_depth = self.padded(-(-self.back_sets // 4))
        self.back_rows = self.rows * self.back_depth
        self.read_rows = round_up(-(-self.steps // self.back_depth) * self.back_rows, 16)
        self.whole_tiles = self.cols % 16 == 0
        self.width = max(LANES, 8 * self.cols)
        self.tile = self.width // self.cols

    def padded(self, sets):
        while sets * self.rows % 8:
            sets += 1
        return sets

    def read_at(self, t, r):
        return t // self.back_depth * self.back_rows + r * self.back_depth + t % self.back_depth


def mod(value, size):
    return value & (size - 1) if size & (size - 1) == 0 else lax.rem(value, size)


def quotient(value, size):
    if size & (size - 1) == 0:
        return lax.shift_right_logical(value, jnp.int32(size.bit_length() - 1))
    return lax.div(value, jnp.int32(size))


def in_block(sz, shape, cut, shift):
    start = cut * sz.cols + shift * sz.quarter
    return mod(iota(shape, len(shape) - 1) + (2 * sz.dk - start), sz.dk) < sz.cols


def iota(shape, dim):
    return lax.broadcasted_iota(jnp.int32, shape, dim)


def one_hot(condition):
    return jnp.where(condition, 1.0, 0.0).astype(BF16)


def dot(lhs, rhs, lhs_dim=1, rhs_dim=0):
    return lax.dot_general(
        lhs, rhs, (((lhs_dim,), (rhs_dim,)), ((), ())), preferred_element_type=F32
    )


def pack_kernel(sz, *refs):
    count = 8
    sources, states_hbm = refs[:count], refs[count]
    pieces, pick, place, final, taps = refs[count + 1 : count + 6]
    scratch = refs[count + 6 :]
    targets, live, rate, beta, proj, hist, decay, filters, states = scratch[: count + 1]
    info, tails, strengths, in_sems = scratch[count + 1 :]
    copies = []

    def start(source, target):
        copies.append(pltpu.make_async_copy(source, target, in_sems.at[len(copies)]))
        copies[-1].start()

    for source, target in zip(sources, scratch):
        start(source, target)
    for r in range(sz.rows):
        for h in range(sz.heads):
            start(states_hbm.at[r, h], states.at[r, h])
    for copy in copies[:count]:
        copy.wait()
    route(sz, targets, pick, place, final)
    own_head = lax.axis_index("rep") // sz.cuts
    head_lanes = pl.ds(pl.multiple_of(own_head * sz.dk, sz.dk), sz.dk)
    for part in range(sz.parts):
        taps[part] = filters[part, :, head_lanes]
    channels, dk = sz.heads * sz.dk, sz.dk
    lane_head = quotient(iota((1, channels), 1), dk)
    rates = jnp.zeros((1, channels), F32)
    for h in range(sz.heads):
        rates = jnp.where(lane_head == h, rate[:, h : h + 1], rates)
    row_ids = iota((sz.rows, channels), 0)

    def keep(target, index, value):
        for h in range(sz.heads):
            rows = pl.ds(index, sz.rows, stride=sz.info_sets)
            target[h, rows, :] = value[:, h * dk : (h + 1) * dk]

    def keep_value(index, value):
        shift = index // sz.value_depth
        at = sz.value_at + index % sz.value_depth
        if shift:
            heads = [value[:, h * dk : (h + 1) * dk] for h in range(sz.heads)]
            heads = [pltpu.roll(head, shift * sz.quarter, 1) for head in heads]
            keep(tails.at[shift - 1], at, jnp.concatenate(heads, axis=1))
        else:
            keep(info, at, value)

    for t in range(sz.steps):
        for part in range(2):
            keep(info, t * 2 + part, proj[t, part].astype(F32))
        keep_value(t, proj[t, 2].astype(F32))
        x = decay[t]
        softplus = jnp.maximum(x, 0.0) + jnp.log1p(jnp.exp(-jnp.abs(x)))
        keep(
            info,
            sz.decay_at + t,
            jnp.where(row_ids < live[:, t : t + 1], rates * softplus, 0.0),
        )
    for tap in range(sz.taps):
        for part in range(2):
            keep(info, sz.hist_at + tap * 2 + part, hist[tap, part].astype(F32))
        keep_value(sz.steps + tap, hist[tap, 2].astype(F32))
    lane = iota((sz.heads, dk), 1)
    strengths[...] = jnp.zeros(strengths.shape, F32)
    for r in range(sz.rows):
        strengths[:, : sz.steps] = beta[r]
        lives = jnp.zeros((sz.heads, dk), F32)
        for t in range(sz.steps):
            lives = jnp.where((lane == t) & (r < live[:, t : t + 1]), 1.0, lives)
        strength = lives / (1.0 + jnp.exp(-strengths[...]))
        high = strength.astype(BF16).astype(F32)
        flags = high + pltpu.roll(lives, 16, 1) + pltpu.roll(strength - high, 32, 1)
        for h in range(sz.heads):
            at = r * sz.info_sets + sz.flag_at
            info[h, at : at + 1, :] = flags[h : h + 1]
    wide = [
        r * sz.info_sets + sz.value_at + i for r in range(sz.rows) for i in range(sz.value_depth)
    ]
    masks = {}
    for tile in sorted({at // 8 for at in wide}):
        row = iota((8, dk), 0) + tile * 8
        narrow = functools.reduce(jnp.logical_or, [row == at for at in wide if at // 8 == tile])
        masks[tile] = [
            [narrow & in_block(sz, (8, dk), cut, shift) for shift in range(1, 4)]
            for cut in range(sz.cuts)
        ]
    shared = [
        at for at in range(0, sz.info_rows, 16) if at // 8 not in masks and at // 8 + 1 not in masks
    ]
    held = [[info[h, at : at + 16, :].astype(BF16) for at in shared] for h in range(sz.heads)]
    for copy in copies[count:]:
        copy.wait()
    for h in range(sz.heads):
        across = [states[r, h].T for r in range(sz.rows)]
        for cut in range(sz.cuts):
            p, at = sz.place_of[h * sz.cuts + cut], cut * sz.cols
            own = [a[at : at + sz.cols] for a in across]
            pieces[p, : sz.state_rows, :] = jnp.concatenate(own, axis=0).astype(BF16)
            for at, value in zip(shared, held[h]):
                to = sz.state_rows + at
                pieces[p, to : to + value.shape[0], :] = value
            for at in range(0, sz.info_rows, 16):
                if at in shared:
                    continue
                rest = []
                for tile in range(at // 8, min(at + 16, sz.info_rows) // 8):
                    rows = slice(tile * 8, tile * 8 + 8)
                    value = info[h, rows, :]
                    for shift in range(3 if tile in masks else 0):
                        value = jnp.where(masks[tile][cut][shift], tails[shift, h, rows, :], value)
                    rest.append(value)
                rest = jnp.concatenate(rest, axis=0)
                to = sz.state_rows + at
                pieces[p, to : to + rest.shape[0], :] = rest.astype(BF16)


def route(sz, targets, pick, place, final):
    n, T = sz.slots, sz.steps
    steps = [one_hot(iota((n, n), 0) == targets[t : t + 1, :]) for t in range(T)]
    chain = [steps[0]]
    for t in range(1, T):
        if t % 2:
            pair = dot(steps[t], steps[t - 1]).astype(BF16)
            chain.append(dot(pair, chain[t - 2]).astype(BF16) if t > 1 else pair)
        else:
            chain.append(dot(steps[t], chain[t - 1]).astype(BF16))
    for t in range(T):
        place[t] = chain[t]
        pick[t] = chain[t].astype(F32).T.astype(BF16)
    slot = iota((8, n), 1)
    row, group = mod(slot, sz.rows), quotient(slot, sz.rows)
    head, cut = quotient(group, sz.cuts), mod(group, sz.cuts)
    far = quotient(head, 2) + mod(head, 2) * ((sz.heads + 1) // 2)
    weights = (cut * sz.heads + far) * sz.rows + row
    places = dot(weights.astype(F32).astype(BF16), chain[T - 1])
    final[...] = (places + 0.5).astype(jnp.int32)


def over_blocks(sz, value):
    step = sz.cols
    while step < sz.dk:
        value = value + pltpu.roll(value, step, 1)
        step *= 2
    return value


def gate_factor(sz, live, gain, gate, factor):
    factor[...] = jnp.zeros(factor.shape, F32)
    row = iota((sz.read_rows, sz.dk), 0)
    alive = row < 0
    for t in range(sz.steps):
        for r in range(sz.rows):
            at = sz.read_at(t, r)
            factor[at : at + 1, :] = gate[t, r : r + 1].astype(F32)
            alive = alive | ((row == at) & (r < live[:, t : t + 1]))
    for h in range(sz.heads):
        lanes = slice(h * sz.dk, (h + 1) * sz.dk)
        gates = gain[...] / (1.0 + jnp.exp(-factor[:, lanes]))
        factor[:, lanes] = jnp.where(alive, gates, 0.0)


def step_kernel(sz, filters, pick, place, came, *refs):
    count = sz.groups
    sources, sent, factor, scratch = refs[:4], refs[4], refs[5], refs[6:]
    scalars, live, gain, gate, info, later, back, sems = scratch
    copies = []
    for i, (source, target) in enumerate(zip(sources, scratch)):
        copies.append(pltpu.make_async_copy(source, target, sems.at[i]))
        copies[-1].start()
    n, dk, T = sz.slots, sz.dk, sz.steps
    mine = lax.axis_index("rep")
    cut = lax.rem(mine, sz.cuts)
    stride = sz.info_rows
    for g in range(count):
        info[g * stride : (g + 1) * stride, :] = came[sz.place_of[g], sz.state_rows :, :].astype(F32)

    def gather(index):
        return info[pl.ds(index, n, stride=sz.info_sets), :]

    def gather_value(index):
        value = gather(sz.value_at + index % sz.value_depth)
        shift = index // sz.value_depth
        return pltpu.roll(value, dk - shift * sz.quarter, 1) if shift else value

    weights = [filters[part] for part in range(sz.parts)]
    flags = gather(sz.flag_at)
    window = [
        [gather(sz.hist_at + tap * 2 + part) for part in range(2)]
        + [gather_value(T + tap)]
        for tap in range(sz.taps)
    ]
    reach = jnp.ones((n, dk), F32)
    keys = []
    from_state, values, strengths, key_mix, read_mix = [], [], [], [], []
    for t in range(T):
        slots = [gather(t * 2 + part) for part in range(2)]
        slots += [gather_value(t), gather(sz.decay_at + t), flags]
        moved = dot(pick[t], jnp.concatenate(slots, axis=1).astype(BF16))
        inputs = [moved[:, i * dk : (i + 1) * dk] for i in range(sz.parts + 2)]
        moved_flags = inputs[sz.parts + 1]
        strength = moved_flags[:, t : t + 1] + moved_flags[:, 32 + t : 33 + t]
        alive = moved_flags[:, 16 + t : 17 + t] > 0.5
        active = []
        for part in range(sz.parts):
            frames = [window[tap][part] for tap in range(sz.taps)] + [inputs[part]]
            total = frames[0] * weights[part][:1]
            for j in range(1, sz.taps + 1):
                total = total + frames[j] * weights[part][j : j + 1]
            active.append(total / (1.0 + jnp.exp(-total)))
            for tap in range(sz.taps):
                window[tap][part] = jnp.where(alive, frames[tap + 1], frames[tap])
        query, key = (
            x * lax.rsqrt(jnp.sum(x * x, axis=1, keepdims=True) + EPSILON) for x in active[:2]
        )
        retain = jnp.exp(-inputs[sz.parts])
        reach = reach * retain
        keys = [k * retain for k in keys]
        key_mix.append([jnp.sum(key * k, axis=1, keepdims=True) for k in keys])
        keys.append(key)
        read_mix.append([jnp.sum(query * k, axis=1, keepdims=True) for k in keys])
        from_state += [reach * key, reach * query]
        values.append(active[2])
        strengths.append(strength)

    own_lanes = in_block(sz, (n, dk), cut, 0)
    wide = sz.width // dk
    value_cols = []
    for value in values:
        value = over_blocks(sz, jnp.where(own_lanes, value, 0.0))
        value_cols.append(jnp.concatenate([value] * wide, axis=1))
    for copy in copies:
        copy.wait()
    gate_factor(sz, live, gain, gate, factor)
    lane_row = quotient(iota((sz.tile, sz.width), 1), sz.cols)
    own = iota((sz.tile, sz.width), 0) == lane_row
    readouts = [[] for _ in range(T)]
    for at in range(0, n, sz.tile):
        rows = slice(at, at + sz.tile)
        block = []
        for g in range(at // sz.rows, (at + sz.tile) // sz.rows):
            for r in range(sz.rows):
                if sz.whole_tiles:
                    block.append(came[sz.place_of[g], r * sz.cols : (r + 1) * sz.cols, :])
                else:
                    piece = came[sz.place_of[g], : sz.state_rows, :].astype(F32)
                    block.append(piece[r * sz.cols : (r + 1) * sz.cols])
        seen = dot(
            jnp.concatenate([x[rows] for x in from_state], axis=0).astype(BF16),
            jnp.concatenate(block, axis=0).astype(BF16),
            1,
            1,
        )
        seen = [seen[i * sz.tile : (i + 1) * sz.tile] for i in range(2 * T)]
        writes = []
        for t in range(T):
            target = value_cols[t][rows] - seen[2 * t]
            target = jnp.where(own, target, 0.0)
            for s in range(t):
                target = target - key_mix[t][s][rows] * writes[s]
            writes.append(strengths[t][rows] * target)
            read = jnp.where(own, seen[2 * t + 1], 0.0)
            for s in range(t + 1):
                read = read + read_mix[t][s][rows] * writes[s]
            readouts[t].append(read * dk ** (-0.5))
        added = dot(
            jnp.concatenate(writes, axis=0).astype(BF16),
            jnp.concatenate([k[rows] for k in keys], axis=0).astype(BF16),
            0,
            0,
        )
        for i in range(sz.tile):
            part = block[i].astype(F32) * reach[at + i : at + i + 1]
            part = part + added[i * sz.cols : (i + 1) * sz.cols]
            to = scalars[0, at + i]
            if sz.whole_tiles:
                start = pl.multiple_of(mod(to, sz.rows) * sz.cols, sz.cols)
                sent[quotient(to, sz.rows), pl.ds(start, sz.cols), :] = part.astype(BF16)
            else:
                later[pl.ds(pl.multiple_of(to * sz.cols, sz.cols), sz.cols), :] = part
    blocks = [in_block(sz, (n, dk), cut, shift) for shift in range(4)]
    placed = [None] * sz.back_depth
    kept = [None] * sz.back_depth
    for index in range(sz.back_sets):
        shift, slot = index // sz.back_depth, index % sz.back_depth
        if index < T:
            folded = jnp.concatenate(readouts[index], axis=0)
            folded = functools.reduce(
                jnp.add, [folded[:, i * dk : (i + 1) * dk] for i in range(wide)]
            )
            folded = jnp.where(blocks[shift], over_blocks(sz, folded), 0.0)
            value = dot(place[index], folded.astype(BF16))
            placed[slot] = value if placed[slot] is None else placed[slot] + value
        else:
            value = window[(index - T) // sz.parts][(index - T) % sz.parts]
            if shift:
                value = pltpu.roll(value, shift * sz.quarter, 1)
            rest = jnp.zeros((n, dk), F32) if kept[slot] is None else kept[slot]
            kept[slot] = jnp.where(blocks[shift], value, rest)
    kept = [jnp.zeros((n, dk), F32) if value is None else value for value in kept]
    held = dot(place[T - 1], jnp.concatenate(kept, axis=1).astype(BF16))
    for slot in range(sz.back_depth):
        value = held[:, slot * dk : (slot + 1) * dk]
        if placed[slot] is not None:
            value = value + placed[slot]
        back[pl.ds(slot, n, stride=sz.back_depth), :] = value
    for g in range(count):
        p = sz.place_of[g]
        if not sz.whole_tiles:
            sent[p, : sz.state_rows, :] = later[
                p * sz.state_rows : (p + 1) * sz.state_rows, :
            ].astype(BF16)
        sent[p, sz.state_rows :, :] = back[
            g * sz.back_rows : (g + 1) * sz.back_rows, :
        ].astype(BF16)


def unpack(sz, came, h, wanted):
    shape = (sz.back_rows, sz.dk)
    pieces = [
        came[sz.place_of[h * sz.cuts + cut], sz.state_rows :, :].astype(F32)
        for cut in range(sz.cuts)
    ]
    narrow = {}
    for shift in sorted({index // sz.back_depth for index in wanted}):
        value = pieces[0]
        for cut in range(1, sz.cuts):
            value = jnp.where(in_block(sz, shape, cut, shift), pieces[cut], value)
        if shift:
            value = pltpu.roll(value, sz.dk - shift * sz.quarter, 1)
        narrow[shift] = value

    return narrow


def project_kernel(sz, blocks, factor, weight, came, *refs):
    dk = sz.dk
    partials, kept = refs[: blocks - 1], refs[blocks - 1]
    gated = []
    for h in range(sz.heads):
        lanes = slice(h * dk, (h + 1) * dk)
        narrow = unpack(sz, came, h, range(sz.steps))
        total = [narrow[quarter] for quarter in sorted(narrow)]
        spare = sz.read_rows - len(total) * sz.back_rows
        if spare:
            total.append(jnp.zeros((spare, dk), F32))
        total = jnp.concatenate(total, axis=0)
        scaling = lax.rsqrt(jnp.mean(total * total, axis=1, keepdims=True) + EPSILON)
        gated.append(total * scaling * factor[:, lanes])
    gated = jnp.concatenate(gated, axis=1).astype(BF16)
    kept[...] = gated
    for shift in range(1, blocks):
        project(sz, blocks, shift, gated, weight, partials[shift - 1])


def project(sz, blocks, shift, gated, weight, partial):
    columns = weight.shape[1] // blocks
    lanes = slice(None)
    if blocks > 1:
        at = lax.rem(lax.axis_index("head") + shift, blocks) * columns
        lanes = pl.ds(pl.multiple_of(at, LANES), columns)
    result = dot(gated, weight[:, lanes])
    for t in range(sz.steps):
        rows = [result[at : at + 1] for at in (sz.read_at(t, r) for r in range(sz.rows))]
        partial[t] = jnp.concatenate(rows, axis=0).astype(partial.dtype)


def restore_kernel(sz, blocks, gated, weight, came, states, partial, hist):
    project(sz, blocks, 0, gated[...], weight, partial)
    for h in range(sz.heads):
        narrow = unpack(sz, came, h, range(sz.steps, sz.back_sets))
        for tap in range(sz.taps):
            for part in range(sz.parts):
                index = sz.steps + tap * sz.parts + part
                held = narrow[index // sz.back_depth]
                at = index % sz.back_depth
                rows = [held[at + r * sz.back_depth :][:1] for r in range(sz.rows)]
                value = jnp.concatenate(rows, axis=0)
                hist[tap, part, :, h * sz.dk : (h + 1) * sz.dk] = value.astype(BF16)
    kind = BF16 if sz.whole_tiles else F32
    for r in range(sz.rows):
        for h in range(sz.heads):
            cuts = [
                came[sz.place_of[h * sz.cuts + cut], : sz.state_rows, :].astype(kind)[
                    r * sz.cols : (r + 1) * sz.cols
                ]
                for cut in range(sz.cuts)
            ]
            states[r, h] = jnp.concatenate(cuts, axis=0).T.astype(F32)


def vmem():
    return pl.BlockSpec(memory_space=pltpu.VMEM)


def smem():
    return pl.BlockSpec(memory_space=pltpu.SMEM)


def anywhere():
    return pl.BlockSpec(memory_space=pl.ANY)


def in_hbm(value):
    return pltpu.with_memory_space_constraint(value, pltpu.HBM)


def call(body, outs, ins, out_specs, scratch, name):
    return pl.pallas_call(
        body,
        out_shape=outs,
        in_specs=ins,
        out_specs=out_specs,
        scratch_shapes=scratch,
        compiler_params=pltpu.CompilerParams(vmem_limit_bytes=VMEM_LIMIT),
        name=name,
    )


def exchange(sz, pieces):
    return lax.all_to_all(
        pieces, "rep", split_axis=0, concat_axis=0, axis_index_groups=[sz.order], tiled=True
    )


def local(
    group_total,
    head_total,
    states,
    conv_states,
    projected,
    conv_weight,
    decay_input,
    decay_rate,
    beta_logit,
    out_gate,
    norm_gain,
    out_weight,
    destinations,
    live_counts,
):
    sz = Sizes(group_total, states, conv_states, projected)
    n, channels = sz.groups, sz.heads * sz.dk
    shape = jax.ShapeDtypeStruct
    lives = live_counts.T
    arguments = (
        destinations,
        lives,
        decay_rate.reshape(1, sz.heads),
        beta_logit.transpose(1, 2, 0),
        projected.transpose(0, 2, 1, 3),
        conv_states.transpose(1, 2, 0, 3),
        decay_input,
        conv_weight.transpose(1, 0, 2),
        states,
    )
    routes = shape((sz.steps, sz.slots, sz.slots), BF16)
    pieces, pick, place, final, taps = call(
        functools.partial(pack_kernel, sz),
        (
            shape((n, sz.state_rows + sz.info_rows, sz.dk), BF16),
            routes,
            routes,
            shape((8, sz.slots), jnp.int32),
            shape((sz.parts, sz.taps + 1, sz.dk), F32),
        ),
        [anywhere()] * len(arguments),
        (vmem(),) * 5,
        [pltpu.VMEM(x.shape, x.dtype) for x in arguments]
        + [
            pltpu.VMEM((sz.heads, sz.info_rows, sz.dk), F32),
            pltpu.VMEM((3, sz.heads, sz.info_rows, sz.dk), F32),
            pltpu.VMEM((sz.heads, sz.dk), F32),
            pltpu.SemaphoreType.DMA((len(arguments) - 1 + sz.rows * sz.heads,)),
        ],
        "pack",
    )(*[in_hbm(x) for x in arguments])
    came = exchange(sz, pieces)
    gain = norm_gain.reshape(1, sz.dk)
    stepped, factor = call(
        functools.partial(step_kernel, sz),
        (
            shape((n, sz.state_rows + sz.back_rows, sz.dk), BF16),
            shape((sz.read_rows, channels), F32),
        ),
        [vmem()] * 4 + [anywhere()] * 4,
        (vmem(), vmem()),
        [
            pltpu.SMEM((8, sz.slots), jnp.int32),
            pltpu.VMEM(lives.shape, lives.dtype),
            pltpu.VMEM(gain.shape, F32),
            pltpu.VMEM(out_gate.shape, BF16),
            pltpu.VMEM((n * sz.info_rows, sz.dk), F32),
            pltpu.VMEM((8 if sz.whole_tiles else n * sz.state_rows, sz.dk), F32),
            pltpu.VMEM((n * sz.back_rows, sz.dk), F32),
            pltpu.SemaphoreType.DMA((4,)),
        ],
        "steps",
    )(taps, pick, place, came, final, in_hbm(lives), in_hbm(gain), in_hbm(out_gate))
    back = exchange(sz, stepped)
    width = out_weight.shape[1]
    columns = width // head_total
    blocks = head_total if columns % LANES == 0 else 1
    *partials, gated = call(
        functools.partial(project_kernel, sz, blocks),
        tuple(shape((sz.steps, sz.rows, columns), BF16) for _ in range(1, blocks))
        + (shape((sz.read_rows, channels), BF16),),
        [vmem()] * 3,
        tuple([vmem()] * blocks),
        [],
        "project",
    )(factor, out_weight, back)
    states_out, own, conv_out = call(
        functools.partial(restore_kernel, sz, blocks),
        (
            shape(states.shape, F32),
            shape((sz.steps, sz.rows, width // blocks), F32),
            shape((sz.taps, sz.parts, sz.rows, channels), BF16),
        ),
        [vmem()] * 3,
        (vmem(),) * 3,
        [],
        "restore",
    )(gated, out_weight, back)
    partials = [own, *partials]
    if blocks != head_total:
        mine = lax.axis_index("head")
        partials = [
            lax.dynamic_slice_in_dim(
                partials[0], lax.rem(mine + shift, head_total) * columns, columns, 2
            )
            for shift in range(head_total)
        ]
    total = partials[0]
    for shift in range(1, head_total):
        pairs = [(i, (i + shift) % head_total) for i in range(head_total)]
        passed = lax.ppermute(partials[shift].astype(BF16), "head", pairs)
        total = total + passed.astype(F32)
    return (total.astype(BF16), states_out, conv_out.transpose(2, 0, 1, 3))


def solution(mesh):
    placed = (
        P("rep", "head", None, None),
        P("rep", None, None, "head"),
        P(None, "rep", None, "head"),
        P(None, None, "head"),
        P(None, "rep", "head"),
        P("head"),
        P(None, "rep", "head"),
        P(None, "rep", "head"),
        P(),
        P("head", None),
        P(),
        P(None, "rep"),
    )
    return jax.shard_map(
        functools.partial(local, mesh.shape["rep"], mesh.shape["head"]),
        mesh=mesh,
        in_specs=placed,
        out_specs=(
            P(None, "rep", "head"),
            P("rep", "head", None, None),
            P("rep", None, None, "head"),
        ),
        check_vma=False,
    )
```

```python
import functools

import jax
import jax.numpy as jnp
from jax import lax
from jax.experimental import pallas as pl
from jax.experimental.pallas import tpu as pltpu
from jax.sharding import PartitionSpec as P

EPSILON = 1e-06
LANES = 128
VMEM_LIMIT = 32 * 1024 * 1024
F32 = jnp.float32
BF16 = jnp.bfloat16


def round_up(value, multiple):
    return -(-value // multiple) * multiple


def power_of_two(value):
    return value & (value - 1) == 0


class Sizes:
    def __init__(self, group_total, states, conv_states, projected):
        self.groups = n = group_total
        self.rows, self.heads, self.dk, _ = states.shape
        self.taps, self.parts = conv_states.shape[1:3]
        self.steps = projected.shape[0]
        self.slots = n * self.rows
        self.cuts = n // self.heads
        far = range(self.heads)
        if power_of_two(self.heads):
            far = [h ^ (h >> 1) for h in far]
        self.order = [h * self.cuts + cut for cut in range(self.cuts) for h in far]
        self.place_of = [self.order.index(p) for p in range(n)]
        self.cols = self.dk // self.cuts
        self.state_rows = self.rows * self.cols
        self.quarter = self.dk // 4
        self.decay_at = self.steps * 2
        self.hist_at = self.decay_at + self.steps
        self.value_at = self.hist_at + self.taps * 2
        self.value_depth = -(-(self.steps + self.taps) // 4)
        self.flag_at = self.value_at + self.value_depth
        self.info_sets = self.padded(self.flag_at + 1)
        self.info_rows = self.rows * self.info_sets
        self.back_sets = self.steps + self.taps * self.parts
        self.back_depth = self.padded(-(-self.back_sets // 4))
        self.back_rows = self.rows * self.back_depth
        self.read_rows = round_up(-(-self.steps // self.back_depth) * self.back_rows, 16)
        self.whole_tiles = self.cols % 16 == 0
        self.width = max(LANES, 8 * self.cols)
        self.tile = self.width // self.cols

    def padded(self, sets):
        while sets * self.rows % 8:
            sets += 1
        return sets

    def read_at(self, t, r):
        return t // self.back_depth * self.back_rows + r * self.back_depth + t % self.back_depth


def mod(value, size):
    return value & (size - 1) if size & (size - 1) == 0 else lax.rem(value, size)


def quotient(value, size):
    if size & (size - 1) == 0:
        return lax.shift_right_logical(value, jnp.int32(size.bit_length() - 1))
    return lax.div(value, jnp.int32(size))


def in_block(sz, shape, cut, shift):
    start = cut * sz.cols + shift * sz.quarter
    return mod(iota(shape, len(shape) - 1) + (2 * sz.dk - start), sz.dk) < sz.cols


def iota(shape, dim):
    return lax.broadcasted_iota(jnp.int32, shape, dim)


def one_hot(condition):
    return jnp.where(condition, 1.0, 0.0).astype(BF16)


def dot(lhs, rhs, lhs_dim=1, rhs_dim=0):
    return lax.dot_general(
        lhs, rhs, (((lhs_dim,), (rhs_dim,)), ((), ())), preferred_element_type=F32
    )


def pack_kernel(sz, *refs):
    count = 8
    sources, states_hbm = refs[:count], refs[count]
    pieces, pick, place, final, taps = refs[count + 1 : count + 6]
    scratch = refs[count + 6 :]
    targets, live, rate, beta, proj, hist, decay, filters, states = scratch[: count + 1]
    info, tails, strengths, in_sems = scratch[count + 1 :]
    copies = []

    def start(source, target):
        copies.append(pltpu.make_async_copy(source, target, in_sems.at[len(copies)]))
        copies[-1].start()

    for source, target in zip(sources, scratch):
        start(source, target)
    for r in range(sz.rows):
        for h in range(sz.heads):
            start(states_hbm.at[r, h], states.at[r, h])
    for copy in copies[:count]:
        copy.wait()
    route(sz, targets, pick, place, final)
    own_head = lax.axis_index("rep") // sz.cuts
    head_lanes = pl.ds(pl.multiple_of(own_head * sz.dk, sz.dk), sz.dk)
    for part in range(sz.parts):
        taps[part] = filters[part, :, head_lanes]
    channels, dk = sz.heads * sz.dk, sz.dk
    lane_head = quotient(iota((1, channels), 1), dk)
    rates = jnp.zeros((1, channels), F32)
    for h in range(sz.heads):
        rates = jnp.where(lane_head == h, rate[:, h : h + 1], rates)
    row_ids = iota((sz.rows, channels), 0)

    def keep(target, index, value):
        for h in range(sz.heads):
            rows = pl.ds(index, sz.rows, stride=sz.info_sets)
            target[h, rows, :] = value[:, h * dk : (h + 1) * dk]

    def keep_value(index, value):
        shift = index // sz.value_depth
        at = sz.value_at + index % sz.value_depth
        if shift:
            heads = [value[:, h * dk : (h + 1) * dk] for h in range(sz.heads)]
            heads = [pltpu.roll(head, shift * sz.quarter, 1) for head in heads]
            keep(tails.at[shift - 1], at, jnp.concatenate(heads, axis=1))
        else:
            keep(info, at, value)

    for t in range(sz.steps):
        for part in range(2):
            keep(info, t * 2 + part, proj[t, part].astype(F32))
        keep_value(t, proj[t, 2].astype(F32))
        x = decay[t]
        softplus = jnp.maximum(x, 0.0) + jnp.log1p(jnp.exp(-jnp.abs(x)))
        keep(
            info,
            sz.decay_at + t,
            jnp.where(row_ids < live[:, t : t + 1], rates * softplus, 0.0),
        )
    for tap in range(sz.taps):
        for part in range(2):
            keep(info, sz.hist_at + tap * 2 + part, hist[tap, part].astype(F32))
        keep_value(sz.steps + tap, hist[tap, 2].astype(F32))
    lane = iota((sz.heads, dk), 1)
    strengths[...] = jnp.zeros(strengths.shape, F32)
    for r in range(sz.rows):
        strengths[:, : sz.steps] = beta[r]
        lives = jnp.zeros((sz.heads, dk), F32)
        for t in range(sz.steps):
            lives = jnp.where((lane == t) & (r < live[:, t : t + 1]), 1.0, lives)
        strength = lives / (1.0 + jnp.exp(-strengths[...]))
        high = strength.astype(BF16).astype(F32)
        flags = high + pltpu.roll(lives, 16, 1) + pltpu.roll(strength - high, 32, 1)
        for h in range(sz.heads):
            at = r * sz.info_sets + sz.flag_at
            info[h, at : at + 1, :] = flags[h : h + 1]
    wide = [
        r * sz.info_sets + sz.value_at + i for r in range(sz.rows) for i in range(sz.value_depth)
    ]
    masks = {}
    for tile in sorted({at // 8 for at in wide}):
        row = iota((8, dk), 0) + tile * 8
        narrow = functools.reduce(jnp.logical_or, [row == at for at in wide if at // 8 == tile])
        masks[tile] = [
            [narrow & in_block(sz, (8, dk), cut, shift) for shift in range(1, 4)]
            for cut in range(sz.cuts)
        ]
    shared = [
        at for at in range(0, sz.info_rows, 16) if at // 8 not in masks and at // 8 + 1 not in masks
    ]
    held = [[info[h, at : at + 16, :].astype(BF16) for at in shared] for h in range(sz.heads)]
    for copy in copies[count:]:
        copy.wait()
    for h in range(sz.heads):
        across = [states[r, h].T for r in range(sz.rows)]
        for cut in range(sz.cuts):
            p, at = sz.place_of[h * sz.cuts + cut], cut * sz.cols
            own = [a[at : at + sz.cols] for a in across]
            pieces[p, : sz.state_rows, :] = jnp.concatenate(own, axis=0).astype(BF16)
            for at, value in zip(shared, held[h]):
                to = sz.state_rows + at
                pieces[p, to : to + value.shape[0], :] = value
            for at in range(0, sz.info_rows, 16):
                if at in shared:
                    continue
                rest = []
                for tile in range(at // 8, min(at + 16, sz.info_rows) // 8):
                    rows = slice(tile * 8, tile * 8 + 8)
                    value = info[h, rows, :]
                    for shift in range(3 if tile in masks else 0):
                        value = jnp.where(masks[tile][cut][shift], tails[shift, h, rows, :], value)
                    rest.append(value)
                rest = jnp.concatenate(rest, axis=0)
                to = sz.state_rows + at
                pieces[p, to : to + rest.shape[0], :] = rest.astype(BF16)


def route(sz, targets, pick, place, final):
    n, T = sz.slots, sz.steps
    steps = [one_hot(iota((n, n), 0) == targets[t : t + 1, :]) for t in range(T)]
    chain = [steps[0]]
    for t in range(1, T):
        if t % 2:
            pair = dot(steps[t], steps[t - 1]).astype(BF16)
            chain.append(dot(pair, chain[t - 2]).astype(BF16) if t > 1 else pair)
        else:
            chain.append(dot(steps[t], chain[t - 1]).astype(BF16))
    for t in range(T):
        place[t] = chain[t]
        pick[t] = chain[t].astype(F32).T.astype(BF16)
    slot = iota((8, n), 1)
    row, group = mod(slot, sz.rows), quotient(slot, sz.rows)
    head, cut = quotient(group, sz.cuts), mod(group, sz.cuts)
    far = head
    step = 1
    while power_of_two(sz.heads) and step < sz.heads:
        far = far ^ lax.shift_right_logical(far, jnp.int32(step))
        step *= 2
    weights = (cut * sz.heads + far) * sz.rows + row
    places = dot(weights.astype(F32).astype(BF16), chain[T - 1])
    final[...] = (places + 0.5).astype(jnp.int32)


def over_blocks(sz, value):
    step = sz.cols
    while step < sz.dk:
        value = value + pltpu.roll(value, step, 1)
        step *= 2
    return value


def gate_factor(sz, live, gain, gate, factor):
    factor[...] = jnp.zeros(factor.shape, F32)
    row = iota((sz.read_rows, sz.dk), 0)
    alive = row < 0
    for t in range(sz.steps):
        for r in range(sz.rows):
            at = sz.read_at(t, r)
            factor[at : at + 1, :] = gate[t, r : r + 1].astype(F32)
            alive = alive | ((row == at) & (r < live[:, t : t + 1]))
    for h in range(sz.heads):
        lanes = slice(h * sz.dk, (h + 1) * sz.dk)
        gates = gain[...] / (1.0 + jnp.exp(-factor[:, lanes]))
        factor[:, lanes] = jnp.where(alive, gates, 0.0)


def step_kernel(sz, filters, pick, place, came, *refs):
    count = sz.groups
    sources, sent, factor, scratch = refs[:4], refs[4], refs[5], refs[6:]
    scalars, live, gain, gate, info, later, back, sems = scratch
    copies = []
    for i, (source, target) in enumerate(zip(sources, scratch)):
        copies.append(pltpu.make_async_copy(source, target, sems.at[i]))
        copies[-1].start()
    n, dk, T = sz.slots, sz.dk, sz.steps
    mine = lax.axis_index("rep")
    cut = lax.rem(mine, sz.cuts)
    stride = sz.info_rows
    for g in range(count):
        info[g * stride : (g + 1) * stride, :] = came[sz.place_of[g], sz.state_rows :, :].astype(F32)

    def gather(index):
        return info[pl.ds(index, n, stride=sz.info_sets), :]

    def gather_value(index):
        value = gather(sz.value_at + index % sz.value_depth)
        shift = index // sz.value_depth
        return pltpu.roll(value, dk - shift * sz.quarter, 1) if shift else value

    weights = [filters[part] for part in range(sz.parts)]
    flags = gather(sz.flag_at)
    window = [
        [gather(sz.hist_at + tap * 2 + part) for part in range(2)]
        + [gather_value(T + tap)]
        for tap in range(sz.taps)
    ]
    reach = jnp.ones((n, dk), F32)
    keys = []
    from_state, values, strengths, key_mix, read_mix = [], [], [], [], []
    for t in range(T):
        slots = [gather(t * 2 + part) for part in range(2)]
        slots += [gather_value(t), gather(sz.decay_at + t), flags]
        moved = dot(pick[t], jnp.concatenate(slots, axis=1).astype(BF16))
        inputs = [moved[:, i * dk : (i + 1) * dk] for i in range(sz.parts + 2)]
        moved_flags = inputs[sz.parts + 1]
        strength = moved_flags[:, t : t + 1] + moved_flags[:, 32 + t : 33 + t]
        alive = moved_flags[:, 16 + t : 17 + t] > 0.5
        active = []
        for part in range(sz.parts):
            frames = [window[tap][part] for tap in range(sz.taps)] + [inputs[part]]
            total = frames[0] * weights[part][:1]
            for j in range(1, sz.taps + 1):
                total = total + frames[j] * weights[part][j : j + 1]
            active.append(total / (1.0 + jnp.exp(-total)))
            for tap in range(sz.taps):
                window[tap][part] = jnp.where(alive, frames[tap + 1], frames[tap])
        query, key = (
            x * lax.rsqrt(jnp.sum(x * x, axis=1, keepdims=True) + EPSILON) for x in active[:2]
        )
        retain = jnp.exp(-inputs[sz.parts])
        reach = reach * retain
        keys = [k * retain for k in keys]
        key_mix.append([jnp.sum(key * k, axis=1, keepdims=True) for k in keys])
        keys.append(key)
        read_mix.append([jnp.sum(query * k, axis=1, keepdims=True) for k in keys])
        from_state += [reach * key, reach * query]
        values.append(active[2])
        strengths.append(strength)

    own_lanes = in_block(sz, (n, dk), cut, 0)
    wide = sz.width // dk
    value_cols = []
    for value in values:
        value = over_blocks(sz, jnp.where(own_lanes, value, 0.0))
        value_cols.append(jnp.concatenate([value] * wide, axis=1))
    for copy in copies:
        copy.wait()
    gate_factor(sz, live, gain, gate, factor)
    lane_row = quotient(iota((sz.tile, sz.width), 1), sz.cols)
    own = iota((sz.tile, sz.width), 0) == lane_row
    readouts = [[] for _ in range(T)]
    for at in range(0, n, sz.tile):
        rows = slice(at, at + sz.tile)
        block = []
        for g in range(at // sz.rows, (at + sz.tile) // sz.rows):
            for r in range(sz.rows):
                if sz.whole_tiles:
                    block.append(came[sz.place_of[g], r * sz.cols : (r + 1) * sz.cols, :])
                else:
                    piece = came[sz.place_of[g], : sz.state_rows, :].astype(F32)
                    block.append(piece[r * sz.cols : (r + 1) * sz.cols])
        seen = dot(
            jnp.concatenate([x[rows] for x in from_state], axis=0).astype(BF16),
            jnp.concatenate(block, axis=0).astype(BF16),
            1,
            1,
        )
        seen = [seen[i * sz.tile : (i + 1) * sz.tile] for i in range(2 * T)]
        writes = []
        for t in range(T):
            target = value_cols[t][rows] - seen[2 * t]
            target = jnp.where(own, target, 0.0)
            for s in range(t):
                target = target - key_mix[t][s][rows] * writes[s]
            writes.append(strengths[t][rows] * target)
            read = jnp.where(own, seen[2 * t + 1], 0.0)
            for s in range(t + 1):
                read = read + read_mix[t][s][rows] * writes[s]
            readouts[t].append(read * dk ** (-0.5))
        added = dot(
            jnp.concatenate(writes, axis=0).astype(BF16),
            jnp.concatenate([k[rows] for k in keys], axis=0).astype(BF16),
            0,
            0,
        )
        for i in range(sz.tile):
            part = block[i].astype(F32) * reach[at + i : at + i + 1]
            part = part + added[i * sz.cols : (i + 1) * sz.cols]
            to = scalars[0, at + i]
            if sz.whole_tiles:
                start = pl.multiple_of(mod(to, sz.rows) * sz.cols, sz.cols)
                sent[quotient(to, sz.rows), pl.ds(start, sz.cols), :] = part.astype(BF16)
            else:
                later[pl.ds(pl.multiple_of(to * sz.cols, sz.cols), sz.cols), :] = part
    blocks = [in_block(sz, (n, dk), cut, shift) for shift in range(4)]
    placed = [None] * sz.back_depth
    kept = [None] * sz.back_depth
    for index in range(sz.back_sets):
        shift, slot = index // sz.back_depth, index % sz.back_depth
        if index < T:
            folded = jnp.concatenate(readouts[index], axis=0)
            folded = functools.reduce(
                jnp.add, [folded[:, i * dk : (i + 1) * dk] for i in range(wide)]
            )
            folded = jnp.where(blocks[shift], over_blocks(sz, folded), 0.0)
            value = dot(place[index], folded.astype(BF16))
            placed[slot] = value if placed[slot] is None else placed[slot] + value
        else:
            value = window[(index - T) // sz.parts][(index - T) % sz.parts]
            if shift:
                value = pltpu.roll(value, shift * sz.quarter, 1)
            rest = jnp.zeros((n, dk), F32) if kept[slot] is None else kept[slot]
            kept[slot] = jnp.where(blocks[shift], value, rest)
    kept = [jnp.zeros((n, dk), F32) if value is None else value for value in kept]
    held = dot(place[T - 1], jnp.concatenate(kept, axis=1).astype(BF16))
    for slot in range(sz.back_depth):
        value = held[:, slot * dk : (slot + 1) * dk]
        if placed[slot] is not None:
            value = value + placed[slot]
        back[pl.ds(slot, n, stride=sz.back_depth), :] = value
    for g in range(count):
        p = sz.place_of[g]
        if not sz.whole_tiles:
            sent[p, : sz.state_rows, :] = later[
                p * sz.state_rows : (p + 1) * sz.state_rows, :
            ].astype(BF16)
        sent[p, sz.state_rows :, :] = back[
            g * sz.back_rows : (g + 1) * sz.back_rows, :
        ].astype(BF16)


def unpack(sz, came, h, wanted):
    shape = (sz.back_rows, sz.dk)
    pieces = [
        came[sz.place_of[h * sz.cuts + cut], sz.state_rows :, :].astype(F32)
        for cut in range(sz.cuts)
    ]
    narrow = {}
    for shift in sorted({index // sz.back_depth for index in wanted}):
        value = pieces[0]
        for cut in range(1, sz.cuts):
            value = jnp.where(in_block(sz, shape, cut, shift), pieces[cut], value)
        if shift:
            value = pltpu.roll(value, sz.dk - shift * sz.quarter, 1)
        narrow[shift] = value

    return narrow


def project_kernel(sz, blocks, factor, weight, came, *refs):
    dk = sz.dk
    partials, kept = refs[: blocks - 1], refs[blocks - 1]
    gated = []
    for h in range(sz.heads):
        lanes = slice(h * dk, (h + 1) * dk)
        narrow = unpack(sz, came, h, range(sz.steps))
        total = [narrow[quarter] for quarter in sorted(narrow)]
        spare = sz.read_rows - len(total) * sz.back_rows
        if spare:
            total.append(jnp.zeros((spare, dk), F32))
        total = jnp.concatenate(total, axis=0)
        scaling = lax.rsqrt(jnp.mean(total * total, axis=1, keepdims=True) + EPSILON)
        gated.append(total * scaling * factor[:, lanes])
    gated = jnp.concatenate(gated, axis=1).astype(BF16)
    kept[...] = gated
    for shift in range(1, blocks):
        project(sz, blocks, shift, gated, weight, partials[shift - 1])


def project(sz, blocks, shift, gated, weight, partial):
    columns = weight.shape[1] // blocks
    lanes = slice(None)
    if blocks > 1:
        at = lax.rem(lax.axis_index("head") + shift, blocks) * columns
        lanes = pl.ds(pl.multiple_of(at, LANES), columns)
    result = dot(gated, weight[:, lanes])
    for t in range(sz.steps):
        rows = [result[at : at + 1] for at in (sz.read_at(t, r) for r in range(sz.rows))]
        partial[t] = jnp.concatenate(rows, axis=0).astype(partial.dtype)


def restore_kernel(sz, blocks, gated, weight, came, states, partial, hist):
    project(sz, blocks, 0, gated[...], weight, partial)
    for h in range(sz.heads):
        narrow = unpack(sz, came, h, range(sz.steps, sz.back_sets))
        for tap in range(sz.taps):
            for part in range(sz.parts):
                index = sz.steps + tap * sz.parts + part
                held = narrow[index // sz.back_depth]
                at = index % sz.back_depth
                rows = [held[at + r * sz.back_depth :][:1] for r in range(sz.rows)]
                value = jnp.concatenate(rows, axis=0)
                hist[tap, part, :, h * sz.dk : (h + 1) * sz.dk] = value.astype(BF16)
    kind = BF16 if sz.whole_tiles else F32
    for r in range(sz.rows):
        for h in range(sz.heads):
            cuts = [
                came[sz.place_of[h * sz.cuts + cut], : sz.state_rows, :].astype(kind)[
                    r * sz.cols : (r + 1) * sz.cols
                ]
                for cut in range(sz.cuts)
            ]
            states[r, h] = jnp.concatenate(cuts, axis=0).T.astype(F32)


def vmem():
    return pl.BlockSpec(memory_space=pltpu.VMEM)


def smem():
    return pl.BlockSpec(memory_space=pltpu.SMEM)


def anywhere():
    return pl.BlockSpec(memory_space=pl.ANY)


def in_hbm(value):
    return pltpu.with_memory_space_constraint(value, pltpu.HBM)


def call(body, outs, ins, out_specs, scratch, name):
    return pl.pallas_call(
        body,
        out_shape=outs,
        in_specs=ins,
        out_specs=out_specs,
        scratch_shapes=scratch,
        compiler_params=pltpu.CompilerParams(vmem_limit_bytes=VMEM_LIMIT),
        name=name,
    )


def exchange(sz, pieces):
    return lax.all_to_all(
        pieces, "rep", split_axis=0, concat_axis=0, axis_index_groups=[sz.order], tiled=True
    )


def local(
    group_total,
    head_total,
    states,
    conv_states,
    projected,
    conv_weight,
    decay_input,
    decay_rate,
    beta_logit,
    out_gate,
    norm_gain,
    out_weight,
    destinations,
    live_counts,
):
    sz = Sizes(group_total, states, conv_states, projected)
    n, channels = sz.groups, sz.heads * sz.dk
    shape = jax.ShapeDtypeStruct
    lives = live_counts.T
    arguments = (
        destinations,
        lives,
        decay_rate.reshape(1, sz.heads),
        beta_logit.transpose(1, 2, 0),
        projected.transpose(0, 2, 1, 3),
        conv_states.transpose(1, 2, 0, 3),
        decay_input,
        conv_weight.transpose(1, 0, 2),
        states,
    )
    routes = shape((sz.steps, sz.slots, sz.slots), BF16)
    pieces, pick, place, final, taps = call(
        functools.partial(pack_kernel, sz),
        (
            shape((n, sz.state_rows + sz.info_rows, sz.dk), BF16),
            routes,
            routes,
            shape((8, sz.slots), jnp.int32),
            shape((sz.parts, sz.taps + 1, sz.dk), F32),
        ),
        [anywhere()] * len(arguments),
        (vmem(),) * 5,
        [pltpu.VMEM(x.shape, x.dtype) for x in arguments]
        + [
            pltpu.VMEM((sz.heads, sz.info_rows, sz.dk), F32),
            pltpu.VMEM((3, sz.heads, sz.info_rows, sz.dk), F32),
            pltpu.VMEM((sz.heads, sz.dk), F32),
            pltpu.SemaphoreType.DMA((len(arguments) - 1 + sz.rows * sz.heads,)),
        ],
        "pack",
    )(*[in_hbm(x) for x in arguments])
    came = exchange(sz, pieces)
    gain = norm_gain.reshape(1, sz.dk)
    stepped, factor = call(
        functools.partial(step_kernel, sz),
        (
            shape((n, sz.state_rows + sz.back_rows, sz.dk), BF16),
            shape((sz.read_rows, channels), F32),
        ),
        [vmem()] * 4 + [anywhere()] * 4,
        (vmem(), vmem()),
        [
            pltpu.SMEM((8, sz.slots), jnp.int32),
            pltpu.VMEM(lives.shape, lives.dtype),
            pltpu.VMEM(gain.shape, F32),
            pltpu.VMEM(out_gate.shape, BF16),
            pltpu.VMEM((n * sz.info_rows, sz.dk), F32),
            pltpu.VMEM((8 if sz.whole_tiles else n * sz.state_rows, sz.dk), F32),
            pltpu.VMEM((n * sz.back_rows, sz.dk), F32),
            pltpu.SemaphoreType.DMA((4,)),
        ],
        "steps",
    )(taps, pick, place, came, final, in_hbm(lives), in_hbm(gain), in_hbm(out_gate))
    back = exchange(sz, stepped)
    width = out_weight.shape[1]
    columns = width // head_total
    blocks = head_total if columns % LANES == 0 else 1
    *partials, gated = call(
        functools.partial(project_kernel, sz, blocks),
        tuple(shape((sz.steps, sz.rows, columns), BF16) for _ in range(1, blocks))
        + (shape((sz.read_rows, channels), BF16),),
        [vmem()] * 3,
        tuple([vmem()] * blocks),
        [],
        "project",
    )(factor, out_weight, back)
    states_out, own, conv_out = call(
        functools.partial(restore_kernel, sz, blocks),
        (
            shape(states.shape, F32),
            shape((sz.steps, sz.rows, width // blocks), F32),
            shape((sz.taps, sz.parts, sz.rows, channels), BF16),
        ),
        [vmem()] * 3,
        (vmem(),) * 3,
        [],
        "restore",
    )(gated, out_weight, back)
    partials = [own, *partials]
    if blocks != head_total:
        mine = lax.axis_index("head")
        partials = [
            lax.dynamic_slice_in_dim(
                partials[0], lax.rem(mine + shift, head_total) * columns, columns, 2
            )
            for shift in range(head_total)
        ]
    total = partials[0]
    for shift in range(1, head_total):
        pairs = [(i, (i + shift) % head_total) for i in range(head_total)]
        passed = lax.ppermute(partials[shift].astype(BF16), "head", pairs)
        total = total + passed.astype(F32)
    return (total.astype(BF16), states_out, conv_out.transpose(2, 0, 1, 3))


def solution(mesh):
    placed = (
        P("rep", "head", None, None),
        P("rep", None, None, "head"),
        P(None, "rep", None, "head"),
        P(None, None, "head"),
        P(None, "rep", "head"),
        P("head"),
        P(None, "rep", "head"),
        P(None, "rep", "head"),
        P(),
        P("head", None),
        P(),
        P(None, "rep"),
    )
    return jax.shard_map(
        functools.partial(local, mesh.shape["rep"], mesh.shape["head"]),
        mesh=mesh,
        in_specs=placed,
        out_specs=(
            P(None, "rep", "head"),
            P("rep", "head", None, None),
            P("rep", None, None, "head"),
        ),
        check_vma=False,
    )
```

```python
import functools

import jax
import jax.numpy as jnp
from jax import lax
from jax.experimental import pallas as pl
from jax.experimental.pallas import tpu as pltpu
from jax.sharding import PartitionSpec as P

EPSILON = 1e-06
LANES = 128
VMEM_LIMIT = 32 * 1024 * 1024
F32 = jnp.float32
BF16 = jnp.bfloat16


def round_up(value, multiple):
    return -(-value // multiple) * multiple


def power_of_two(value):
    return value & (value - 1) == 0


class Sizes:
    def __init__(self, group_total, states, conv_states, projected):
        self.groups = n = group_total
        self.rows, self.heads, self.dk, _ = states.shape
        self.taps, self.parts = conv_states.shape[1:3]
        self.steps = projected.shape[0]
        self.slots = n * self.rows
        self.cuts = n // self.heads
        far = range(self.heads)
        if power_of_two(self.heads):
            far = [h ^ (h >> 1) for h in far]
        self.order = [h * self.cuts + cut for cut in range(self.cuts) for h in far]
        self.place_of = [self.order.index(p) for p in range(n)]
        self.cols = self.dk // self.cuts
        self.state_rows = self.rows * self.cols
        self.quarter = self.dk // 4
        self.decay_at = self.steps * 2
        self.hist_at = self.decay_at + self.steps
        self.value_at = self.hist_at + self.taps * 2
        self.value_depth = -(-(self.steps + self.taps) // 4)
        self.flag_at = self.value_at + self.value_depth
        self.info_sets = self.padded(self.flag_at + 1)
        self.info_rows = self.rows * self.info_sets
        self.back_sets = self.steps + self.taps * self.parts
        self.back_depth = self.padded(-(-self.back_sets // 4))
        self.back_rows = self.rows * self.back_depth
        self.read_rows = round_up(-(-self.steps // self.back_depth) * self.back_rows, 16)
        self.whole_tiles = self.cols % 16 == 0
        self.width = max(LANES, 8 * self.cols)
        self.tile = self.width // self.cols

    def padded(self, sets):
        while sets * self.rows % 8:
            sets += 1
        return sets

    def read_at(self, t, r):
        return t // self.back_depth * self.back_rows + r * self.back_depth + t % self.back_depth


def mod(value, size):
    return value & (size - 1) if size & (size - 1) == 0 else lax.rem(value, size)


def quotient(value, size):
    if size & (size - 1) == 0:
        return lax.shift_right_logical(value, jnp.int32(size.bit_length() - 1))
    return lax.div(value, jnp.int32(size))


def in_block(sz, shape, cut, shift):
    start = cut * sz.cols + shift * sz.quarter
    return mod(iota(shape, len(shape) - 1) + (2 * sz.dk - start), sz.dk) < sz.cols


def iota(shape, dim):
    return lax.broadcasted_iota(jnp.int32, shape, dim)


def one_hot(condition):
    return jnp.where(condition, 1.0, 0.0).astype(BF16)


def dot(lhs, rhs, lhs_dim=1, rhs_dim=0):
    return lax.dot_general(
        lhs, rhs, (((lhs_dim,), (rhs_dim,)), ((), ())), preferred_element_type=F32
    )


def pack_kernel(sz, *refs):
    count = 8
    sources, states_hbm = refs[:count], refs[count]
    pieces, pick, place, final, taps = refs[count + 1 : count + 6]
    scratch = refs[count + 6 :]
    targets, live, rate, beta, proj, hist, decay, filters, states = scratch[: count + 1]
    info, tails, strengths, in_sems = scratch[count + 1 :]
    copies = []

    def start(source, target):
        copies.append(pltpu.make_async_copy(source, target, in_sems.at[len(copies)]))
        copies[-1].start()

    for source, target in zip(sources, scratch):
        start(source, target)
    for r in range(sz.rows):
        for h in range(sz.heads):
            start(states_hbm.at[r, h], states.at[r, h])
    for copy in copies[:count]:
        copy.wait()
    route(sz, targets, pick, place, final)
    own_head = lax.axis_index("rep") // sz.cuts
    head_lanes = pl.ds(pl.multiple_of(own_head * sz.dk, sz.dk), sz.dk)
    for part in range(sz.parts):
        taps[part] = filters[part, :, head_lanes]
    channels, dk = sz.heads * sz.dk, sz.dk
    lane_head = quotient(iota((1, channels), 1), dk)
    rates = jnp.zeros((1, channels), F32)
    for h in range(sz.heads):
        rates = jnp.where(lane_head == h, rate[:, h : h + 1], rates)
    row_ids = iota((sz.rows, channels), 0)

    def keep(target, index, value):
        for h in range(sz.heads):
            rows = pl.ds(index, sz.rows, stride=sz.info_sets)
            target[h, rows, :] = value[:, h * dk : (h + 1) * dk]

    def keep_value(index, value):
        shift = index // sz.value_depth
        at = sz.value_at + index % sz.value_depth
        if shift:
            heads = [value[:, h * dk : (h + 1) * dk] for h in range(sz.heads)]
            heads = [pltpu.roll(head, shift * sz.quarter, 1) for head in heads]
            keep(tails.at[shift - 1], at, jnp.concatenate(heads, axis=1))
        else:
            keep(info, at, value)

    for t in range(sz.steps):
        for part in range(2):
            keep(info, t * 2 + part, proj[t, part].astype(F32))
        keep_value(t, proj[t, 2].astype(F32))
        x = decay[t]
        softplus = jnp.maximum(x, 0.0) + jnp.log1p(jnp.exp(-jnp.abs(x)))
        keep(
            info,
            sz.decay_at + t,
            jnp.where(row_ids < live[:, t : t + 1], rates * softplus, 0.0),
        )
    for tap in range(sz.taps):
        for part in range(2):
            keep(info, sz.hist_at + tap * 2 + part, hist[tap, part].astype(F32))
        keep_value(sz.steps + tap, hist[tap, 2].astype(F32))
    lane = iota((sz.heads, dk), 1)
    strengths[...] = jnp.zeros(strengths.shape, F32)
    for r in range(sz.rows):
        strengths[:, : sz.steps] = beta[r]
        lives = jnp.zeros((sz.heads, dk), F32)
        for t in range(sz.steps):
            lives = jnp.where((lane == t) & (r < live[:, t : t + 1]), 1.0, lives)
        strength = lives / (1.0 + jnp.exp(-strengths[...]))
        high = strength.astype(BF16).astype(F32)
        flags = high + pltpu.roll(lives, 16, 1) + pltpu.roll(strength - high, 32, 1)
        for h in range(sz.heads):
            at = r * sz.info_sets + sz.flag_at
            info[h, at : at + 1, :] = flags[h : h + 1]
    wide = [
        r * sz.info_sets + sz.value_at + i for r in range(sz.rows) for i in range(sz.value_depth)
    ]
    masks = {}
    for tile in sorted({at // 8 for at in wide}):
        row = iota((8, dk), 0) + tile * 8
        narrow = functools.reduce(jnp.logical_or, [row == at for at in wide if at // 8 == tile])
        masks[tile] = [
            [narrow & in_block(sz, (8, dk), cut, shift) for shift in range(1, 4)]
            for cut in range(sz.cuts)
        ]
    shared = [
        at for at in range(0, sz.info_rows, 16) if at // 8 not in masks and at // 8 + 1 not in masks
    ]
    held = [[info[h, at : at + 16, :].astype(BF16) for at in shared] for h in range(sz.heads)]
    for copy in copies[count:]:
        copy.wait()
    for h in range(sz.heads):
        across = [states[r, h].T for r in range(sz.rows)]
        for cut in range(sz.cuts):
            p, at = sz.place_of[h * sz.cuts + cut], cut * sz.cols
            own = [a[at : at + sz.cols] for a in across]
            pieces[p, : sz.state_rows, :] = jnp.concatenate(own, axis=0).astype(BF16)
            for at, value in zip(shared, held[h]):
                to = sz.state_rows + at
                pieces[p, to : to + value.shape[0], :] = value
            for at in range(0, sz.info_rows, 16):
                if at in shared:
                    continue
                rest = []
                for tile in range(at // 8, min(at + 16, sz.info_rows) // 8):
                    rows = slice(tile * 8, tile * 8 + 8)
                    value = info[h, rows, :]
                    for shift in range(3 if tile in masks else 0):
                        value = jnp.where(masks[tile][cut][shift], tails[shift, h, rows, :], value)
                    rest.append(value)
                rest = jnp.concatenate(rest, axis=0)
                to = sz.state_rows + at
                pieces[p, to : to + rest.shape[0], :] = rest.astype(BF16)


def route(sz, targets, pick, place, final):
    n, T = sz.slots, sz.steps
    steps = [one_hot(iota((n, n), 0) == targets[t : t + 1, :]) for t in range(T)]
    chain = [steps[0]]
    for t in range(1, T):
        if t % 2:
            pair = dot(steps[t], steps[t - 1]).astype(BF16)
            chain.append(dot(pair, chain[t - 2]).astype(BF16) if t > 1 else pair)
        else:
            chain.append(dot(steps[t], chain[t - 1]).astype(BF16))
    for t in range(T):
        place[t] = chain[t]
        pick[t] = chain[t].astype(F32).T.astype(BF16)
    slot = iota((8, n), 1)
    row, group = mod(slot, sz.rows), quotient(slot, sz.rows)
    head, cut = quotient(group, sz.cuts), mod(group, sz.cuts)
    far = head
    step = 1
    while power_of_two(sz.heads) and step < sz.heads:
        far = far ^ lax.shift_right_logical(far, jnp.int32(step))
        step *= 2
    weights = (cut * sz.heads + far) * sz.rows + row
    places = dot(weights.astype(F32).astype(BF16), chain[T - 1])
    final[...] = (places + 0.5).astype(jnp.int32)


def over_blocks(sz, value):
    step = sz.cols
    while step < sz.dk:
        value = value + pltpu.roll(value, step, 1)
        step *= 2
    return value


def gate_factor(sz, live, gain, gate, factor):
    factor[...] = jnp.zeros(factor.shape, F32)
    row = iota((sz.read_rows, sz.dk), 0)
    alive = row < 0
    for t in range(sz.steps):
        for r in range(sz.rows):
            at = sz.read_at(t, r)
            factor[at : at + 1, :] = gate[t, r : r + 1].astype(F32)
            alive = alive | ((row == at) & (r < live[:, t : t + 1]))
    for h in range(sz.heads):
        lanes = slice(h * sz.dk, (h + 1) * sz.dk)
        gates = gain[...] / (1.0 + jnp.exp(-factor[:, lanes]))
        factor[:, lanes] = jnp.where(alive, gates, 0.0)


def step_kernel(sz, filters, pick, place, came, *refs):
    count = sz.groups
    sources, sent, factor, scratch = refs[:4], refs[4], refs[5], refs[6:]
    scalars, live, gain, gate, info, later, back, sems = scratch
    copies = []
    for i, (source, target) in enumerate(zip(sources, scratch)):
        copies.append(pltpu.make_async_copy(source, target, sems.at[i]))
        copies[-1].start()
    n, dk, T = sz.slots, sz.dk, sz.steps
    mine = lax.axis_index("rep")
    cut = lax.rem(mine, sz.cuts)
    stride = sz.info_rows
    for g in range(count):
        info[g * stride : (g + 1) * stride, :] = came[sz.place_of[g], sz.state_rows :, :].astype(F32)

    def gather(index):
        return info[pl.ds(index, n, stride=sz.info_sets), :]

    def gather_value(index):
        value = gather(sz.value_at + index % sz.value_depth)
        shift = index // sz.value_depth
        return pltpu.roll(value, dk - shift * sz.quarter, 1) if shift else value

    weights = [filters[part] for part in range(sz.parts)]
    flags = gather(sz.flag_at)
    window = [
        [gather(sz.hist_at + tap * 2 + part) for part in range(2)]
        + [gather_value(T + tap)]
        for tap in range(sz.taps)
    ]
    active, retains, strengths = [], [], []
    for t in range(T):
        slots = [gather(t * 2 + part) for part in range(2)]
        slots += [gather_value(t), gather(sz.decay_at + t), flags]
        moved = dot(pick[t], jnp.concatenate(slots, axis=1).astype(BF16))
        inputs = [moved[:, i * dk : (i + 1) * dk] for i in range(sz.parts + 2)]
        moved_flags = inputs[sz.parts + 1]
        strength = moved_flags[:, t : t + 1] + moved_flags[:, 32 + t : 33 + t]
        alive = moved_flags[:, 16 + t : 17 + t] > 0.5
        for part in range(sz.parts):
            frames = [window[tap][part] for tap in range(sz.taps)] + [inputs[part]]
            total = frames[0] * weights[part][:1]
            for j in range(1, sz.taps + 1):
                total = total + frames[j] * weights[part][j : j + 1]
            active.append(total / (1.0 + jnp.exp(-total)))
            for tap in range(sz.taps):
                window[tap][part] = jnp.where(alive, frames[tap + 1], frames[tap])
        retains.append(jnp.exp(-inputs[sz.parts]))
        strengths.append(strength)

    ones = jnp.ones((dk, dk), BF16)

    def summed(products):
        sums = dot(jnp.concatenate([x.astype(BF16) for x in products], axis=0), ones)
        return [sums[i * n : (i + 1) * n] for i in range(len(products))]

    values = active[2 :: sz.parts]
    units = [x for i, x in enumerate(active) if i % sz.parts < 2]
    norms = summed([x * x for x in units])
    units = [x * lax.rsqrt(norm + EPSILON) for x, norm in zip(units, norms)]
    reach = jnp.ones((n, dk), F32)
    keys = []
    from_state, pairs = [], []
    for t in range(T):
        query, key = units[2 * t], units[2 * t + 1]
        reach = reach * retains[t]
        keys = [k * retains[t] for k in keys]
        pairs += [key * k for k in keys]
        keys.append(key)
        pairs += [query * k for k in keys]
        from_state += [reach * key, reach * query]
    mixes = summed(pairs)
    key_mix, read_mix = [], []
    for t in range(T):
        key_mix.append(mixes[:t])
        read_mix.append(mixes[t : 2 * t + 1])
        mixes = mixes[2 * t + 1 :]

    own_lanes = in_block(sz, (n, dk), cut, 0)
    wide = sz.width // dk
    value_cols = []
    for value in values:
        value = over_blocks(sz, jnp.where(own_lanes, value, 0.0))
        value_cols.append(jnp.concatenate([value] * wide, axis=1))
    for copy in copies:
        copy.wait()
    gate_factor(sz, live, gain, gate, factor)
    lane_row = quotient(iota((sz.tile, sz.width), 1), sz.cols)
    own = iota((sz.tile, sz.width), 0) == lane_row
    readouts = [[] for _ in range(T)]

    def widen(value):
        return jnp.concatenate([value] * wide, axis=1)

    for at in range(0, n, sz.tile):
        rows = slice(at, at + sz.tile)
        block = []
        for g in range(at // sz.rows, (at + sz.tile) // sz.rows):
            for r in range(sz.rows):
                if sz.whole_tiles:
                    block.append(came[sz.place_of[g], r * sz.cols : (r + 1) * sz.cols, :])
                else:
                    piece = came[sz.place_of[g], : sz.state_rows, :].astype(F32)
                    block.append(piece[r * sz.cols : (r + 1) * sz.cols])
        seen = dot(
            jnp.concatenate([x[rows] for x in from_state], axis=0).astype(BF16),
            jnp.concatenate(block, axis=0).astype(BF16),
            1,
            1,
        )
        seen = [seen[i * sz.tile : (i + 1) * sz.tile] for i in range(2 * T)]
        writes = []
        for t in range(T):
            target = value_cols[t][rows] - seen[2 * t]
            target = jnp.where(own, target, 0.0)
            for s in range(t):
                target = target - widen(key_mix[t][s][rows]) * writes[s]
            writes.append(strengths[t][rows] * target)
            read = jnp.where(own, seen[2 * t + 1], 0.0)
            for s in range(t + 1):
                read = read + widen(read_mix[t][s][rows]) * writes[s]
            readouts[t].append(read * dk ** (-0.5))
        added = dot(
            jnp.concatenate(writes, axis=0).astype(BF16),
            jnp.concatenate([k[rows] for k in keys], axis=0).astype(BF16),
            0,
            0,
        )
        for i in range(sz.tile):
            part = block[i].astype(F32) * reach[at + i : at + i + 1]
            part = part + added[i * sz.cols : (i + 1) * sz.cols]
            to = scalars[0, at + i]
            if sz.whole_tiles:
                start = pl.multiple_of(mod(to, sz.rows) * sz.cols, sz.cols)
                sent[quotient(to, sz.rows), pl.ds(start, sz.cols), :] = part.astype(BF16)
            else:
                later[pl.ds(pl.multiple_of(to * sz.cols, sz.cols), sz.cols), :] = part
    blocks = [in_block(sz, (n, dk), cut, shift) for shift in range(4)]
    placed = [None] * sz.back_depth
    kept = [None] * sz.back_depth
    for index in range(sz.back_sets):
        shift, slot = index // sz.back_depth, index % sz.back_depth
        if index < T:
            folded = jnp.concatenate(readouts[index], axis=0)
            folded = functools.reduce(
                jnp.add, [folded[:, i * dk : (i + 1) * dk] for i in range(wide)]
            )
            folded = jnp.where(blocks[shift], over_blocks(sz, folded), 0.0)
            value = dot(place[index], folded.astype(BF16))
            placed[slot] = value if placed[slot] is None else placed[slot] + value
        else:
            value = window[(index - T) // sz.parts][(index - T) % sz.parts]
            if shift:
                value = pltpu.roll(value, shift * sz.quarter, 1)
            rest = jnp.zeros((n, dk), F32) if kept[slot] is None else kept[slot]
            kept[slot] = jnp.where(blocks[shift], value, rest)
    kept = [jnp.zeros((n, dk), F32) if value is None else value for value in kept]
    held = dot(place[T - 1], jnp.concatenate(kept, axis=1).astype(BF16))
    for slot in range(sz.back_depth):
        value = held[:, slot * dk : (slot + 1) * dk]
        if placed[slot] is not None:
            value = value + placed[slot]
        back[pl.ds(slot, n, stride=sz.back_depth), :] = value
    for g in range(count):
        p = sz.place_of[g]
        if not sz.whole_tiles:
            sent[p, : sz.state_rows, :] = later[
                p * sz.state_rows : (p + 1) * sz.state_rows, :
            ].astype(BF16)
        sent[p, sz.state_rows :, :] = back[
            g * sz.back_rows : (g + 1) * sz.back_rows, :
        ].astype(BF16)


def unpack(sz, came, h, wanted):
    shape = (sz.back_rows, sz.dk)
    pieces = [
        came[sz.place_of[h * sz.cuts + cut], sz.state_rows :, :].astype(F32)
        for cut in range(sz.cuts)
    ]
    narrow = {}
    for shift in sorted({index // sz.back_depth for index in wanted}):
        value = pieces[0]
        for cut in range(1, sz.cuts):
            value = jnp.where(in_block(sz, shape, cut, shift), pieces[cut], value)
        if shift:
            value = pltpu.roll(value, sz.dk - shift * sz.quarter, 1)
        narrow[shift] = value

    return narrow


def project_kernel(sz, blocks, factor, weight, came, *refs):
    dk = sz.dk
    partials, kept = refs[: blocks - 1], refs[blocks - 1]
    gated = []
    for h in range(sz.heads):
        lanes = slice(h * dk, (h + 1) * dk)
        narrow = unpack(sz, came, h, range(sz.steps))
        total = [narrow[quarter] for quarter in sorted(narrow)]
        spare = sz.read_rows - len(total) * sz.back_rows
        if spare:
            total.append(jnp.zeros((spare, dk), F32))
        total = jnp.concatenate(total, axis=0)
        scaling = lax.rsqrt(jnp.mean(total * total, axis=1, keepdims=True) + EPSILON)
        gated.append(total * scaling * factor[:, lanes])
    gated = jnp.concatenate(gated, axis=1).astype(BF16)
    kept[...] = gated
    for shift in range(1, blocks):
        project(sz, blocks, shift, gated, weight, partials[shift - 1])


def project(sz, blocks, shift, gated, weight, partial):
    columns = weight.shape[1] // blocks
    lanes = slice(None)
    if blocks > 1:
        at = lax.rem(lax.axis_index("head") + shift, blocks) * columns
        lanes = pl.ds(pl.multiple_of(at, LANES), columns)
    result = dot(gated, weight[:, lanes])
    for t in range(sz.steps):
        rows = [result[at : at + 1] for at in (sz.read_at(t, r) for r in range(sz.rows))]
        partial[t] = jnp.concatenate(rows, axis=0).astype(partial.dtype)


def restore_kernel(sz, blocks, gated, weight, came, states, partial, hist):
    project(sz, blocks, 0, gated[...], weight, partial)
    for h in range(sz.heads):
        narrow = unpack(sz, came, h, range(sz.steps, sz.back_sets))
        for tap in range(sz.taps):
            for part in range(sz.parts):
                index = sz.steps + tap * sz.parts + part
                held = narrow[index // sz.back_depth]
                at = index % sz.back_depth
                rows = [held[at + r * sz.back_depth :][:1] for r in range(sz.rows)]
                value = jnp.concatenate(rows, axis=0)
                hist[tap, part, :, h * sz.dk : (h + 1) * sz.dk] = value.astype(BF16)
    kind = BF16 if sz.whole_tiles else F32
    for r in range(sz.rows):
        for h in range(sz.heads):
            cuts = [
                came[sz.place_of[h * sz.cuts + cut], : sz.state_rows, :].astype(kind)[
                    r * sz.cols : (r + 1) * sz.cols
                ]
                for cut in range(sz.cuts)
            ]
            states[r, h] = jnp.concatenate(cuts, axis=0).T.astype(F32)


def vmem():
    return pl.BlockSpec(memory_space=pltpu.VMEM)


def smem():
    return pl.BlockSpec(memory_space=pltpu.SMEM)


def anywhere():
    return pl.BlockSpec(memory_space=pl.ANY)


def in_hbm(value):
    return pltpu.with_memory_space_constraint(value, pltpu.HBM)


def call(body, outs, ins, out_specs, scratch, name):
    return pl.pallas_call(
        body,
        out_shape=outs,
        in_specs=ins,
        out_specs=out_specs,
        scratch_shapes=scratch,
        compiler_params=pltpu.CompilerParams(vmem_limit_bytes=VMEM_LIMIT),
        name=name,
    )


def exchange(sz, pieces):
    return lax.all_to_all(
        pieces, "rep", split_axis=0, concat_axis=0, axis_index_groups=[sz.order], tiled=True
    )


def local(
    group_total,
    head_total,
    states,
    conv_states,
    projected,
    conv_weight,
    decay_input,
    decay_rate,
    beta_logit,
    out_gate,
    norm_gain,
    out_weight,
    destinations,
    live_counts,
):
    sz = Sizes(group_total, states, conv_states, projected)
    n, channels = sz.groups, sz.heads * sz.dk
    shape = jax.ShapeDtypeStruct
    lives = live_counts.T
    arguments = (
        destinations,
        lives,
        decay_rate.reshape(1, sz.heads),
        beta_logit.transpose(1, 2, 0),
        projected.transpose(0, 2, 1, 3),
        conv_states.transpose(1, 2, 0, 3),
        decay_input,
        conv_weight.transpose(1, 0, 2),
        states,
    )
    routes = shape((sz.steps, sz.slots, sz.slots), BF16)
    pieces, pick, place, final, taps = call(
        functools.partial(pack_kernel, sz),
        (
            shape((n, sz.state_rows + sz.info_rows, sz.dk), BF16),
            routes,
            routes,
            shape((8, sz.slots), jnp.int32),
            shape((sz.parts, sz.taps + 1, sz.dk), F32),
        ),
        [anywhere()] * len(arguments),
        (vmem(),) * 5,
        [pltpu.VMEM(x.shape, x.dtype) for x in arguments]
        + [
            pltpu.VMEM((sz.heads, sz.info_rows, sz.dk), F32),
            pltpu.VMEM((3, sz.heads, sz.info_rows, sz.dk), F32),
            pltpu.VMEM((sz.heads, sz.dk), F32),
            pltpu.SemaphoreType.DMA((len(arguments) - 1 + sz.rows * sz.heads,)),
        ],
        "pack",
    )(*[in_hbm(x) for x in arguments])
    came = exchange(sz, pieces)
    gain = norm_gain.reshape(1, sz.dk)
    stepped, factor = call(
        functools.partial(step_kernel, sz),
        (
            shape((n, sz.state_rows + sz.back_rows, sz.dk), BF16),
            shape((sz.read_rows, channels), F32),
        ),
        [vmem()] * 4 + [anywhere()] * 4,
        (vmem(), vmem()),
        [
            pltpu.SMEM((8, sz.slots), jnp.int32),
            pltpu.VMEM(lives.shape, lives.dtype),
            pltpu.VMEM(gain.shape, F32),
            pltpu.VMEM(out_gate.shape, BF16),
            pltpu.VMEM((n * sz.info_rows, sz.dk), F32),
            pltpu.VMEM((8 if sz.whole_tiles else n * sz.state_rows, sz.dk), F32),
            pltpu.VMEM((n * sz.back_rows, sz.dk), F32),
            pltpu.SemaphoreType.DMA((4,)),
        ],
        "steps",
    )(taps, pick, place, came, final, in_hbm(lives), in_hbm(gain), in_hbm(out_gate))
    back = exchange(sz, stepped)
    width = out_weight.shape[1]
    columns = width // head_total
    blocks = head_total if columns % LANES == 0 else 1
    *partials, gated = call(
        functools.partial(project_kernel, sz, blocks),
        tuple(shape((sz.steps, sz.rows, columns), BF16) for _ in range(1, blocks))
        + (shape((sz.read_rows, channels), BF16),),
        [vmem()] * 3,
        tuple([vmem()] * blocks),
        [],
        "project",
    )(factor, out_weight, back)
    states_out, own, conv_out = call(
        functools.partial(restore_kernel, sz, blocks),
        (
            shape(states.shape, F32),
            shape((sz.steps, sz.rows, width // blocks), F32),
            shape((sz.taps, sz.parts, sz.rows, channels), BF16),
        ),
        [vmem()] * 3,
        (vmem(),) * 3,
        [],
        "restore",
    )(gated, out_weight, back)
    partials = [own, *partials]
    if blocks != head_total:
        mine = lax.axis_index("head")
        partials = [
            lax.dynamic_slice_in_dim(
                partials[0], lax.rem(mine + shift, head_total) * columns, columns, 2
            )
            for shift in range(head_total)
        ]
    total = partials[0]
    for shift in range(1, head_total):
        pairs = [(i, (i + shift) % head_total) for i in range(head_total)]
        passed = lax.ppermute(partials[shift].astype(BF16), "head", pairs)
        total = total + passed.astype(F32)
    return (total.astype(BF16), states_out, conv_out.transpose(2, 0, 1, 3))


def solution(mesh):
    placed = (
        P("rep", "head", None, None),
        P("rep", None, None, "head"),
        P(None, "rep", None, "head"),
        P(None, None, "head"),
        P(None, "rep", "head"),
        P("head"),
        P(None, "rep", "head"),
        P(None, "rep", "head"),
        P(),
        P("head", None),
        P(),
        P(None, "rep"),
    )
    return jax.shard_map(
        functools.partial(local, mesh.shape["rep"], mesh.shape["head"]),
        mesh=mesh,
        in_specs=placed,
        out_specs=(
            P(None, "rep", "head"),
            P("rep", "head", None, None),
            P("rep", None, None, "head"),
        ),
        check_vma=False,
    )
```

```python
import functools

import jax
import jax.numpy as jnp
from jax import lax
from jax.experimental import pallas as pl
from jax.experimental.pallas import tpu as pltpu
from jax.sharding import PartitionSpec as P

EPSILON = 1e-06
LANES = 128
VMEM_LIMIT = 32 * 1024 * 1024
F32 = jnp.float32
BF16 = jnp.bfloat16


def round_up(value, multiple):
    return -(-value // multiple) * multiple


def power_of_two(value):
    return value & (value - 1) == 0


class Sizes:
    def __init__(self, group_total, states, conv_states, projected):
        self.groups = n = group_total
        self.rows, self.heads, self.dk, _ = states.shape
        self.taps, self.parts = conv_states.shape[1:3]
        self.steps = projected.shape[0]
        self.slots = n * self.rows
        self.cuts = n // self.heads
        far = range(self.heads)
        if power_of_two(self.heads):
            far = [h ^ (h >> 1) for h in far]
        self.order = [h * self.cuts + cut for cut in range(self.cuts) for h in far]
        self.place_of = [self.order.index(p) for p in range(n)]
        self.cols = self.dk // self.cuts
        self.state_rows = self.rows * self.cols
        self.quarter = self.dk // 4
        self.decay_at = self.steps * 2
        self.hist_at = self.decay_at + self.steps
        self.value_at = self.hist_at + self.taps * 2
        self.value_depth = -(-(self.steps + self.taps) // 4)
        self.flag_at = self.value_at + self.value_depth
        self.info_sets = self.padded(self.flag_at + 1)
        self.info_rows = self.rows * self.info_sets
        self.back_sets = self.steps + self.taps * self.parts
        self.back_depth = self.padded(-(-self.back_sets // 4))
        self.back_rows = self.rows * self.back_depth
        self.read_rows = round_up(-(-self.steps // self.back_depth) * self.back_rows, 16)
        self.whole_tiles = self.cols % 16 == 0
        self.width = max(LANES, 8 * self.cols)
        self.tile = self.width // self.cols

    def padded(self, sets):
        while sets * self.rows % 8:
            sets += 1
        return sets

    def read_at(self, t, r):
        return t // self.back_depth * self.back_rows + r * self.back_depth + t % self.back_depth


def mod(value, size):
    return value & (size - 1) if size & (size - 1) == 0 else lax.rem(value, size)


def quotient(value, size):
    if size & (size - 1) == 0:
        return lax.shift_right_logical(value, jnp.int32(size.bit_length() - 1))
    return lax.div(value, jnp.int32(size))


def in_block(sz, shape, cut, shift):
    start = cut * sz.cols + shift * sz.quarter
    return mod(iota(shape, len(shape) - 1) + (2 * sz.dk - start), sz.dk) < sz.cols


def iota(shape, dim):
    return lax.broadcasted_iota(jnp.int32, shape, dim)


def one_hot(condition):
    return jnp.where(condition, 1.0, 0.0).astype(BF16)


def dot(lhs, rhs, lhs_dim=1, rhs_dim=0):
    return lax.dot_general(
        lhs, rhs, (((lhs_dim,), (rhs_dim,)), ((), ())), preferred_element_type=F32
    )


def pack_kernel(sz, *refs):
    count = 8
    sources, states_hbm = refs[:count], refs[count]
    pieces, place, taps = refs[count + 1 : count + 4]
    scratch = refs[count + 4 :]
    targets, live, rate, beta, proj, hist, decay, filters, states = scratch[: count + 1]
    info, tails, strengths, in_sems = scratch[count + 1 :]
    copies = []

    def start(source, target):
        copies.append(pltpu.make_async_copy(source, target, in_sems.at[len(copies)]))
        copies[-1].start()

    for source, target in zip(sources, scratch):
        start(source, target)
    for r in range(sz.rows):
        for h in range(sz.heads):
            start(states_hbm.at[r, h], states.at[r, h])
    for copy in copies[:count]:
        copy.wait()
    own_head = lax.axis_index("rep") // sz.cuts
    head_lanes = pl.ds(pl.multiple_of(own_head * sz.dk, sz.dk), sz.dk)
    for part in range(sz.parts):
        taps[part] = filters[part, :, head_lanes]
    channels, dk = sz.heads * sz.dk, sz.dk
    lane_head = quotient(iota((1, channels), 1), dk)
    rates = jnp.zeros((1, channels), F32)
    for h in range(sz.heads):
        rates = jnp.where(lane_head == h, rate[:, h : h + 1], rates)
    row_ids = iota((sz.rows, channels), 0)

    def keep(target, index, value):
        for h in range(sz.heads):
            rows = pl.ds(index, sz.rows, stride=sz.info_sets)
            target[h, rows, :] = value[:, h * dk : (h + 1) * dk]

    def keep_value(index, value):
        shift = index // sz.value_depth
        at = sz.value_at + index % sz.value_depth
        if shift:
            heads = [value[:, h * dk : (h + 1) * dk] for h in range(sz.heads)]
            heads = [pltpu.roll(head, shift * sz.quarter, 1) for head in heads]
            keep(tails.at[shift - 1], at, jnp.concatenate(heads, axis=1))
        else:
            keep(info, at, value)

    for t in range(sz.steps):
        for part in range(2):
            keep(info, t * 2 + part, proj[t, part].astype(F32))
        keep_value(t, proj[t, 2].astype(F32))
        x = decay[t]
        softplus = jnp.maximum(x, 0.0) + jnp.log1p(jnp.exp(-jnp.abs(x)))
        keep(
            info,
            sz.decay_at + t,
            jnp.where(row_ids < live[:, t : t + 1], rates * softplus, 0.0),
        )
    for tap in range(sz.taps):
        for part in range(2):
            keep(info, sz.hist_at + tap * 2 + part, hist[tap, part].astype(F32))
        keep_value(sz.steps + tap, hist[tap, 2].astype(F32))
    lane = iota((sz.heads, dk), 1)
    strengths[...] = jnp.zeros(strengths.shape, F32)
    for r in range(sz.rows):
        strengths[:, : sz.steps] = beta[r]
        lives = jnp.zeros((sz.heads, dk), F32)
        for t in range(sz.steps):
            lives = jnp.where((lane == t) & (r < live[:, t : t + 1]), 1.0, lives)
        strength = lives / (1.0 + jnp.exp(-strengths[...]))
        high = strength.astype(BF16).astype(F32)
        flags = high + pltpu.roll(lives, 16, 1) + pltpu.roll(strength - high, 32, 1)
        for h in range(sz.heads):
            at = r * sz.info_sets + sz.flag_at
            info[h, at : at + 1, :] = flags[h : h + 1]
    wide = [
        r * sz.info_sets + sz.value_at + i for r in range(sz.rows) for i in range(sz.value_depth)
    ]
    masks = {}
    for tile in sorted({at // 8 for at in wide}):
        row = iota((8, dk), 0) + tile * 8
        narrow = functools.reduce(jnp.logical_or, [row == at for at in wide if at // 8 == tile])
        masks[tile] = [
            [narrow & in_block(sz, (8, dk), cut, shift) for shift in range(1, 4)]
            for cut in range(sz.cuts)
        ]
    shared = [
        at for at in range(0, sz.info_rows, 16) if at // 8 not in masks and at // 8 + 1 not in masks
    ]
    held = [[info[h, at : at + 16, :].astype(BF16) for at in shared] for h in range(sz.heads)]
    for copy in copies[count:]:
        copy.wait()
    route(sz, targets, place)
    for h in range(sz.heads):
        across = [states[r, h].T for r in range(sz.rows)]
        for cut in range(sz.cuts):
            p, at = sz.place_of[h * sz.cuts + cut], cut * sz.cols
            own = [a[at : at + sz.cols] for a in across]
            pieces[p, : sz.state_rows, :] = jnp.concatenate(own, axis=0).astype(BF16)
            for at, value in zip(shared, held[h]):
                to = sz.state_rows + at
                pieces[p, to : to + value.shape[0], :] = value
            for at in range(0, sz.info_rows, 16):
                if at in shared:
                    continue
                rest = []
                for tile in range(at // 8, min(at + 16, sz.info_rows) // 8):
                    rows = slice(tile * 8, tile * 8 + 8)
                    value = info[h, rows, :]
                    for shift in range(3 if tile in masks else 0):
                        value = jnp.where(masks[tile][cut][shift], tails[shift, h, rows, :], value)
                    rest.append(value)
                rest = jnp.concatenate(rest, axis=0)
                to = sz.state_rows + at
                pieces[p, to : to + rest.shape[0], :] = rest.astype(BF16)


def route(sz, targets, place):
    n, T = sz.slots, sz.steps
    steps = [one_hot(iota((n, n), 0) == targets[t : t + 1, :]) for t in range(T)]
    chain = [steps[0]]
    for t in range(1, T):
        if t % 2:
            pair = dot(steps[t], steps[t - 1]).astype(BF16)
            chain.append(dot(pair, chain[t - 2]).astype(BF16) if t > 1 else pair)
        else:
            chain.append(dot(steps[t], chain[t - 1]).astype(BF16))
    for t in range(T):
        place[t] = chain[t]


def final_places(sz, place):
    slot = iota((8, sz.slots), 1)
    row, group = mod(slot, sz.rows), quotient(slot, sz.rows)
    head, cut = quotient(group, sz.cuts), mod(group, sz.cuts)
    far = head
    step = 1
    while power_of_two(sz.heads) and step < sz.heads:
        far = far ^ lax.shift_right_logical(far, jnp.int32(step))
        step *= 2
    weights = (cut * sz.heads + far) * sz.rows + row
    places = dot(weights.astype(F32).astype(BF16), place)
    return (places + 0.5).astype(jnp.int32)


def over_blocks(sz, value):
    step = sz.cols
    while step < sz.dk:
        value = value + pltpu.roll(value, step, 1)
        step *= 2
    return value


def gate_factor(sz, live, gain, gate, factor):
    factor[...] = jnp.zeros(factor.shape, F32)
    row = iota((sz.read_rows, sz.dk), 0)
    alive = row < 0
    for t in range(sz.steps):
        for r in range(sz.rows):
            at = sz.read_at(t, r)
            factor[at : at + 1, :] = gate[t, r : r + 1].astype(F32)
            alive = alive | ((row == at) & (r < live[:, t : t + 1]))
    for h in range(sz.heads):
        lanes = slice(h * sz.dk, (h + 1) * sz.dk)
        gates = gain[...] / (1.0 + jnp.exp(-factor[:, lanes]))
        factor[:, lanes] = jnp.where(alive, gates, 0.0)


def step_kernel(sz, filters, place, came, *refs):
    count = sz.groups
    sources, sent, factor, scratch = refs[:3], refs[3], refs[4], refs[5:]
    live, gain, gate, final, scalars, info, later, back, sems = scratch
    copies = []

    def start(source, target):
        copies.append(pltpu.make_async_copy(source, target, sems.at[len(copies)]))
        copies[-1].start()

    for source, target in zip(sources, scratch):
        start(source, target)
    n, dk, T = sz.slots, sz.dk, sz.steps
    mine = lax.axis_index("rep")
    cut = lax.rem(mine, sz.cuts)
    stride = sz.info_rows
    for g in range(count):
        info[g * stride : (g + 1) * stride, :] = came[sz.place_of[g], sz.state_rows :, :].astype(F32)

    def gather(index):
        return info[pl.ds(index, n, stride=sz.info_sets), :]

    def gather_value(index):
        value = gather(sz.value_at + index % sz.value_depth)
        shift = index // sz.value_depth
        return pltpu.roll(value, dk - shift * sz.quarter, 1) if shift else value

    final[...] = final_places(sz, place[T - 1])
    start(final, scalars)
    weights = [filters[part] for part in range(sz.parts)]
    flags = gather(sz.flag_at)
    window = [
        [gather(sz.hist_at + tap * 2 + part) for part in range(2)]
        + [gather_value(T + tap)]
        for tap in range(sz.taps)
    ]
    active, retains, strengths = [], [], []
    for t in range(T):
        slots = [gather(t * 2 + part) for part in range(2)]
        slots += [gather_value(t), gather(sz.decay_at + t), flags]
        moved = dot(place[t], jnp.concatenate(slots, axis=1).astype(BF16), 0, 0)
        inputs = [moved[:, i * dk : (i + 1) * dk] for i in range(sz.parts + 2)]
        moved_flags = inputs[sz.parts + 1]
        strength = moved_flags[:, t : t + 1] + moved_flags[:, 32 + t : 33 + t]
        alive = moved_flags[:, 16 + t : 17 + t] > 0.5
        for part in range(sz.parts):
            frames = [window[tap][part] for tap in range(sz.taps)] + [inputs[part]]
            total = frames[0] * weights[part][:1]
            for j in range(1, sz.taps + 1):
                total = total + frames[j] * weights[part][j : j + 1]
            active.append(total / (1.0 + jnp.exp(-total)))
            for tap in range(sz.taps):
                window[tap][part] = jnp.where(alive, frames[tap + 1], frames[tap])
        retains.append(jnp.exp(-inputs[sz.parts]))
        strengths.append(strength)

    ones = jnp.ones((dk, dk), BF16)

    def summed(products):
        sums = dot(jnp.concatenate([x.astype(BF16) for x in products], axis=0), ones)
        return [sums[i * n : (i + 1) * n] for i in range(len(products))]

    values = active[2 :: sz.parts]
    units = [x for i, x in enumerate(active) if i % sz.parts < 2]
    norms = summed([x * x for x in units])
    units = [x * lax.rsqrt(norm + EPSILON) for x, norm in zip(units, norms)]
    reach = jnp.ones((n, dk), F32)
    keys = []
    from_state, pairs = [], []
    for t in range(T):
        query, key = units[2 * t], units[2 * t + 1]
        reach = reach * retains[t]
        keys = [k * retains[t] for k in keys]
        pairs += [key * k for k in keys]
        keys.append(key)
        pairs += [query * k for k in keys]
        from_state += [reach * key, reach * query]
    mixes = summed(pairs)
    key_mix, read_mix = [], []
    for t in range(T):
        key_mix.append(mixes[:t])
        read_mix.append(mixes[t : 2 * t + 1])
        mixes = mixes[2 * t + 1 :]

    own_lanes = in_block(sz, (n, dk), cut, 0)
    wide = sz.width // dk
    value_cols = []
    for value in values:
        value = over_blocks(sz, jnp.where(own_lanes, value, 0.0))
        value_cols.append(jnp.concatenate([value] * wide, axis=1))
    for copy in copies:
        copy.wait()
    gate_factor(sz, live, gain, gate, factor)
    lane_row = quotient(iota((sz.tile, sz.width), 1), sz.cols)
    own = iota((sz.tile, sz.width), 0) == lane_row
    readouts = [[] for _ in range(T)]

    def widen(value):
        return jnp.concatenate([value] * wide, axis=1)

    for at in range(0, n, sz.tile):
        rows = slice(at, at + sz.tile)
        block = []
        for g in range(at // sz.rows, (at + sz.tile) // sz.rows):
            for r in range(sz.rows):
                if sz.whole_tiles:
                    block.append(came[sz.place_of[g], r * sz.cols : (r + 1) * sz.cols, :])
                else:
                    piece = came[sz.place_of[g], : sz.state_rows, :].astype(F32)
                    block.append(piece[r * sz.cols : (r + 1) * sz.cols])
        seen = dot(
            jnp.concatenate([x[rows] for x in from_state], axis=0).astype(BF16),
            jnp.concatenate(block, axis=0).astype(BF16),
            1,
            1,
        )
        seen = [seen[i * sz.tile : (i + 1) * sz.tile] for i in range(2 * T)]
        writes = []
        for t in range(T):
            target = value_cols[t][rows] - seen[2 * t]
            target = jnp.where(own, target, 0.0)
            for s in range(t):
                target = target - widen(key_mix[t][s][rows]) * writes[s]
            writes.append(strengths[t][rows] * target)
            read = jnp.where(own, seen[2 * t + 1], 0.0)
            for s in range(t + 1):
                read = read + widen(read_mix[t][s][rows]) * writes[s]
            readouts[t].append(read * dk ** (-0.5))
        added = dot(
            jnp.concatenate(writes, axis=0).astype(BF16),
            jnp.concatenate([k[rows] for k in keys], axis=0).astype(BF16),
            0,
            0,
        )
        for i in range(sz.tile):
            part = block[i].astype(F32) * reach[at + i : at + i + 1]
            part = part + added[i * sz.cols : (i + 1) * sz.cols]
            to = scalars[0, at + i]
            if sz.whole_tiles:
                start = pl.multiple_of(mod(to, sz.rows) * sz.cols, sz.cols)
                sent[quotient(to, sz.rows), pl.ds(start, sz.cols), :] = part.astype(BF16)
            else:
                later[pl.ds(pl.multiple_of(to * sz.cols, sz.cols), sz.cols), :] = part
    blocks = [in_block(sz, (n, dk), cut, shift) for shift in range(4)]
    placed = [None] * sz.back_depth
    kept = [None] * sz.back_depth
    for index in range(sz.back_sets):
        shift, slot = index // sz.back_depth, index % sz.back_depth
        if index < T:
            folded = jnp.concatenate(readouts[index], axis=0)
            folded = functools.reduce(
                jnp.add, [folded[:, i * dk : (i + 1) * dk] for i in range(wide)]
            )
            folded = jnp.where(blocks[shift], over_blocks(sz, folded), 0.0)
            value = dot(place[index], folded.astype(BF16))
            placed[slot] = value if placed[slot] is None else placed[slot] + value
        else:
            value = window[(index - T) // sz.parts][(index - T) % sz.parts]
            if shift:
                value = pltpu.roll(value, shift * sz.quarter, 1)
            rest = jnp.zeros((n, dk), F32) if kept[slot] is None else kept[slot]
            kept[slot] = jnp.where(blocks[shift], value, rest)
    kept = [jnp.zeros((n, dk), F32) if value is None else value for value in kept]
    held = dot(place[T - 1], jnp.concatenate(kept, axis=1).astype(BF16))
    for slot in range(sz.back_depth):
        value = held[:, slot * dk : (slot + 1) * dk]
        if placed[slot] is not None:
            value = value + placed[slot]
        back[pl.ds(slot, n, stride=sz.back_depth), :] = value
    for g in range(count):
        p = sz.place_of[g]
        if not sz.whole_tiles:
            sent[p, : sz.state_rows, :] = later[
                p * sz.state_rows : (p + 1) * sz.state_rows, :
            ].astype(BF16)
        sent[p, sz.state_rows :, :] = back[
            g * sz.back_rows : (g + 1) * sz.back_rows, :
        ].astype(BF16)


def unpack(sz, came, h, wanted):
    shape = (sz.back_rows, sz.dk)
    pieces = [
        came[sz.place_of[h * sz.cuts + cut], sz.state_rows :, :].astype(F32)
        for cut in range(sz.cuts)
    ]
    narrow = {}
    for shift in sorted({index // sz.back_depth for index in wanted}):
        value = pieces[0]
        for cut in range(1, sz.cuts):
            value = jnp.where(in_block(sz, shape, cut, shift), pieces[cut], value)
        if shift:
            value = pltpu.roll(value, sz.dk - shift * sz.quarter, 1)
        narrow[shift] = value

    return narrow


def project_kernel(sz, blocks, factor, weight, came, *refs):
    dk = sz.dk
    partials, kept = refs[: blocks - 1], refs[blocks - 1]
    gated = []
    for h in range(sz.heads):
        lanes = slice(h * dk, (h + 1) * dk)
        narrow = unpack(sz, came, h, range(sz.steps))
        total = [narrow[quarter] for quarter in sorted(narrow)]
        spare = sz.read_rows - len(total) * sz.back_rows
        if spare:
            total.append(jnp.zeros((spare, dk), F32))
        total = jnp.concatenate(total, axis=0)
        scaling = lax.rsqrt(jnp.mean(total * total, axis=1, keepdims=True) + EPSILON)
        gated.append(total * scaling * factor[:, lanes])
    gated = jnp.concatenate(gated, axis=1).astype(BF16)
    kept[...] = gated
    for shift in range(1, blocks):
        project(sz, blocks, shift, gated, weight, partials[shift - 1])


def project(sz, blocks, shift, gated, weight, partial):
    columns = weight.shape[1] // blocks
    lanes = slice(None)
    if blocks > 1:
        at = lax.rem(lax.axis_index("head") + shift, blocks) * columns
        lanes = pl.ds(pl.multiple_of(at, LANES), columns)
    result = dot(gated, weight[:, lanes])
    for t in range(sz.steps):
        rows = [result[at : at + 1] for at in (sz.read_at(t, r) for r in range(sz.rows))]
        partial[t] = jnp.concatenate(rows, axis=0).astype(partial.dtype)


def restore_kernel(sz, blocks, gated, weight, came, states, partial, hist):
    project(sz, blocks, 0, gated[...], weight, partial)
    for h in range(sz.heads):
        narrow = unpack(sz, came, h, range(sz.steps, sz.back_sets))
        for tap in range(sz.taps):
            for part in range(sz.parts):
                index = sz.steps + tap * sz.parts + part
                held = narrow[index // sz.back_depth]
                at = index % sz.back_depth
                rows = [held[at + r * sz.back_depth :][:1] for r in range(sz.rows)]
                value = jnp.concatenate(rows, axis=0)
                hist[tap, part, :, h * sz.dk : (h + 1) * sz.dk] = value.astype(BF16)
    kind = BF16 if sz.whole_tiles else F32
    for r in range(sz.rows):
        for h in range(sz.heads):
            cuts = [
                came[sz.place_of[h * sz.cuts + cut], : sz.state_rows, :].astype(kind)[
                    r * sz.cols : (r + 1) * sz.cols
                ]
                for cut in range(sz.cuts)
            ]
            states[r, h] = jnp.concatenate(cuts, axis=0).T.astype(F32)


def vmem():
    return pl.BlockSpec(memory_space=pltpu.VMEM)


def smem():
    return pl.BlockSpec(memory_space=pltpu.SMEM)


def anywhere():
    return pl.BlockSpec(memory_space=pl.ANY)


def in_hbm(value):
    return pltpu.with_memory_space_constraint(value, pltpu.HBM)


def call(body, outs, ins, out_specs, scratch, name):
    return pl.pallas_call(
        body,
        out_shape=outs,
        in_specs=ins,
        out_specs=out_specs,
        scratch_shapes=scratch,
        compiler_params=pltpu.CompilerParams(vmem_limit_bytes=VMEM_LIMIT),
        name=name,
    )


def exchange(sz, pieces):
    return lax.all_to_all(
        pieces, "rep", split_axis=0, concat_axis=0, axis_index_groups=[sz.order], tiled=True
    )


def local(
    group_total,
    head_total,
    states,
    conv_states,
    projected,
    conv_weight,
    decay_input,
    decay_rate,
    beta_logit,
    out_gate,
    norm_gain,
    out_weight,
    destinations,
    live_counts,
):
    sz = Sizes(group_total, states, conv_states, projected)
    n, channels = sz.groups, sz.heads * sz.dk
    shape = jax.ShapeDtypeStruct
    lives = live_counts.T
    arguments = (
        destinations,
        lives,
        decay_rate.reshape(1, sz.heads),
        beta_logit.transpose(1, 2, 0),
        projected.transpose(0, 2, 1, 3),
        conv_states.transpose(1, 2, 0, 3),
        decay_input,
        conv_weight.transpose(1, 0, 2),
        states,
    )
    pieces, place, taps = call(
        functools.partial(pack_kernel, sz),
        (
            shape((n, sz.state_rows + sz.info_rows, sz.dk), BF16),
            shape((sz.steps, sz.slots, sz.slots), BF16),
            shape((sz.parts, sz.taps + 1, sz.dk), F32),
        ),
        [anywhere()] * len(arguments),
        (vmem(),) * 3,
        [pltpu.VMEM(x.shape, x.dtype) for x in arguments]
        + [
            pltpu.VMEM((sz.heads, sz.info_rows, sz.dk), F32),
            pltpu.VMEM((3, sz.heads, sz.info_rows, sz.dk), F32),
            pltpu.VMEM((sz.heads, sz.dk), F32),
            pltpu.SemaphoreType.DMA((len(arguments) - 1 + sz.rows * sz.heads,)),
        ],
        "pack",
    )(*[in_hbm(x) for x in arguments])
    came = exchange(sz, pieces)
    gain = norm_gain.reshape(1, sz.dk)
    stepped, factor = call(
        functools.partial(step_kernel, sz),
        (
            shape((n, sz.state_rows + sz.back_rows, sz.dk), BF16),
            shape((sz.read_rows, channels), F32),
        ),
        [vmem()] * 3 + [anywhere()] * 3,
        (vmem(), vmem()),
        [
            pltpu.VMEM(lives.shape, lives.dtype),
            pltpu.VMEM(gain.shape, F32),
            pltpu.VMEM(out_gate.shape, BF16),
            pltpu.VMEM((8, sz.slots), jnp.int32),
            pltpu.SMEM((8, sz.slots), jnp.int32),
            pltpu.VMEM((n * sz.info_rows, sz.dk), F32),
            pltpu.VMEM((8 if sz.whole_tiles else n * sz.state_rows, sz.dk), F32),
            pltpu.VMEM((n * sz.back_rows, sz.dk), F32),
            pltpu.SemaphoreType.DMA((4,)),
        ],
        "steps",
    )(taps, place, came, in_hbm(lives), in_hbm(gain), in_hbm(out_gate))
    back = exchange(sz, stepped)
    width = out_weight.shape[1]
    columns = width // head_total
    blocks = head_total if columns % LANES == 0 else 1
    *partials, gated = call(
        functools.partial(project_kernel, sz, blocks),
        tuple(shape((sz.steps, sz.rows, columns), BF16) for _ in range(1, blocks))
        + (shape((sz.read_rows, channels), BF16),),
        [vmem()] * 3,
        tuple([vmem()] * blocks),
        [],
        "project",
    )(factor, out_weight, back)
    states_out, own, conv_out = call(
        functools.partial(restore_kernel, sz, blocks),
        (
            shape(states.shape, F32),
            shape((sz.steps, sz.rows, width // blocks), F32),
            shape((sz.taps, sz.parts, sz.rows, channels), BF16),
        ),
        [vmem()] * 3,
        (vmem(),) * 3,
        [],
        "restore",
    )(gated, out_weight, back)
    partials = [own, *partials]
    if blocks != head_total:
        mine = lax.axis_index("head")
        partials = [
            lax.dynamic_slice_in_dim(
                partials[0], lax.rem(mine + shift, head_total) * columns, columns, 2
            )
            for shift in range(head_total)
        ]
    total = partials[0]
    for shift in range(1, head_total):
        pairs = [(i, (i + shift) % head_total) for i in range(head_total)]
        passed = lax.ppermute(partials[shift].astype(BF16), "head", pairs)
        total = total + passed.astype(F32)
    return (total.astype(BF16), states_out, conv_out.transpose(2, 0, 1, 3))


def solution(mesh):
    placed = (
        P("rep", "head", None, None),
        P("rep", None, None, "head"),
        P(None, "rep", None, "head"),
        P(None, None, "head"),
        P(None, "rep", "head"),
        P("head"),
        P(None, "rep", "head"),
        P(None, "rep", "head"),
        P(),
        P("head", None),
        P(),
        P(None, "rep"),
    )
    return jax.shard_map(
        functools.partial(local, mesh.shape["rep"], mesh.shape["head"]),
        mesh=mesh,
        in_specs=placed,
        out_specs=(
            P(None, "rep", "head"),
            P("rep", "head", None, None),
            P("rep", None, None, "head"),
        ),
        check_vma=False,
    )
```

```python
import functools

import jax
import jax.numpy as jnp
from jax import lax
from jax.experimental import pallas as pl
from jax.experimental.pallas import tpu as pltpu
from jax.sharding import PartitionSpec as P

EPSILON = 1e-06
LANES = 128
VMEM_LIMIT = 32 * 1024 * 1024
F32 = jnp.float32
BF16 = jnp.bfloat16


def round_up(value, multiple):
    return -(-value // multiple) * multiple


def power_of_two(value):
    return value & (value - 1) == 0


class Sizes:
    def __init__(self, group_total, states, conv_states, projected):
        self.groups = n = group_total
        self.rows, self.heads, self.dk, _ = states.shape
        self.taps, self.parts = conv_states.shape[1:3]
        self.steps = projected.shape[0]
        self.slots = n * self.rows
        self.cuts = n // self.heads
        far = range(self.heads)
        if power_of_two(self.heads):
            far = [h ^ (h >> 1) for h in far]
        self.order = [h * self.cuts + cut for cut in range(self.cuts) for h in far]
        self.place_of = [self.order.index(p) for p in range(n)]
        self.cols = self.dk // self.cuts
        self.state_rows = self.rows * self.cols
        self.quarter = self.dk // 4
        self.decay_at = self.steps * 2
        self.hist_at = self.decay_at + self.steps
        self.value_at = self.hist_at + self.taps * 2
        self.value_depth = -(-(self.steps + self.taps) // 4)
        self.flag_at = self.value_at + self.value_depth
        self.info_sets = self.padded(self.flag_at + 1)
        self.info_rows = self.rows * self.info_sets
        self.back_sets = self.steps + self.taps * self.parts
        self.back_depth = self.padded(-(-self.back_sets // 4))
        self.back_rows = self.rows * self.back_depth
        self.read_rows = round_up(-(-self.steps // self.back_depth) * self.back_rows, 16)
        self.whole_tiles = self.cols % 16 == 0
        self.width = max(LANES, 8 * self.cols)
        self.tile = self.width // self.cols

    def padded(self, sets):
        while sets * self.rows % 8:
            sets += 1
        return sets

    def read_at(self, t, r):
        return t // self.back_depth * self.back_rows + r * self.back_depth + t % self.back_depth


def mod(value, size):
    return value & (size - 1) if size & (size - 1) == 0 else lax.rem(value, size)


def quotient(value, size):
    if size & (size - 1) == 0:
        return lax.shift_right_logical(value, jnp.int32(size.bit_length() - 1))
    return lax.div(value, jnp.int32(size))


def in_block(sz, shape, cut, shift):
    start = cut * sz.cols + shift * sz.quarter
    return mod(iota(shape, len(shape) - 1) + (2 * sz.dk - start), sz.dk) < sz.cols


def iota(shape, dim):
    return lax.broadcasted_iota(jnp.int32, shape, dim)


def one_hot(condition):
    return jnp.where(condition, 1.0, 0.0).astype(BF16)


def dot(lhs, rhs, lhs_dim=1, rhs_dim=0):
    return lax.dot_general(
        lhs, rhs, (((lhs_dim,), (rhs_dim,)), ((), ())), preferred_element_type=F32
    )


def pack_kernel(sz, *refs):
    count = 8
    sources, states_hbm = refs[:count], refs[count]
    pieces, pick, place, final, taps = refs[count + 1 : count + 6]
    scratch = refs[count + 6 :]
    targets, live, rate, beta, proj, hist, decay, filters, states = scratch[: count + 1]
    info, tails, strengths, in_sems = scratch[count + 1 :]
    copies = []

    def start(source, target):
        copies.append(pltpu.make_async_copy(source, target, in_sems.at[len(copies)]))
        copies[-1].start()

    for source, target in zip(sources, scratch):
        start(source, target)
    for h in range(sz.heads):
        for r in range(sz.rows):
            start(states_hbm.at[r, h], states.at[r, h])
    for copy in copies[:count]:
        copy.wait()
    route(sz, targets, pick, place, final)
    own_head = lax.axis_index("rep") // sz.cuts
    head_lanes = pl.ds(pl.multiple_of(own_head * sz.dk, sz.dk), sz.dk)
    for part in range(sz.parts):
        taps[part] = filters[part, :, head_lanes]
    channels, dk = sz.heads * sz.dk, sz.dk
    lane_head = quotient(iota((1, channels), 1), dk)
    rates = jnp.zeros((1, channels), F32)
    for h in range(sz.heads):
        rates = jnp.where(lane_head == h, rate[:, h : h + 1], rates)
    row_ids = iota((sz.rows, channels), 0)

    def keep(target, index, value):
        for h in range(sz.heads):
            rows = pl.ds(index, sz.rows, stride=sz.info_sets)
            target[h, rows, :] = value[:, h * dk : (h + 1) * dk]

    def keep_value(index, value):
        shift = index // sz.value_depth
        at = sz.value_at + index % sz.value_depth
        if shift:
            heads = [value[:, h * dk : (h + 1) * dk] for h in range(sz.heads)]
            heads = [pltpu.roll(head, shift * sz.quarter, 1) for head in heads]
            keep(tails.at[shift - 1], at, jnp.concatenate(heads, axis=1))
        else:
            keep(info, at, value)

    for t in range(sz.steps):
        for part in range(2):
            keep(info, t * 2 + part, proj[t, part].astype(F32))
        keep_value(t, proj[t, 2].astype(F32))
        x = decay[t]
        softplus = jnp.maximum(x, 0.0) + jnp.log1p(jnp.exp(-jnp.abs(x)))
        keep(
            info,
            sz.decay_at + t,
            jnp.where(row_ids < live[:, t : t + 1], rates * softplus, 0.0),
        )
    for tap in range(sz.taps):
        for part in range(2):
            keep(info, sz.hist_at + tap * 2 + part, hist[tap, part].astype(F32))
        keep_value(sz.steps + tap, hist[tap, 2].astype(F32))
    lane = iota((sz.heads, dk), 1)
    strengths[...] = jnp.zeros(strengths.shape, F32)
    for r in range(sz.rows):
        strengths[:, : sz.steps] = beta[r]
        lives = jnp.zeros((sz.heads, dk), F32)
        for t in range(sz.steps):
            lives = jnp.where((lane == t) & (r < live[:, t : t + 1]), 1.0, lives)
        strength = lives / (1.0 + jnp.exp(-strengths[...]))
        high = strength.astype(BF16).astype(F32)
        flags = high + pltpu.roll(lives, 16, 1) + pltpu.roll(strength - high, 32, 1)
        for h in range(sz.heads):
            at = r * sz.info_sets + sz.flag_at
            info[h, at : at + 1, :] = flags[h : h + 1]
    wide = [
        r * sz.info_sets + sz.value_at + i for r in range(sz.rows) for i in range(sz.value_depth)
    ]
    masks = {}
    for tile in sorted({at // 8 for at in wide}):
        row = iota((8, dk), 0) + tile * 8
        narrow = functools.reduce(jnp.logical_or, [row == at for at in wide if at // 8 == tile])
        masks[tile] = [
            [narrow & in_block(sz, (8, dk), cut, shift) for shift in range(1, 4)]
            for cut in range(sz.cuts)
        ]
    shared = [
        at for at in range(0, sz.info_rows, 16) if at // 8 not in masks and at // 8 + 1 not in masks
    ]
    held = [[info[h, at : at + 16, :].astype(BF16) for at in shared] for h in range(sz.heads)]
    for h in range(sz.heads):
        for copy in copies[count + h * sz.rows :][: sz.rows]:
            copy.wait()
        across = [states[r, h].T for r in range(sz.rows)]
        for cut in range(sz.cuts):
            p, at = sz.place_of[h * sz.cuts + cut], cut * sz.cols
            own = [a[at : at + sz.cols] for a in across]
            pieces[p, : sz.state_rows, :] = jnp.concatenate(own, axis=0).astype(BF16)
            for at, value in zip(shared, held[h]):
                to = sz.state_rows + at
                pieces[p, to : to + value.shape[0], :] = value
            for at in range(0, sz.info_rows, 16):
                if at in shared:
                    continue
                rest = []
                for tile in range(at // 8, min(at + 16, sz.info_rows) // 8):
                    rows = slice(tile * 8, tile * 8 + 8)
                    value = info[h, rows, :]
                    for shift in range(3 if tile in masks else 0):
                        value = jnp.where(masks[tile][cut][shift], tails[shift, h, rows, :], value)
                    rest.append(value)
                rest = jnp.concatenate(rest, axis=0)
                to = sz.state_rows + at
                pieces[p, to : to + rest.shape[0], :] = rest.astype(BF16)


def route(sz, targets, pick, place, final):
    n, T = sz.slots, sz.steps
    steps = [one_hot(iota((n, n), 0) == targets[t : t + 1, :]) for t in range(T)]
    chain = [steps[0]]
    for t in range(1, T):
        if t % 2:
            pair = dot(steps[t], steps[t - 1]).astype(BF16)
            chain.append(dot(pair, chain[t - 2]).astype(BF16) if t > 1 else pair)
        else:
            chain.append(dot(steps[t], chain[t - 1]).astype(BF16))
    for t in range(T):
        place[t] = chain[t]
        pick[t] = chain[t].astype(F32).T.astype(BF16)
    slot = iota((8, n), 1)
    row, group = mod(slot, sz.rows), quotient(slot, sz.rows)
    head, cut = quotient(group, sz.cuts), mod(group, sz.cuts)
    far = head
    step = 1
    while power_of_two(sz.heads) and step < sz.heads:
        far = far ^ lax.shift_right_logical(far, jnp.int32(step))
        step *= 2
    weights = (cut * sz.heads + far) * sz.rows + row
    places = dot(weights.astype(F32).astype(BF16), chain[T - 1])
    final[...] = (places + 0.5).astype(jnp.int32)


def over_blocks(sz, value):
    step = sz.cols
    while step < sz.dk:
        value = value + pltpu.roll(value, step, 1)
        step *= 2
    return value


def gate_factor(sz, live, gain, gate, factor):
    factor[...] = jnp.zeros(factor.shape, F32)
    row = iota((sz.read_rows, sz.dk), 0)
    alive = row < 0
    for t in range(sz.steps):
        for r in range(sz.rows):
            at = sz.read_at(t, r)
            factor[at : at + 1, :] = gate[t, r : r + 1].astype(F32)
            alive = alive | ((row == at) & (r < live[:, t : t + 1]))
    for h in range(sz.heads):
        lanes = slice(h * sz.dk, (h + 1) * sz.dk)
        gates = gain[...] / (1.0 + jnp.exp(-factor[:, lanes]))
        factor[:, lanes] = jnp.where(alive, gates, 0.0)


def step_kernel(sz, filters, pick, place, came, *refs):
    count = sz.groups
    sources, sent, factor, scratch = refs[:4], refs[4], refs[5], refs[6:]
    scalars, live, gain, gate, info, later, back, sems = scratch
    copies = []
    for i, (source, target) in enumerate(zip(sources, scratch)):
        copies.append(pltpu.make_async_copy(source, target, sems.at[i]))
        copies[-1].start()
    n, dk, T = sz.slots, sz.dk, sz.steps
    mine = lax.axis_index("rep")
    cut = lax.rem(mine, sz.cuts)
    stride = sz.info_rows
    for g in range(count):
        info[g * stride : (g + 1) * stride, :] = came[sz.place_of[g], sz.state_rows :, :].astype(F32)

    def gather(index):
        return info[pl.ds(index, n, stride=sz.info_sets), :]

    def gather_value(index):
        value = gather(sz.value_at + index % sz.value_depth)
        shift = index // sz.value_depth
        return pltpu.roll(value, dk - shift * sz.quarter, 1) if shift else value

    weights = [filters[part] for part in range(sz.parts)]
    flags = gather(sz.flag_at)
    window = [
        [gather(sz.hist_at + tap * 2 + part) for part in range(2)]
        + [gather_value(T + tap)]
        for tap in range(sz.taps)
    ]
    active, retains, strengths = [], [], []
    for t in range(T):
        slots = [gather(t * 2 + part) for part in range(2)]
        slots += [gather_value(t), gather(sz.decay_at + t), flags]
        moved = dot(pick[t], jnp.concatenate(slots, axis=1).astype(BF16))
        inputs = [moved[:, i * dk : (i + 1) * dk] for i in range(sz.parts + 2)]
        moved_flags = inputs[sz.parts + 1]
        strength = moved_flags[:, t : t + 1] + moved_flags[:, 32 + t : 33 + t]
        alive = moved_flags[:, 16 + t : 17 + t] > 0.5
        for part in range(sz.parts):
            frames = [window[tap][part] for tap in range(sz.taps)] + [inputs[part]]
            total = frames[0] * weights[part][:1]
            for j in range(1, sz.taps + 1):
                total = total + frames[j] * weights[part][j : j + 1]
            active.append(total / (1.0 + jnp.exp(-total)))
            for tap in range(sz.taps):
                window[tap][part] = jnp.where(alive, frames[tap + 1], frames[tap])
        retains.append(jnp.exp(-inputs[sz.parts]))
        strengths.append(strength)

    ones = jnp.ones((dk, dk), BF16)

    def summed(products):
        sums = dot(jnp.concatenate([x.astype(BF16) for x in products], axis=0), ones)
        return [sums[i * n : (i + 1) * n] for i in range(len(products))]

    values = active[2 :: sz.parts]
    units = [x for i, x in enumerate(active) if i % sz.parts < 2]
    norms = summed([x * x for x in units])
    units = [x * lax.rsqrt(norm + EPSILON) for x, norm in zip(units, norms)]
    reach = jnp.ones((n, dk), F32)
    keys = []
    from_state, pairs = [], []
    for t in range(T):
        query, key = units[2 * t], units[2 * t + 1]
        reach = reach * retains[t]
        keys = [k * retains[t] for k in keys]
        pairs += [key * k for k in keys]
        keys.append(key)
        pairs += [query * k for k in keys]
        from_state += [reach * key, reach * query]
    mixes = summed(pairs)
    key_mix, read_mix = [], []
    for t in range(T):
        key_mix.append(mixes[:t])
        read_mix.append(mixes[t : 2 * t + 1])
        mixes = mixes[2 * t + 1 :]

    own_lanes = in_block(sz, (n, dk), cut, 0)
    wide = sz.width // dk
    value_cols = []
    for value in values:
        value = over_blocks(sz, jnp.where(own_lanes, value, 0.0))
        value_cols.append(jnp.concatenate([value] * wide, axis=1))
    for copy in copies:
        copy.wait()
    gate_factor(sz, live, gain, gate, factor)
    lane_row = quotient(iota((sz.tile, sz.width), 1), sz.cols)
    own = iota((sz.tile, sz.width), 0) == lane_row
    readouts = [[] for _ in range(T)]

    def widen(value):
        return jnp.concatenate([value] * wide, axis=1)

    for at in range(0, n, sz.tile):
        rows = slice(at, at + sz.tile)
        block = []
        for g in range(at // sz.rows, (at + sz.tile) // sz.rows):
            for r in range(sz.rows):
                if sz.whole_tiles:
                    block.append(came[sz.place_of[g], r * sz.cols : (r + 1) * sz.cols, :])
                else:
                    piece = came[sz.place_of[g], : sz.state_rows, :].astype(F32)
                    block.append(piece[r * sz.cols : (r + 1) * sz.cols])
        seen = dot(
            jnp.concatenate([x[rows] for x in from_state], axis=0).astype(BF16),
            jnp.concatenate(block, axis=0).astype(BF16),
            1,
            1,
        )
        seen = [seen[i * sz.tile : (i + 1) * sz.tile] for i in range(2 * T)]
        writes = []
        for t in range(T):
            target = value_cols[t][rows] - seen[2 * t]
            target = jnp.where(own, target, 0.0)
            for s in range(t):
                target = target - widen(key_mix[t][s][rows]) * writes[s]
            writes.append(strengths[t][rows] * target)
            read = jnp.where(own, seen[2 * t + 1], 0.0)
            for s in range(t + 1):
                read = read + widen(read_mix[t][s][rows]) * writes[s]
            readouts[t].append(read * dk ** (-0.5))
        added = dot(
            jnp.concatenate(writes, axis=0).astype(BF16),
            jnp.concatenate([k[rows] for k in keys], axis=0).astype(BF16),
            0,
            0,
        )
        for i in range(sz.tile):
            part = block[i].astype(F32) * reach[at + i : at + i + 1]
            part = part + added[i * sz.cols : (i + 1) * sz.cols]
            to = scalars[0, at + i]
            if sz.whole_tiles:
                start = pl.multiple_of(mod(to, sz.rows) * sz.cols, sz.cols)
                sent[quotient(to, sz.rows), pl.ds(start, sz.cols), :] = part.astype(BF16)
            else:
                later[pl.ds(pl.multiple_of(to * sz.cols, sz.cols), sz.cols), :] = part
    blocks = [in_block(sz, (n, dk), cut, shift) for shift in range(4)]
    placed = [None] * sz.back_depth
    kept = [None] * sz.back_depth
    for index in range(sz.back_sets):
        shift, slot = index // sz.back_depth, index % sz.back_depth
        if index < T:
            folded = jnp.concatenate(readouts[index], axis=0)
            folded = functools.reduce(
                jnp.add, [folded[:, i * dk : (i + 1) * dk] for i in range(wide)]
            )
            folded = jnp.where(blocks[shift], over_blocks(sz, folded), 0.0)
            value = dot(place[index], folded.astype(BF16))
            placed[slot] = value if placed[slot] is None else placed[slot] + value
        else:
            value = window[(index - T) // sz.parts][(index - T) % sz.parts]
            if shift:
                value = pltpu.roll(value, shift * sz.quarter, 1)
            rest = jnp.zeros((n, dk), F32) if kept[slot] is None else kept[slot]
            kept[slot] = jnp.where(blocks[shift], value, rest)
    kept = [jnp.zeros((n, dk), F32) if value is None else value for value in kept]
    held = dot(place[T - 1], jnp.concatenate(kept, axis=1).astype(BF16))
    for slot in range(sz.back_depth):
        value = held[:, slot * dk : (slot + 1) * dk]
        if placed[slot] is not None:
            value = value + placed[slot]
        back[pl.ds(slot, n, stride=sz.back_depth), :] = value
    for g in range(count):
        p = sz.place_of[g]
        if not sz.whole_tiles:
            sent[p, : sz.state_rows, :] = later[
                p * sz.state_rows : (p + 1) * sz.state_rows, :
            ].astype(BF16)
        sent[p, sz.state_rows :, :] = back[
            g * sz.back_rows : (g + 1) * sz.back_rows, :
        ].astype(BF16)


def unpack(sz, came, h, wanted):
    shape = (sz.back_rows, sz.dk)
    pieces = [
        came[sz.place_of[h * sz.cuts + cut], sz.state_rows :, :].astype(F32)
        for cut in range(sz.cuts)
    ]
    narrow = {}
    for shift in sorted({index // sz.back_depth for index in wanted}):
        value = pieces[0]
        for cut in range(1, sz.cuts):
            value = jnp.where(in_block(sz, shape, cut, shift), pieces[cut], value)
        if shift:
            value = pltpu.roll(value, sz.dk - shift * sz.quarter, 1)
        narrow[shift] = value

    return narrow


def project_kernel(sz, blocks, factor, weight, came, *refs):
    dk = sz.dk
    partials, kept = refs[: blocks - 1], refs[blocks - 1]
    gated = []
    for h in range(sz.heads):
        lanes = slice(h * dk, (h + 1) * dk)
        narrow = unpack(sz, came, h, range(sz.steps))
        total = [narrow[quarter] for quarter in sorted(narrow)]
        spare = sz.read_rows - len(total) * sz.back_rows
        if spare:
            total.append(jnp.zeros((spare, dk), F32))
        total = jnp.concatenate(total, axis=0)
        scaling = lax.rsqrt(jnp.mean(total * total, axis=1, keepdims=True) + EPSILON)
        gated.append(total * scaling * factor[:, lanes])
    gated = jnp.concatenate(gated, axis=1).astype(BF16)
    kept[...] = gated
    for shift in range(1, blocks):
        project(sz, blocks, shift, gated, weight, partials[shift - 1])


def project(sz, blocks, shift, gated, weight, partial):
    columns = weight.shape[1] // blocks
    lanes = slice(None)
    if blocks > 1:
        at = lax.rem(lax.axis_index("head") + shift, blocks) * columns
        lanes = pl.ds(pl.multiple_of(at, LANES), columns)
    result = dot(gated, weight[:, lanes])
    for t in range(sz.steps):
        rows = [result[at : at + 1] for at in (sz.read_at(t, r) for r in range(sz.rows))]
        partial[t] = jnp.concatenate(rows, axis=0).astype(partial.dtype)


def restore_kernel(sz, blocks, gated, weight, came, states, partial, hist):
    project(sz, blocks, 0, gated[...], weight, partial)
    for h in range(sz.heads):
        narrow = unpack(sz, came, h, range(sz.steps, sz.back_sets))
        for tap in range(sz.taps):
            for part in range(sz.parts):
                index = sz.steps + tap * sz.parts + part
                held = narrow[index // sz.back_depth]
                at = index % sz.back_depth
                rows = [held[at + r * sz.back_depth :][:1] for r in range(sz.rows)]
                value = jnp.concatenate(rows, axis=0)
                hist[tap, part, :, h * sz.dk : (h + 1) * sz.dk] = value.astype(BF16)
    kind = BF16 if sz.whole_tiles else F32
    for r in range(sz.rows):
        for h in range(sz.heads):
            cuts = [
                came[sz.place_of[h * sz.cuts + cut], : sz.state_rows, :].astype(kind)[
                    r * sz.cols : (r + 1) * sz.cols
                ]
                for cut in range(sz.cuts)
            ]
            states[r, h] = jnp.concatenate(cuts, axis=0).T.astype(F32)


def vmem():
    return pl.BlockSpec(memory_space=pltpu.VMEM)


def smem():
    return pl.BlockSpec(memory_space=pltpu.SMEM)


def anywhere():
    return pl.BlockSpec(memory_space=pl.ANY)


def in_hbm(value):
    return pltpu.with_memory_space_constraint(value, pltpu.HBM)


def call(body, outs, ins, out_specs, scratch, name):
    return pl.pallas_call(
        body,
        out_shape=outs,
        in_specs=ins,
        out_specs=out_specs,
        scratch_shapes=scratch,
        compiler_params=pltpu.CompilerParams(vmem_limit_bytes=VMEM_LIMIT),
        name=name,
    )


def exchange(sz, pieces):
    return lax.all_to_all(
        pieces, "rep", split_axis=0, concat_axis=0, axis_index_groups=[sz.order], tiled=True
    )


def local(
    group_total,
    head_total,
    states,
    conv_states,
    projected,
    conv_weight,
    decay_input,
    decay_rate,
    beta_logit,
    out_gate,
    norm_gain,
    out_weight,
    destinations,
    live_counts,
):
    sz = Sizes(group_total, states, conv_states, projected)
    n, channels = sz.groups, sz.heads * sz.dk
    shape = jax.ShapeDtypeStruct
    lives = live_counts.T
    arguments = (
        destinations,
        lives,
        decay_rate.reshape(1, sz.heads),
        beta_logit.transpose(1, 2, 0),
        projected.transpose(0, 2, 1, 3),
        conv_states.transpose(1, 2, 0, 3),
        decay_input,
        conv_weight.transpose(1, 0, 2),
        states,
    )
    routes = shape((sz.steps, sz.slots, sz.slots), BF16)
    pieces, pick, place, final, taps = call(
        functools.partial(pack_kernel, sz),
        (
            shape((n, sz.state_rows + sz.info_rows, sz.dk), BF16),
            routes,
            routes,
            shape((8, sz.slots), jnp.int32),
            shape((sz.parts, sz.taps + 1, sz.dk), F32),
        ),
        [anywhere()] * len(arguments),
        (vmem(),) * 5,
        [pltpu.VMEM(x.shape, x.dtype) for x in arguments]
        + [
            pltpu.VMEM((sz.heads, sz.info_rows, sz.dk), F32),
            pltpu.VMEM((3, sz.heads, sz.info_rows, sz.dk), F32),
            pltpu.VMEM((sz.heads, sz.dk), F32),
            pltpu.SemaphoreType.DMA((len(arguments) - 1 + sz.rows * sz.heads,)),
        ],
        "pack",
    )(*[in_hbm(x) for x in arguments])
    came = exchange(sz, pieces)
    gain = norm_gain.reshape(1, sz.dk)
    stepped, factor = call(
        functools.partial(step_kernel, sz),
        (
            shape((n, sz.state_rows + sz.back_rows, sz.dk), BF16),
            shape((sz.read_rows, channels), F32),
        ),
        [vmem()] * 4 + [anywhere()] * 4,
        (vmem(), vmem()),
        [
            pltpu.SMEM((8, sz.slots), jnp.int32),
            pltpu.VMEM(lives.shape, lives.dtype),
            pltpu.VMEM(gain.shape, F32),
            pltpu.VMEM(out_gate.shape, BF16),
            pltpu.VMEM((n * sz.info_rows, sz.dk), F32),
            pltpu.VMEM((8 if sz.whole_tiles else n * sz.state_rows, sz.dk), F32),
            pltpu.VMEM((n * sz.back_rows, sz.dk), F32),
            pltpu.SemaphoreType.DMA((4,)),
        ],
        "steps",
    )(taps, pick, place, came, final, in_hbm(lives), in_hbm(gain), in_hbm(out_gate))
    back = exchange(sz, stepped)
    width = out_weight.shape[1]
    columns = width // head_total
    blocks = head_total if columns % LANES == 0 else 1
    *partials, gated = call(
        functools.partial(project_kernel, sz, blocks),
        tuple(shape((sz.steps, sz.rows, columns), BF16) for _ in range(1, blocks))
        + (shape((sz.read_rows, channels), BF16),),
        [vmem()] * 3,
        tuple([vmem()] * blocks),
        [],
        "project",
    )(factor, out_weight, back)
    states_out, own, conv_out = call(
        functools.partial(restore_kernel, sz, blocks),
        (
            shape(states.shape, F32),
            shape((sz.steps, sz.rows, width // blocks), F32),
            shape((sz.taps, sz.parts, sz.rows, channels), BF16),
        ),
        [vmem()] * 3,
        (vmem(),) * 3,
        [],
        "restore",
    )(gated, out_weight, back)
    partials = [own, *partials]
    if blocks != head_total:
        mine = lax.axis_index("head")
        partials = [
            lax.dynamic_slice_in_dim(
                partials[0], lax.rem(mine + shift, head_total) * columns, columns, 2
            )
            for shift in range(head_total)
        ]
    total = partials[0]
    for shift in range(1, head_total):
        pairs = [(i, (i + shift) % head_total) for i in range(head_total)]
        passed = lax.ppermute(partials[shift].astype(BF16), "head", pairs)
        total = total + passed.astype(F32)
    return (total.astype(BF16), states_out, conv_out.transpose(2, 0, 1, 3))


def solution(mesh):
    placed = (
        P("rep", "head", None, None),
        P("rep", None, None, "head"),
        P(None, "rep", None, "head"),
        P(None, None, "head"),
        P(None, "rep", "head"),
        P("head"),
        P(None, "rep", "head"),
        P(None, "rep", "head"),
        P(),
        P("head", None),
        P(),
        P(None, "rep"),
    )
    return jax.shard_map(
        functools.partial(local, mesh.shape["rep"], mesh.shape["head"]),
        mesh=mesh,
        in_specs=placed,
        out_specs=(
            P(None, "rep", "head"),
            P("rep", "head", None, None),
            P("rep", None, None, "head"),
        ),
        check_vma=False,
    )
```

```python
import functools

import jax
import jax.numpy as jnp
from jax import lax
from jax.experimental import pallas as pl
from jax.experimental.pallas import tpu as pltpu
from jax.sharding import PartitionSpec as P

EPSILON = 1e-06
LANES = 128
VMEM_LIMIT = 32 * 1024 * 1024
F32 = jnp.float32
BF16 = jnp.bfloat16


def round_up(value, multiple):
    return -(-value // multiple) * multiple


def power_of_two(value):
    return value & (value - 1) == 0


class Sizes:
    def __init__(self, group_total, states, conv_states, projected):
        self.groups = n = group_total
        self.rows, self.heads, self.dk, _ = states.shape
        self.taps, self.parts = conv_states.shape[1:3]
        self.steps = projected.shape[0]
        self.slots = n * self.rows
        self.cuts = n // self.heads
        far = range(self.heads)
        if power_of_two(self.heads):
            far = [h ^ (h >> 1) for h in far]
        self.order = [h * self.cuts + cut for cut in range(self.cuts) for h in far]
        self.place_of = [self.order.index(p) for p in range(n)]
        self.cols = self.dk // self.cuts
        self.state_rows = self.rows * self.cols
        self.quarter = self.dk // 4
        self.decay_at = self.steps * 2
        self.hist_at = self.decay_at + self.steps
        self.value_at = self.hist_at + self.taps * 2
        self.value_depth = -(-(self.steps + self.taps) // 4)
        self.flag_at = self.value_at + self.value_depth
        self.info_sets = self.padded(self.flag_at + 1)
        self.info_rows = self.rows * self.info_sets
        self.back_sets = self.steps + self.taps * self.parts
        self.back_depth = self.padded(-(-self.back_sets // 4))
        self.back_rows = self.rows * self.back_depth
        self.read_rows = round_up(-(-self.steps // self.back_depth) * self.back_rows, 16)
        self.whole_tiles = self.cols % 16 == 0
        self.width = max(LANES, 8 * self.cols)
        self.tile = self.width // self.cols

    def padded(self, sets):
        while sets * self.rows % 8:
            sets += 1
        return sets

    def read_at(self, t, r):
        return t // self.back_depth * self.back_rows + r * self.back_depth + t % self.back_depth


def mod(value, size):
    return value & (size - 1) if size & (size - 1) == 0 else lax.rem(value, size)


def quotient(value, size):
    if size & (size - 1) == 0:
        return lax.shift_right_logical(value, jnp.int32(size.bit_length() - 1))
    return lax.div(value, jnp.int32(size))


def in_block(sz, shape, cut, shift):
    start = cut * sz.cols + shift * sz.quarter
    return mod(iota(shape, len(shape) - 1) + (2 * sz.dk - start), sz.dk) < sz.cols


def iota(shape, dim):
    return lax.broadcasted_iota(jnp.int32, shape, dim)


def one_hot(condition):
    return jnp.where(condition, 1.0, 0.0).astype(BF16)


def dot(lhs, rhs, lhs_dim=1, rhs_dim=0):
    return lax.dot_general(
        lhs, rhs, (((lhs_dim,), (rhs_dim,)), ((), ())), preferred_element_type=F32
    )


def pack_kernel(sz, *refs):
    count = 8
    sources, states_hbm = refs[:count], refs[count]
    pieces, pick, place, final, taps = refs[count + 1 : count + 6]
    scratch = refs[count + 6 :]
    targets, live, rate, beta, proj, hist, decay, filters, states = scratch[: count + 1]
    info, tails, strengths, in_sems = scratch[count + 1 :]
    copies = []

    def start(source, target):
        copies.append(pltpu.make_async_copy(source, target, in_sems.at[len(copies)]))
        copies[-1].start()

    for source, target in zip(sources, scratch):
        start(source, target)
    start(states_hbm, states)
    for copy in copies[:count]:
        copy.wait()
    route(sz, targets, pick, place, final)
    own_head = lax.axis_index("rep") // sz.cuts
    head_lanes = pl.ds(pl.multiple_of(own_head * sz.dk, sz.dk), sz.dk)
    for part in range(sz.parts):
        taps[part] = filters[part, :, head_lanes]
    channels, dk = sz.heads * sz.dk, sz.dk
    lane_head = quotient(iota((1, channels), 1), dk)
    rates = jnp.zeros((1, channels), F32)
    for h in range(sz.heads):
        rates = jnp.where(lane_head == h, rate[:, h : h + 1], rates)
    row_ids = iota((sz.rows, channels), 0)

    def keep(target, index, value):
        for h in range(sz.heads):
            rows = pl.ds(index, sz.rows, stride=sz.info_sets)
            target[h, rows, :] = value[:, h * dk : (h + 1) * dk]

    def keep_value(index, value):
        shift = index // sz.value_depth
        at = sz.value_at + index % sz.value_depth
        if shift:
            heads = [value[:, h * dk : (h + 1) * dk] for h in range(sz.heads)]
            heads = [pltpu.roll(head, shift * sz.quarter, 1) for head in heads]
            keep(tails.at[shift - 1], at, jnp.concatenate(heads, axis=1))
        else:
            keep(info, at, value)

    for t in range(sz.steps):
        for part in range(2):
            keep(info, t * 2 + part, proj[t, part].astype(F32))
        keep_value(t, proj[t, 2].astype(F32))
        x = decay[t]
        softplus = jnp.maximum(x, 0.0) + jnp.log1p(jnp.exp(-jnp.abs(x)))
        keep(
            info,
            sz.decay_at + t,
            jnp.where(row_ids < live[:, t : t + 1], rates * softplus, 0.0),
        )
    for tap in range(sz.taps):
        for part in range(2):
            keep(info, sz.hist_at + tap * 2 + part, hist[tap, part].astype(F32))
        keep_value(sz.steps + tap, hist[tap, 2].astype(F32))
    lane = iota((sz.heads, dk), 1)
    strengths[...] = jnp.zeros(strengths.shape, F32)
    for r in range(sz.rows):
        strengths[:, : sz.steps] = beta[r]
        lives = jnp.zeros((sz.heads, dk), F32)
        for t in range(sz.steps):
            lives = jnp.where((lane == t) & (r < live[:, t : t + 1]), 1.0, lives)
        strength = lives / (1.0 + jnp.exp(-strengths[...]))
        high = strength.astype(BF16).astype(F32)
        flags = high + pltpu.roll(lives, 16, 1) + pltpu.roll(strength - high, 32, 1)
        for h in range(sz.heads):
            at = r * sz.info_sets + sz.flag_at
            info[h, at : at + 1, :] = flags[h : h + 1]
    wide = [
        r * sz.info_sets + sz.value_at + i for r in range(sz.rows) for i in range(sz.value_depth)
    ]
    masks = {}
    for tile in sorted({at // 8 for at in wide}):
        row = iota((8, dk), 0) + tile * 8
        narrow = functools.reduce(jnp.logical_or, [row == at for at in wide if at // 8 == tile])
        masks[tile] = [
            [narrow & in_block(sz, (8, dk), cut, shift) for shift in range(1, 4)]
            for cut in range(sz.cuts)
        ]
    shared = [
        at for at in range(0, sz.info_rows, 16) if at // 8 not in masks and at // 8 + 1 not in masks
    ]
    held = [[info[h, at : at + 16, :].astype(BF16) for at in shared] for h in range(sz.heads)]
    for copy in copies[count:]:
        copy.wait()
    for h in range(sz.heads):
        across = [states[r, h].T for r in range(sz.rows)]
        for cut in range(sz.cuts):
            p, at = sz.place_of[h * sz.cuts + cut], cut * sz.cols
            own = [a[at : at + sz.cols] for a in across]
            pieces[p, : sz.state_rows, :] = jnp.concatenate(own, axis=0).astype(BF16)
            for at, value in zip(shared, held[h]):
                to = sz.state_rows + at
                pieces[p, to : to + value.shape[0], :] = value
            for at in range(0, sz.info_rows, 16):
                if at in shared:
                    continue
                rest = []
                for tile in range(at // 8, min(at + 16, sz.info_rows) // 8):
                    rows = slice(tile * 8, tile * 8 + 8)
                    value = info[h, rows, :]
                    for shift in range(3 if tile in masks else 0):
                        value = jnp.where(masks[tile][cut][shift], tails[shift, h, rows, :], value)
                    rest.append(value)
                rest = jnp.concatenate(rest, axis=0)
                to = sz.state_rows + at
                pieces[p, to : to + rest.shape[0], :] = rest.astype(BF16)


def route(sz, targets, pick, place, final):
    n, T = sz.slots, sz.steps
    steps = [one_hot(iota((n, n), 0) == targets[t : t + 1, :]) for t in range(T)]
    chain = [steps[0]]
    for t in range(1, T):
        if t % 2:
            pair = dot(steps[t], steps[t - 1]).astype(BF16)
            chain.append(dot(pair, chain[t - 2]).astype(BF16) if t > 1 else pair)
        else:
            chain.append(dot(steps[t], chain[t - 1]).astype(BF16))
    for t in range(T):
        place[t] = chain[t]
        pick[t] = chain[t].astype(F32).T.astype(BF16)
    slot = iota((8, n), 1)
    row, group = mod(slot, sz.rows), quotient(slot, sz.rows)
    head, cut = quotient(group, sz.cuts), mod(group, sz.cuts)
    far = head
    step = 1
    while power_of_two(sz.heads) and step < sz.heads:
        far = far ^ lax.shift_right_logical(far, jnp.int32(step))
        step *= 2
    weights = (cut * sz.heads + far) * sz.rows + row
    places = dot(weights.astype(F32).astype(BF16), chain[T - 1])
    final[...] = (places + 0.5).astype(jnp.int32)


def over_blocks(sz, value):
    step = sz.cols
    while step < sz.dk:
        value = value + pltpu.roll(value, step, 1)
        step *= 2
    return value


def gate_factor(sz, live, gain, gate, factor):
    factor[...] = jnp.zeros(factor.shape, F32)
    row = iota((sz.read_rows, sz.dk), 0)
    alive = row < 0
    for t in range(sz.steps):
        for r in range(sz.rows):
            at = sz.read_at(t, r)
            factor[at : at + 1, :] = gate[t, r : r + 1].astype(F32)
            alive = alive | ((row == at) & (r < live[:, t : t + 1]))
    for h in range(sz.heads):
        lanes = slice(h * sz.dk, (h + 1) * sz.dk)
        gates = gain[...] / (1.0 + jnp.exp(-factor[:, lanes]))
        factor[:, lanes] = jnp.where(alive, gates, 0.0)


def step_kernel(sz, filters, pick, place, came, *refs):
    count = sz.groups
    sources, sent, factor, scratch = refs[:4], refs[4], refs[5], refs[6:]
    scalars, live, gain, gate, info, later, back, sems = scratch
    copies = []
    for i, (source, target) in enumerate(zip(sources, scratch)):
        copies.append(pltpu.make_async_copy(source, target, sems.at[i]))
        copies[-1].start()
    n, dk, T = sz.slots, sz.dk, sz.steps
    mine = lax.axis_index("rep")
    cut = lax.rem(mine, sz.cuts)
    stride = sz.info_rows
    for g in range(count):
        info[g * stride : (g + 1) * stride, :] = came[sz.place_of[g], sz.state_rows :, :].astype(F32)

    def gather(index):
        return info[pl.ds(index, n, stride=sz.info_sets), :]

    def gather_value(index):
        value = gather(sz.value_at + index % sz.value_depth)
        shift = index // sz.value_depth
        return pltpu.roll(value, dk - shift * sz.quarter, 1) if shift else value

    weights = [filters[part] for part in range(sz.parts)]
    flags = gather(sz.flag_at)
    window = [
        [gather(sz.hist_at + tap * 2 + part) for part in range(2)]
        + [gather_value(T + tap)]
        for tap in range(sz.taps)
    ]
    active, retains, strengths = [], [], []
    for t in range(T):
        slots = [gather(t * 2 + part) for part in range(2)]
        slots += [gather_value(t), gather(sz.decay_at + t), flags]
        moved = dot(pick[t], jnp.concatenate(slots, axis=1).astype(BF16))
        inputs = [moved[:, i * dk : (i + 1) * dk] for i in range(sz.parts + 2)]
        moved_flags = inputs[sz.parts + 1]
        strength = moved_flags[:, t : t + 1] + moved_flags[:, 32 + t : 33 + t]
        alive = moved_flags[:, 16 + t : 17 + t] > 0.5
        for part in range(sz.parts):
            frames = [window[tap][part] for tap in range(sz.taps)] + [inputs[part]]
            total = frames[0] * weights[part][:1]
            for j in range(1, sz.taps + 1):
                total = total + frames[j] * weights[part][j : j + 1]
            below = 1.0 + jnp.exp(-total)
            inverse = pltpu.reciprocal(below, approx=True)
            inverse = inverse * (2.0 - below * inverse)
            active.append(total * inverse)
            for tap in range(sz.taps):
                window[tap][part] = jnp.where(alive, frames[tap + 1], frames[tap])
        retains.append(jnp.exp(-inputs[sz.parts]))
        strengths.append(strength)

    ones = jnp.ones((dk, dk), BF16)

    def summed(products):
        sums = dot(jnp.concatenate([x.astype(BF16) for x in products], axis=0), ones)
        return [sums[i * n : (i + 1) * n] for i in range(len(products))]

    values = active[2 :: sz.parts]
    units = [x for i, x in enumerate(active) if i % sz.parts < 2]
    norms = summed([x * x for x in units])
    units = [x * lax.rsqrt(norm + EPSILON) for x, norm in zip(units, norms)]
    reach = jnp.ones((n, dk), F32)
    keys = []
    from_state, pairs = [], []
    for t in range(T):
        query, key = units[2 * t], units[2 * t + 1]
        reach = reach * retains[t]
        keys = [k * retains[t] for k in keys]
        pairs += [key * k for k in keys]
        keys.append(key)
        pairs += [query * k for k in keys]
        from_state += [reach * key, reach * query]
    mixes = summed(pairs)
    key_mix, read_mix = [], []
    for t in range(T):
        key_mix.append(mixes[:t])
        read_mix.append(mixes[t : 2 * t + 1])
        mixes = mixes[2 * t + 1 :]

    own_lanes = in_block(sz, (n, dk), cut, 0)
    wide = sz.width // dk
    value_cols = []
    for value in values:
        value = over_blocks(sz, jnp.where(own_lanes, value, 0.0))
        value_cols.append(jnp.concatenate([value] * wide, axis=1))
    for copy in copies:
        copy.wait()
    gate_factor(sz, live, gain, gate, factor)
    lane_row = quotient(iota((sz.tile, sz.width), 1), sz.cols)
    own = iota((sz.tile, sz.width), 0) == lane_row
    readouts = [[] for _ in range(T)]

    def widen(value):
        return jnp.concatenate([value] * wide, axis=1)

    for at in range(0, n, sz.tile):
        rows = slice(at, at + sz.tile)
        block = []
        for g in range(at // sz.rows, (at + sz.tile) // sz.rows):
            for r in range(sz.rows):
                if sz.whole_tiles:
                    block.append(came[sz.place_of[g], r * sz.cols : (r + 1) * sz.cols, :])
                else:
                    piece = came[sz.place_of[g], : sz.state_rows, :].astype(F32)
                    block.append(piece[r * sz.cols : (r + 1) * sz.cols])
        seen = dot(
            jnp.concatenate([x[rows] for x in from_state], axis=0).astype(BF16),
            jnp.concatenate(block, axis=0).astype(BF16),
            1,
            1,
        )
        seen = [seen[i * sz.tile : (i + 1) * sz.tile] for i in range(2 * T)]
        writes = []
        for t in range(T):
            target = value_cols[t][rows] - seen[2 * t]
            target = jnp.where(own, target, 0.0)
            for s in range(t):
                target = target - widen(key_mix[t][s][rows]) * writes[s]
            writes.append(strengths[t][rows] * target)
            read = jnp.where(own, seen[2 * t + 1], 0.0)
            for s in range(t + 1):
                read = read + widen(read_mix[t][s][rows]) * writes[s]
            readouts[t].append(read * dk ** (-0.5))
        added = dot(
            jnp.concatenate(writes, axis=0).astype(BF16),
            jnp.concatenate([k[rows] for k in keys], axis=0).astype(BF16),
            0,
            0,
        )
        for i in range(sz.tile):
            part = block[i].astype(F32) * reach[at + i : at + i + 1]
            part = part + added[i * sz.cols : (i + 1) * sz.cols]
            to = scalars[0, at + i]
            if sz.whole_tiles:
                start = pl.multiple_of(mod(to, sz.rows) * sz.cols, sz.cols)
                sent[quotient(to, sz.rows), pl.ds(start, sz.cols), :] = part.astype(BF16)
            else:
                later[pl.ds(pl.multiple_of(to * sz.cols, sz.cols), sz.cols), :] = part
    blocks = [in_block(sz, (n, dk), cut, shift) for shift in range(4)]
    placed = [None] * sz.back_depth
    kept = [None] * sz.back_depth
    for index in range(sz.back_sets):
        shift, slot = index // sz.back_depth, index % sz.back_depth
        if index < T:
            folded = jnp.concatenate(readouts[index], axis=0)
            folded = functools.reduce(
                jnp.add, [folded[:, i * dk : (i + 1) * dk] for i in range(wide)]
            )
            folded = jnp.where(blocks[shift], over_blocks(sz, folded), 0.0)
            value = dot(place[index], folded.astype(BF16))
            placed[slot] = value if placed[slot] is None else placed[slot] + value
        else:
            value = window[(index - T) // sz.parts][(index - T) % sz.parts]
            if shift:
                value = pltpu.roll(value, shift * sz.quarter, 1)
            rest = jnp.zeros((n, dk), F32) if kept[slot] is None else kept[slot]
            kept[slot] = jnp.where(blocks[shift], value, rest)
    kept = [jnp.zeros((n, dk), F32) if value is None else value for value in kept]
    held = dot(place[T - 1], jnp.concatenate(kept, axis=1).astype(BF16))
    for slot in range(sz.back_depth):
        value = held[:, slot * dk : (slot + 1) * dk]
        if placed[slot] is not None:
            value = value + placed[slot]
        back[pl.ds(slot, n, stride=sz.back_depth), :] = value
    for g in range(count):
        p = sz.place_of[g]
        if not sz.whole_tiles:
            sent[p, : sz.state_rows, :] = later[
                p * sz.state_rows : (p + 1) * sz.state_rows, :
            ].astype(BF16)
        sent[p, sz.state_rows :, :] = back[
            g * sz.back_rows : (g + 1) * sz.back_rows, :
        ].astype(BF16)


def unpack(sz, came, h, wanted):
    shape = (sz.back_rows, sz.dk)
    pieces = [
        came[sz.place_of[h * sz.cuts + cut], sz.state_rows :, :].astype(F32)
        for cut in range(sz.cuts)
    ]
    narrow = {}
    for shift in sorted({index // sz.back_depth for index in wanted}):
        value = pieces[0]
        for cut in range(1, sz.cuts):
            value = jnp.where(in_block(sz, shape, cut, shift), pieces[cut], value)
        if shift:
            value = pltpu.roll(value, sz.dk - shift * sz.quarter, 1)
        narrow[shift] = value

    return narrow


def project_kernel(sz, blocks, factor, weight, came, *refs):
    dk = sz.dk
    partials, kept = refs[: blocks - 1], refs[blocks - 1]
    gated = []
    for h in range(sz.heads):
        lanes = slice(h * dk, (h + 1) * dk)
        narrow = unpack(sz, came, h, range(sz.steps))
        total = [narrow[quarter] for quarter in sorted(narrow)]
        spare = sz.read_rows - len(total) * sz.back_rows
        if spare:
            total.append(jnp.zeros((spare, dk), F32))
        total = jnp.concatenate(total, axis=0)
        scaling = lax.rsqrt(jnp.mean(total * total, axis=1, keepdims=True) + EPSILON)
        gated.append(total * scaling * factor[:, lanes])
    gated = jnp.concatenate(gated, axis=1).astype(BF16)
    kept[...] = gated
    for shift in range(1, blocks):
        project(sz, blocks, shift, gated, weight, partials[shift - 1])


def project(sz, blocks, shift, gated, weight, partial):
    columns = weight.shape[1] // blocks
    lanes = slice(None)
    if blocks > 1:
        at = lax.rem(lax.axis_index("head") + shift, blocks) * columns
        lanes = pl.ds(pl.multiple_of(at, LANES), columns)
    result = dot(gated, weight[:, lanes])
    for t in range(sz.steps):
        rows = [result[at : at + 1] for at in (sz.read_at(t, r) for r in range(sz.rows))]
        partial[t] = jnp.concatenate(rows, axis=0).astype(partial.dtype)


def restore_kernel(sz, blocks, gated, weight, came, states, partial, hist):
    project(sz, blocks, 0, gated[...], weight, partial)
    for h in range(sz.heads):
        narrow = unpack(sz, came, h, range(sz.steps, sz.back_sets))
        for tap in range(sz.taps):
            for part in range(sz.parts):
                index = sz.steps + tap * sz.parts + part
                held = narrow[index // sz.back_depth]
                at = index % sz.back_depth
                rows = [held[at + r * sz.back_depth :][:1] for r in range(sz.rows)]
                value = jnp.concatenate(rows, axis=0)
                hist[tap, part, :, h * sz.dk : (h + 1) * sz.dk] = value.astype(BF16)
    kind = BF16 if sz.whole_tiles else F32
    for r in range(sz.rows):
        for h in range(sz.heads):
            cuts = [
                came[sz.place_of[h * sz.cuts + cut], : sz.state_rows, :].astype(kind)[
                    r * sz.cols : (r + 1) * sz.cols
                ]
                for cut in range(sz.cuts)
            ]
            states[r, h] = jnp.concatenate(cuts, axis=0).T.astype(F32)


def vmem():
    return pl.BlockSpec(memory_space=pltpu.VMEM)


def smem():
    return pl.BlockSpec(memory_space=pltpu.SMEM)


def anywhere():
    return pl.BlockSpec(memory_space=pl.ANY)


def in_hbm(value):
    return pltpu.with_memory_space_constraint(value, pltpu.HBM)


def call(body, outs, ins, out_specs, scratch, name):
    return pl.pallas_call(
        body,
        out_shape=outs,
        in_specs=ins,
        out_specs=out_specs,
        scratch_shapes=scratch,
        compiler_params=pltpu.CompilerParams(vmem_limit_bytes=VMEM_LIMIT),
        name=name,
    )


def exchange(sz, pieces):
    return lax.all_to_all(
        pieces, "rep", split_axis=0, concat_axis=0, axis_index_groups=[sz.order], tiled=True
    )


def local(
    group_total,
    head_total,
    states,
    conv_states,
    projected,
    conv_weight,
    decay_input,
    decay_rate,
    beta_logit,
    out_gate,
    norm_gain,
    out_weight,
    destinations,
    live_counts,
):
    sz = Sizes(group_total, states, conv_states, projected)
    n, channels = sz.groups, sz.heads * sz.dk
    shape = jax.ShapeDtypeStruct
    lives = live_counts.T
    arguments = (
        destinations,
        lives,
        decay_rate.reshape(1, sz.heads),
        beta_logit.transpose(1, 2, 0),
        projected.transpose(0, 2, 1, 3),
        conv_states.transpose(1, 2, 0, 3),
        decay_input,
        conv_weight.transpose(1, 0, 2),
        states,
    )
    routes = shape((sz.steps, sz.slots, sz.slots), BF16)
    pieces, pick, place, final, taps = call(
        functools.partial(pack_kernel, sz),
        (
            shape((n, sz.state_rows + sz.info_rows, sz.dk), BF16),
            routes,
            routes,
            shape((8, sz.slots), jnp.int32),
            shape((sz.parts, sz.taps + 1, sz.dk), F32),
        ),
        [anywhere()] * len(arguments),
        (vmem(),) * 5,
        [pltpu.VMEM(x.shape, x.dtype) for x in arguments]
        + [
            pltpu.VMEM((sz.heads, sz.info_rows, sz.dk), F32),
            pltpu.VMEM((3, sz.heads, sz.info_rows, sz.dk), F32),
            pltpu.VMEM((sz.heads, sz.dk), F32),
            pltpu.SemaphoreType.DMA((len(arguments),)),
        ],
        "pack",
    )(*[in_hbm(x) for x in arguments])
    came = exchange(sz, pieces)
    gain = norm_gain.reshape(1, sz.dk)
    stepped, factor = call(
        functools.partial(step_kernel, sz),
        (
            shape((n, sz.state_rows + sz.back_rows, sz.dk), BF16),
            shape((sz.read_rows, channels), F32),
        ),
        [vmem()] * 4 + [anywhere()] * 4,
        (vmem(), vmem()),
        [
            pltpu.SMEM((8, sz.slots), jnp.int32),
            pltpu.VMEM(lives.shape, lives.dtype),
            pltpu.VMEM(gain.shape, F32),
            pltpu.VMEM(out_gate.shape, BF16),
            pltpu.VMEM((n * sz.info_rows, sz.dk), F32),
            pltpu.VMEM((8 if sz.whole_tiles else n * sz.state_rows, sz.dk), F32),
            pltpu.VMEM((n * sz.back_rows, sz.dk), F32),
            pltpu.SemaphoreType.DMA((4,)),
        ],
        "steps",
    )(taps, pick, place, came, final, in_hbm(lives), in_hbm(gain), in_hbm(out_gate))
    back = exchange(sz, stepped)
    width = out_weight.shape[1]
    columns = width // head_total
    blocks = head_total if columns % LANES == 0 else 1
    *partials, gated = call(
        functools.partial(project_kernel, sz, blocks),
        tuple(shape((sz.steps, sz.rows, columns), BF16) for _ in range(1, blocks))
        + (shape((sz.read_rows, channels), BF16),),
        [vmem()] * 3,
        tuple([vmem()] * blocks),
        [],
        "project",
    )(factor, out_weight, back)
    states_out, own, conv_out = call(
        functools.partial(restore_kernel, sz, blocks),
        (
            shape(states.shape, F32),
            shape((sz.steps, sz.rows, width // blocks), F32),
            shape((sz.taps, sz.parts, sz.rows, channels), BF16),
        ),
        [vmem()] * 3,
        (vmem(),) * 3,
        [],
        "restore",
    )(gated, out_weight, back)
    partials = [own, *partials]
    if blocks != head_total:
        mine = lax.axis_index("head")
        partials = [
            lax.dynamic_slice_in_dim(
                partials[0], lax.rem(mine + shift, head_total) * columns, columns, 2
            )
            for shift in range(head_total)
        ]
    total = partials[0]
    for shift in range(1, head_total):
        pairs = [(i, (i + shift) % head_total) for i in range(head_total)]
        passed = lax.ppermute(partials[shift].astype(BF16), "head", pairs)
        total = total + passed.astype(F32)
    return (total.astype(BF16), states_out, conv_out.transpose(2, 0, 1, 3))


def solution(mesh):
    placed = (
        P("rep", "head", None, None),
        P("rep", None, None, "head"),
        P(None, "rep", None, "head"),
        P(None, None, "head"),
        P(None, "rep", "head"),
        P("head"),
        P(None, "rep", "head"),
        P(None, "rep", "head"),
        P(),
        P("head", None),
        P(),
        P(None, "rep"),
    )
    return jax.shard_map(
        functools.partial(local, mesh.shape["rep"], mesh.shape["head"]),
        mesh=mesh,
        in_specs=placed,
        out_specs=(
            P(None, "rep", "head"),
            P("rep", "head", None, None),
            P("rep", None, None, "head"),
        ),
        check_vma=False,
    )
```

```python
import functools

import jax
import jax.numpy as jnp
from jax import lax
from jax.experimental import pallas as pl
from jax.experimental.pallas import tpu as pltpu
from jax.sharding import PartitionSpec as P

EPSILON = 1e-06
LANES = 128
VMEM_LIMIT = 32 * 1024 * 1024
F32 = jnp.float32
BF16 = jnp.bfloat16


def round_up(value, multiple):
    return -(-value // multiple) * multiple


def power_of_two(value):
    return value & (value - 1) == 0


class Sizes:
    def __init__(self, group_total, states, conv_states, projected):
        self.groups = n = group_total
        self.rows, self.heads, self.dk, _ = states.shape
        self.taps, self.parts = conv_states.shape[1:3]
        self.steps = projected.shape[0]
        self.slots = n * self.rows
        self.cuts = n // self.heads
        far = range(self.heads)
        if power_of_two(self.heads):
            far = [h ^ (h >> 1) for h in far]
        self.order = [h * self.cuts + cut for cut in range(self.cuts) for h in far]
        self.place_of = [self.order.index(p) for p in range(n)]
        self.cols = self.dk // self.cuts
        self.state_rows = self.rows * self.cols
        self.quarter = self.dk // 4
        self.decay_at = self.steps * 2
        self.hist_at = self.decay_at + self.steps
        self.value_at = self.hist_at + self.taps * 2
        self.value_depth = -(-(self.steps + self.taps) // 4)
        self.flag_at = self.value_at + self.value_depth
        self.info_sets = self.padded(self.flag_at + 1)
        self.info_rows = self.rows * self.info_sets
        self.back_sets = self.steps + self.taps * self.parts
        self.back_depth = self.padded(-(-self.back_sets // 4))
        self.back_rows = self.rows * self.back_depth
        self.read_rows = round_up(-(-self.steps // self.back_depth) * self.back_rows, 16)
        self.whole_tiles = self.cols % 16 == 0
        self.width = max(LANES, 8 * self.cols)
        self.tile = self.width // self.cols

    def padded(self, sets):
        while sets * self.rows % 8:
            sets += 1
        return sets

    def read_at(self, t, r):
        return t // self.back_depth * self.back_rows + r * self.back_depth + t % self.back_depth


def mod(value, size):
    return value & (size - 1) if size & (size - 1) == 0 else lax.rem(value, size)


def quotient(value, size):
    if size & (size - 1) == 0:
        return lax.shift_right_logical(value, jnp.int32(size.bit_length() - 1))
    return lax.div(value, jnp.int32(size))


def in_block(sz, shape, cut, shift):
    start = cut * sz.cols + shift * sz.quarter
    return mod(iota(shape, len(shape) - 1) + (2 * sz.dk - start), sz.dk) < sz.cols


def iota(shape, dim):
    return lax.broadcasted_iota(jnp.int32, shape, dim)


def one_hot(condition):
    return jnp.where(condition, 1.0, 0.0).astype(BF16)


def dot(lhs, rhs, lhs_dim=1, rhs_dim=0):
    return lax.dot_general(
        lhs, rhs, (((lhs_dim,), (rhs_dim,)), ((), ())), preferred_element_type=F32
    )


def pack_kernel(sz, *refs):
    count = 8
    sources, states_hbm = refs[:count], refs[count]
    pieces, pick, place, final, taps = refs[count + 1 : count + 6]
    scratch = refs[count + 6 :]
    targets, live, rate, beta, proj, hist, decay, filters, states = scratch[: count + 1]
    info, tails, strengths, in_sems = scratch[count + 1 :]
    copies = []

    def start(source, target):
        copies.append(pltpu.make_async_copy(source, target, in_sems.at[len(copies)]))
        copies[-1].start()

    for source, target in zip(sources, scratch):
        start(source, target)
    start(states_hbm, states)
    for copy in copies[:count]:
        copy.wait()
    route(sz, targets, pick, place, final)
    own_head = lax.axis_index("rep") // sz.cuts
    head_lanes = pl.ds(pl.multiple_of(own_head * sz.dk, sz.dk), sz.dk)
    for part in range(sz.parts):
        taps[part] = filters[part, :, head_lanes]
    channels, dk = sz.heads * sz.dk, sz.dk
    lane_head = quotient(iota((1, channels), 1), dk)
    rates = jnp.zeros((1, channels), F32)
    for h in range(sz.heads):
        rates = jnp.where(lane_head == h, rate[:, h : h + 1], rates)
    row_ids = iota((sz.rows, channels), 0)

    def keep(target, index, value):
        for h in range(sz.heads):
            rows = pl.ds(index, sz.rows, stride=sz.info_sets)
            target[h, rows, :] = value[:, h * dk : (h + 1) * dk]

    def keep_value(index, value):
        shift = index // sz.value_depth
        at = sz.value_at + index % sz.value_depth
        if shift:
            heads = [value[:, h * dk : (h + 1) * dk] for h in range(sz.heads)]
            heads = [pltpu.roll(head, shift * sz.quarter, 1) for head in heads]
            keep(tails.at[shift - 1], at, jnp.concatenate(heads, axis=1))
        else:
            keep(info, at, value)

    for t in range(sz.steps):
        for part in range(2):
            keep(info, t * 2 + part, proj[t, part].astype(F32))
        keep_value(t, proj[t, 2].astype(F32))
        x = decay[t]
        softplus = jnp.maximum(x, 0.0) + jnp.log1p(jnp.exp(-jnp.abs(x)))
        keep(
            info,
            sz.decay_at + t,
            jnp.where(row_ids < live[:, t : t + 1], rates * softplus, 0.0),
        )
    for tap in range(sz.taps):
        for part in range(2):
            keep(info, sz.hist_at + tap * 2 + part, hist[tap, part].astype(F32))
        keep_value(sz.steps + tap, hist[tap, 2].astype(F32))
    lane = iota((sz.heads, dk), 1)
    strengths[...] = jnp.zeros(strengths.shape, F32)
    for r in range(sz.rows):
        strengths[:, : sz.steps] = beta[r]
        lives = jnp.zeros((sz.heads, dk), F32)
        for t in range(sz.steps):
            lives = jnp.where((lane == t) & (r < live[:, t : t + 1]), 1.0, lives)
        strength = lives / (1.0 + jnp.exp(-strengths[...]))
        high = strength.astype(BF16).astype(F32)
        flags = high + pltpu.roll(lives, 16, 1) + pltpu.roll(strength - high, 32, 1)
        for h in range(sz.heads):
            at = r * sz.info_sets + sz.flag_at
            info[h, at : at + 1, :] = flags[h : h + 1]
    wide = [
        r * sz.info_sets + sz.value_at + i for r in range(sz.rows) for i in range(sz.value_depth)
    ]
    masks = {}
    for tile in sorted({at // 8 for at in wide}):
        row = iota((8, dk), 0) + tile * 8
        narrow = functools.reduce(jnp.logical_or, [row == at for at in wide if at // 8 == tile])
        masks[tile] = [
            [narrow & in_block(sz, (8, dk), cut, shift) for shift in range(1, 4)]
            for cut in range(sz.cuts)
        ]
    shared = [
        at for at in range(0, sz.info_rows, 16) if at // 8 not in masks and at // 8 + 1 not in masks
    ]
    held = [[info[h, at : at + 16, :].astype(BF16) for at in shared] for h in range(sz.heads)]
    for copy in copies[count:]:
        copy.wait()
    for h in range(sz.heads):
        across = [states[r, h].T for r in range(sz.rows)]
        for cut in range(sz.cuts):
            p, at = sz.place_of[h * sz.cuts + cut], cut * sz.cols
            own = [a[at : at + sz.cols] for a in across]
            pieces[p, : sz.state_rows, :] = jnp.concatenate(own, axis=0).astype(BF16)
            for at, value in zip(shared, held[h]):
                to = sz.state_rows + at
                pieces[p, to : to + value.shape[0], :] = value
            for at in range(0, sz.info_rows, 16):
                if at in shared:
                    continue
                rest = []
                for tile in range(at // 8, min(at + 16, sz.info_rows) // 8):
                    rows = slice(tile * 8, tile * 8 + 8)
                    value = info[h, rows, :]
                    for shift in range(3 if tile in masks else 0):
                        value = jnp.where(masks[tile][cut][shift], tails[shift, h, rows, :], value)
                    rest.append(value)
                rest = jnp.concatenate(rest, axis=0)
                to = sz.state_rows + at
                pieces[p, to : to + rest.shape[0], :] = rest.astype(BF16)


def route(sz, targets, pick, place, final):
    n, T = sz.slots, sz.steps
    steps = [one_hot(iota((n, n), 0) == targets[t : t + 1, :]) for t in range(T)]
    chain = [steps[0]]
    for t in range(1, T):
        if t % 2:
            pair = dot(steps[t], steps[t - 1]).astype(BF16)
            chain.append(dot(pair, chain[t - 2]).astype(BF16) if t > 1 else pair)
        else:
            chain.append(dot(steps[t], chain[t - 1]).astype(BF16))
    for t in range(T):
        place[t] = chain[t]
        pick[t] = chain[t].astype(F32).T.astype(BF16)
    slot = iota((8, n), 1)
    row, group = mod(slot, sz.rows), quotient(slot, sz.rows)
    head, cut = quotient(group, sz.cuts), mod(group, sz.cuts)
    far = head
    step = 1
    while power_of_two(sz.heads) and step < sz.heads:
        far = far ^ lax.shift_right_logical(far, jnp.int32(step))
        step *= 2
    weights = (cut * sz.heads + far) * sz.rows + row
    places = dot(weights.astype(F32).astype(BF16), chain[T - 1])
    final[...] = (places + 0.5).astype(jnp.int32)


def over_blocks(sz, value):
    step = sz.cols
    while step < sz.dk:
        value = value + pltpu.roll(value, step, 1)
        step *= 2
    return value


def gate_factor(sz, live, gain, gate, factor):
    factor[...] = jnp.zeros(factor.shape, F32)
    row = iota((sz.read_rows, sz.dk), 0)
    alive = row < 0
    for t in range(sz.steps):
        for r in range(sz.rows):
            at = sz.read_at(t, r)
            factor[at : at + 1, :] = gate[t, r : r + 1].astype(F32)
            alive = alive | ((row == at) & (r < live[:, t : t + 1]))
    for h in range(sz.heads):
        lanes = slice(h * sz.dk, (h + 1) * sz.dk)
        gates = gain[...] / (1.0 + jnp.exp(-factor[:, lanes]))
        factor[:, lanes] = jnp.where(alive, gates, 0.0)


def step_kernel(sz, filters, pick, place, came, *refs):
    count = sz.groups
    sources, sent, factor, scratch = refs[:4], refs[4], refs[5], refs[6:]
    scalars, live, gain, gate, info, later, back, sems = scratch
    copies = []
    for i, (source, target) in enumerate(zip(sources, scratch)):
        copies.append(pltpu.make_async_copy(source, target, sems.at[i]))
        copies[-1].start()
    n, dk, T = sz.slots, sz.dk, sz.steps
    mine = lax.axis_index("rep")
    cut = lax.rem(mine, sz.cuts)
    stride = sz.info_rows
    for g in range(count):
        info[g * stride : (g + 1) * stride, :] = came[sz.place_of[g], sz.state_rows :, :].astype(F32)

    def gather(index):
        return info[pl.ds(index, n, stride=sz.info_sets), :]

    def gather_value(index):
        value = gather(sz.value_at + index % sz.value_depth)
        shift = index // sz.value_depth
        return pltpu.roll(value, dk - shift * sz.quarter, 1) if shift else value

    weights = [filters[part] for part in range(sz.parts)]
    flags = gather(sz.flag_at)
    window = [
        [gather(sz.hist_at + tap * 2 + part) for part in range(2)]
        + [gather_value(T + tap)]
        for tap in range(sz.taps)
    ]
    active, retains, strengths = [], [], []
    for t in range(T):
        slots = [gather(t * 2 + part) for part in range(2)]
        slots += [gather_value(t), gather(sz.decay_at + t), flags]
        moved = dot(pick[t], jnp.concatenate(slots, axis=1).astype(BF16))
        inputs = [moved[:, i * dk : (i + 1) * dk] for i in range(sz.parts + 2)]
        moved_flags = inputs[sz.parts + 1]
        strength = moved_flags[:, t : t + 1] + moved_flags[:, 32 + t : 33 + t]
        alive = moved_flags[:, 16 + t : 17 + t] > 0.5
        for part in range(sz.parts):
            frames = [window[tap][part] for tap in range(sz.taps)] + [inputs[part]]
            total = frames[0] * weights[part][:1]
            for j in range(1, sz.taps + 1):
                total = total + frames[j] * weights[part][j : j + 1]
            active.append(total / (1.0 + jnp.exp(-total)))
            for tap in range(sz.taps):
                window[tap][part] = jnp.where(alive, frames[tap + 1], frames[tap])
        retains.append(jnp.exp(-inputs[sz.parts]))
        strengths.append(strength)

    ones = jnp.ones((dk, dk), BF16)

    def summed(products):
        sums = dot(jnp.concatenate([x.astype(BF16) for x in products], axis=0), ones)
        return [sums[i * n : (i + 1) * n] for i in range(len(products))]

    values = active[2 :: sz.parts]
    units = [x for i, x in enumerate(active) if i % sz.parts < 2]
    norms = summed([x * x for x in units])
    units = [x * lax.rsqrt(norm + EPSILON) for x, norm in zip(units, norms)]
    reach = jnp.ones((n, dk), F32)
    keys = []
    from_state, pairs = [], []
    for t in range(T):
        query, key = units[2 * t], units[2 * t + 1]
        reach = reach * retains[t]
        keys = [k * retains[t] for k in keys]
        pairs += [key * k for k in keys]
        keys.append(key)
        pairs += [query * k for k in keys]
        from_state += [reach * key, reach * query]
    mixes = summed(pairs)
    key_mix, read_mix = [], []
    for t in range(T):
        key_mix.append(mixes[:t])
        read_mix.append(mixes[t : 2 * t + 1])
        mixes = mixes[2 * t + 1 :]

    own_lanes = in_block(sz, (n, dk), cut, 0)
    wide = sz.width // dk
    value_cols = []
    for value in values:
        value = over_blocks(sz, jnp.where(own_lanes, value, 0.0))
        value_cols.append(jnp.concatenate([value] * wide, axis=1))
    for copy in copies:
        copy.wait()
    gate_factor(sz, live, gain, gate, factor)
    lane_row = quotient(iota((sz.tile, sz.width), 1), sz.cols)
    own = iota((sz.tile, sz.width), 0) == lane_row
    readouts = [[] for _ in range(T)]

    def widen(value):
        return jnp.concatenate([value] * wide, axis=1)

    for at in range(0, n, sz.tile):
        rows = slice(at, at + sz.tile)
        block = []
        for g in range(at // sz.rows, (at + sz.tile) // sz.rows):
            for r in range(sz.rows):
                if sz.whole_tiles:
                    block.append(came[sz.place_of[g], r * sz.cols : (r + 1) * sz.cols, :])
                else:
                    piece = came[sz.place_of[g], : sz.state_rows, :].astype(F32)
                    block.append(piece[r * sz.cols : (r + 1) * sz.cols])
        seen = dot(
            jnp.concatenate([x[rows] for x in from_state], axis=0).astype(BF16),
            jnp.concatenate(block, axis=0).astype(BF16),
            1,
            1,
        )
        seen = [seen[i * sz.tile : (i + 1) * sz.tile] for i in range(2 * T)]
        writes = []
        for t in range(T):
            target = value_cols[t][rows] - seen[2 * t]
            target = jnp.where(own, target, 0.0)
            for s in range(t):
                target = target - widen(key_mix[t][s][rows]) * writes[s]
            writes.append(strengths[t][rows] * target)
            read = jnp.where(own, seen[2 * t + 1], 0.0)
            for s in range(t + 1):
                read = read + widen(read_mix[t][s][rows]) * writes[s]
            readouts[t].append(read * dk ** (-0.5))
        added = dot(
            jnp.concatenate(writes, axis=0).astype(BF16),
            jnp.concatenate([k[rows] for k in keys], axis=0).astype(BF16),
            0,
            0,
        )
        for i in range(sz.tile):
            part = block[i].astype(F32) * reach[at + i : at + i + 1]
            part = part + added[i * sz.cols : (i + 1) * sz.cols]
            to = scalars[0, at + i]
            if sz.whole_tiles:
                start = pl.multiple_of(mod(to, sz.rows) * sz.cols, sz.cols)
                sent[quotient(to, sz.rows), pl.ds(start, sz.cols), :] = part.astype(BF16)
            else:
                later[pl.ds(pl.multiple_of(to * sz.cols, sz.cols), sz.cols), :] = part
    blocks = [in_block(sz, (n, dk), cut, shift) for shift in range(4)]
    placed = [None] * sz.back_depth
    kept = [None] * sz.back_depth
    for index in range(sz.back_sets):
        shift, slot = index // sz.back_depth, index % sz.back_depth
        if index < T:
            folded = jnp.concatenate(readouts[index], axis=0)
            folded = functools.reduce(
                jnp.add, [folded[:, i * dk : (i + 1) * dk] for i in range(wide)]
            )
            folded = jnp.where(blocks[shift], over_blocks(sz, folded), 0.0)
            value = dot(place[index], folded.astype(BF16))
            placed[slot] = value if placed[slot] is None else placed[slot] + value
        else:
            value = window[(index - T) // sz.parts][(index - T) % sz.parts]
            if shift:
                value = pltpu.roll(value, shift * sz.quarter, 1)
            rest = jnp.zeros((n, dk), F32) if kept[slot] is None else kept[slot]
            kept[slot] = jnp.where(blocks[shift], value, rest)
    kept = [jnp.zeros((n, dk), F32) if value is None else value for value in kept]
    held = dot(place[T - 1], jnp.concatenate(kept, axis=1).astype(BF16))
    for slot in range(sz.back_depth):
        value = held[:, slot * dk : (slot + 1) * dk]
        if placed[slot] is not None:
            value = value + placed[slot]
        back[pl.ds(slot, n, stride=sz.back_depth), :] = value
    for g in range(count):
        p = sz.place_of[g]
        if not sz.whole_tiles:
            sent[p, : sz.state_rows, :] = later[
                p * sz.state_rows : (p + 1) * sz.state_rows, :
            ].astype(BF16)
        sent[p, sz.state_rows :, :] = back[
            g * sz.back_rows : (g + 1) * sz.back_rows, :
        ].astype(BF16)


def unpack(sz, came, h, wanted):
    shape = (sz.back_rows, sz.dk)
    pieces = [
        came[sz.place_of[h * sz.cuts + cut], sz.state_rows :, :].astype(F32)
        for cut in range(sz.cuts)
    ]
    narrow = {}
    for shift in sorted({index // sz.back_depth for index in wanted}):
        value = pieces[0]
        for cut in range(1, sz.cuts):
            value = jnp.where(in_block(sz, shape, cut, shift), pieces[cut], value)
        if shift:
            value = pltpu.roll(value, sz.dk - shift * sz.quarter, 1)
        narrow[shift] = value

    return narrow


def project_kernel(sz, blocks, factor, weight, came, *refs):
    dk = sz.dk
    partials, kept = refs[: blocks - 1], refs[blocks - 1]
    gated = []
    for h in range(sz.heads):
        lanes = slice(h * dk, (h + 1) * dk)
        narrow = unpack(sz, came, h, range(sz.steps))
        total = [narrow[quarter] for quarter in sorted(narrow)]
        spare = sz.read_rows - len(total) * sz.back_rows
        if spare:
            total.append(jnp.zeros((spare, dk), F32))
        total = jnp.concatenate(total, axis=0)
        scaling = lax.rsqrt(jnp.mean(total * total, axis=1, keepdims=True) + EPSILON)
        gated.append(total * scaling * factor[:, lanes])
    gated = jnp.concatenate(gated, axis=1).astype(BF16)
    kept[...] = gated
    for shift in range(1, blocks):
        project(sz, blocks, shift, gated, weight, partials[shift - 1])


def project(sz, blocks, shift, gated, weight, partial):
    columns = weight.shape[1] // blocks
    lanes = slice(None)
    if blocks > 1:
        at = lax.rem(lax.axis_index("head") + shift, blocks) * columns
        lanes = pl.ds(pl.multiple_of(at, LANES), columns)
    result = dot(gated, weight[:, lanes])
    for t in range(sz.steps):
        rows = [result[at : at + 1] for at in (sz.read_at(t, r) for r in range(sz.rows))]
        partial[t] = jnp.concatenate(rows, axis=0).astype(partial.dtype)


def restore_kernel(sz, blocks, gated, weight, came, states, partial, hist):
    project(sz, blocks, 0, gated[...], weight, partial)
    for h in range(sz.heads):
        narrow = unpack(sz, came, h, range(sz.steps, sz.back_sets))
        for tap in range(sz.taps):
            for part in range(sz.parts):
                index = sz.steps + tap * sz.parts + part
                held = narrow[index // sz.back_depth]
                at = index % sz.back_depth
                rows = [held[at + r * sz.back_depth :][:1] for r in range(sz.rows)]
                value = jnp.concatenate(rows, axis=0)
                hist[tap, part, :, h * sz.dk : (h + 1) * sz.dk] = value.astype(BF16)
    kind = BF16 if sz.whole_tiles else F32
    for r in range(sz.rows):
        for h in range(sz.heads):
            cuts = [
                came[sz.place_of[h * sz.cuts + cut], : sz.state_rows, :].astype(kind)[
                    r * sz.cols : (r + 1) * sz.cols
                ]
                for cut in range(sz.cuts)
            ]
            states[r, h] = jnp.concatenate(cuts, axis=0).T.astype(F32)


def vmem():
    return pl.BlockSpec(memory_space=pltpu.VMEM)


def smem():
    return pl.BlockSpec(memory_space=pltpu.SMEM)


def anywhere():
    return pl.BlockSpec(memory_space=pl.ANY)


def in_hbm(value):
    return pltpu.with_memory_space_constraint(value, pltpu.HBM)


def call(body, outs, ins, out_specs, scratch, name):
    return pl.pallas_call(
        body,
        out_shape=outs,
        in_specs=ins,
        out_specs=out_specs,
        scratch_shapes=scratch,
        compiler_params=pltpu.CompilerParams(vmem_limit_bytes=VMEM_LIMIT),
        name=name,
    )


def exchange(sz, pieces):
    return lax.all_to_all(
        pieces, "rep", split_axis=0, concat_axis=0, axis_index_groups=[sz.order], tiled=True
    )


def local(
    group_total,
    head_total,
    states,
    conv_states,
    projected,
    conv_weight,
    decay_input,
    decay_rate,
    beta_logit,
    out_gate,
    norm_gain,
    out_weight,
    destinations,
    live_counts,
):
    sz = Sizes(group_total, states, conv_states, projected)
    n, channels = sz.groups, sz.heads * sz.dk
    shape = jax.ShapeDtypeStruct
    lives = live_counts.T
    arguments = (
        destinations,
        lives,
        decay_rate.reshape(1, sz.heads),
        beta_logit.transpose(1, 2, 0),
        projected.transpose(0, 2, 1, 3),
        conv_states.transpose(1, 2, 0, 3),
        decay_input,
        conv_weight.transpose(1, 0, 2),
        states,
    )
    routes = shape((sz.steps, sz.slots, sz.slots), BF16)
    pieces, pick, place, final, taps = call(
        functools.partial(pack_kernel, sz),
        (
            shape((n, sz.state_rows + sz.info_rows, sz.dk), BF16),
            routes,
            routes,
            shape((8, sz.slots), jnp.int32),
            shape((sz.parts, sz.taps + 1, sz.dk), F32),
        ),
        [anywhere()] * len(arguments),
        (vmem(),) * 5,
        [pltpu.VMEM(x.shape, x.dtype) for x in arguments]
        + [
            pltpu.VMEM((sz.heads, sz.info_rows, sz.dk), F32),
            pltpu.VMEM((3, sz.heads, sz.info_rows, sz.dk), F32),
            pltpu.VMEM((sz.heads, sz.dk), F32),
            pltpu.SemaphoreType.DMA((len(arguments),)),
        ],
        "pack",
    )(*[in_hbm(x) for x in arguments])
    came = exchange(sz, pieces)
    gain = norm_gain.reshape(1, sz.dk)
    stepped, factor = call(
        functools.partial(step_kernel, sz),
        (
            shape((n, sz.state_rows + sz.back_rows, sz.dk), BF16),
            shape((sz.read_rows, channels), F32),
        ),
        [vmem()] * 4 + [anywhere()] * 4,
        (vmem(), vmem()),
        [
            pltpu.SMEM((8, sz.slots), jnp.int32),
            pltpu.VMEM(lives.shape, lives.dtype),
            pltpu.VMEM(gain.shape, F32),
            pltpu.VMEM(out_gate.shape, BF16),
            pltpu.VMEM((n * sz.info_rows, sz.dk), F32),
            pltpu.VMEM((8 if sz.whole_tiles else n * sz.state_rows, sz.dk), F32),
            pltpu.VMEM((n * sz.back_rows, sz.dk), F32),
            pltpu.SemaphoreType.DMA((4,)),
        ],
        "steps",
    )(taps, pick, place, came, final, in_hbm(lives), in_hbm(gain), in_hbm(out_gate))
    back = exchange(sz, stepped)
    width = out_weight.shape[1]
    columns = width // head_total
    blocks = head_total if columns % LANES == 0 else 1
    *partials, gated = call(
        functools.partial(project_kernel, sz, blocks),
        tuple(shape((sz.steps, sz.rows, columns), BF16) for _ in range(1, blocks))
        + (shape((sz.read_rows, channels), BF16),),
        [vmem()] * 3,
        tuple([vmem()] * blocks),
        [],
        "project",
    )(factor, out_weight, back)
    states_out, own, conv_out = call(
        functools.partial(restore_kernel, sz, blocks),
        (
            shape(states.shape, F32),
            shape((sz.steps, sz.rows, width // blocks), F32),
            shape((sz.taps, sz.parts, sz.rows, channels), BF16),
        ),
        [vmem()] * 3,
        (vmem(),) * 3,
        [],
        "restore",
    )(gated, out_weight, back)
    partials = [own, *partials]
    if blocks != head_total:
        mine = lax.axis_index("head")
        partials = [
            lax.dynamic_slice_in_dim(
                partials[0], lax.rem(mine + shift, head_total) * columns, columns, 2
            )
            for shift in range(head_total)
        ]
    total = partials[0]
    for shift in range(1, head_total):
        pairs = [(i, (i + shift) % head_total) for i in range(head_total)]
        passed = lax.ppermute(partials[shift].astype(BF16), "head", pairs)
        total = total + passed.astype(F32)
    return (total.astype(BF16), states_out, conv_out.transpose(2, 0, 1, 3))


def solution(mesh):
    placed = (
        P("rep", "head", None, None),
        P("rep", None, None, "head"),
        P(None, "rep", None, "head"),
        P(None, None, "head"),
        P(None, "rep", "head"),
        P("head"),
        P(None, "rep", "head"),
        P(None, "rep", "head"),
        P(),
        P("head", None),
        P(),
        P(None, "rep"),
    )
    return jax.shard_map(
        functools.partial(local, mesh.shape["rep"], mesh.shape["head"]),
        mesh=mesh,
        in_specs=placed,
        out_specs=(
            P(None, "rep", "head"),
            P("rep", "head", None, None),
            P("rep", None, None, "head"),
        ),
        check_vma=False,
    )
```

```python
import functools

import jax
import jax.numpy as jnp
from jax import lax
from jax.experimental import pallas as pl
from jax.experimental.pallas import tpu as pltpu
from jax.sharding import PartitionSpec as P

EPSILON = 1e-06
LANES = 128
VMEM_LIMIT = 32 * 1024 * 1024
F32 = jnp.float32
BF16 = jnp.bfloat16


def round_up(value, multiple):
    return -(-value // multiple) * multiple


def power_of_two(value):
    return value & (value - 1) == 0


class Sizes:
    def __init__(self, group_total, states, conv_states, projected):
        self.groups = n = group_total
        self.rows, self.heads, self.dk, _ = states.shape
        self.taps, self.parts = conv_states.shape[1:3]
        self.steps = projected.shape[0]
        self.slots = n * self.rows
        self.cuts = n // self.heads
        far = range(self.heads)
        if power_of_two(self.heads):
            far = [h ^ (h >> 1) for h in far]
        self.order = [h * self.cuts + cut for cut in range(self.cuts) for h in far]
        self.place_of = [self.order.index(p) for p in range(n)]
        self.cols = self.dk // self.cuts
        self.state_rows = self.rows * self.cols
        self.quarter = self.dk // 4
        self.decay_at = self.steps * 2
        self.hist_at = self.decay_at + self.steps
        self.value_at = self.hist_at + self.taps * 2
        self.value_depth = -(-(self.steps + self.taps) // 4)
        self.flag_at = self.value_at + self.value_depth
        self.info_sets = self.padded(self.flag_at + 1)
        self.info_rows = self.rows * self.info_sets
        self.back_sets = self.steps + self.taps * self.parts
        self.back_depth = self.padded(-(-self.back_sets // 4))
        self.back_rows = self.rows * self.back_depth
        self.read_rows = round_up(-(-self.steps // self.back_depth) * self.back_rows, 16)
        self.whole_tiles = self.cols % 16 == 0
        self.width = max(LANES, 8 * self.cols)
        self.tile = self.width // self.cols

    def padded(self, sets):
        while sets * self.rows % 8:
            sets += 1
        return sets

    def read_at(self, t, r):
        return t // self.back_depth * self.back_rows + r * self.back_depth + t % self.back_depth


def mod(value, size):
    return value & (size - 1) if size & (size - 1) == 0 else lax.rem(value, size)


def quotient(value, size):
    if size & (size - 1) == 0:
        return lax.shift_right_logical(value, jnp.int32(size.bit_length() - 1))
    return lax.div(value, jnp.int32(size))


def in_block(sz, shape, cut, shift):
    start = cut * sz.cols + shift * sz.quarter
    return mod(iota(shape, len(shape) - 1) + (2 * sz.dk - start), sz.dk) < sz.cols


def iota(shape, dim):
    return lax.broadcasted_iota(jnp.int32, shape, dim)


def one_hot(condition):
    return jnp.where(condition, 1.0, 0.0).astype(BF16)


def dot(lhs, rhs, lhs_dim=1, rhs_dim=0):
    return lax.dot_general(
        lhs, rhs, (((lhs_dim,), (rhs_dim,)), ((), ())), preferred_element_type=F32
    )


def pack_kernel(sz, *refs):
    count = 8
    sources, states_hbm = refs[:count], refs[count]
    pieces, pick, place, final, taps = refs[count + 1 : count + 6]
    scratch = refs[count + 6 :]
    targets, live, rate, beta, proj, hist, decay, filters, states = scratch[: count + 1]
    info, tails, strengths, in_sems = scratch[count + 1 :]
    copies = []

    def start(source, target):
        copies.append(pltpu.make_async_copy(source, target, in_sems.at[len(copies)]))
        copies[-1].start()

    for source, target in zip(sources, scratch):
        start(source, target)
    start(states_hbm, states)
    for copy in copies[:count]:
        copy.wait()
    route(sz, targets, pick, place, final)
    own_head = lax.axis_index("rep") // sz.cuts
    head_lanes = pl.ds(pl.multiple_of(own_head * sz.dk, sz.dk), sz.dk)
    for part in range(sz.parts):
        taps[part] = filters[part, :, head_lanes]
    channels, dk = sz.heads * sz.dk, sz.dk
    lane_head = quotient(iota((1, channels), 1), dk)
    rates = jnp.zeros((1, channels), F32)
    for h in range(sz.heads):
        rates = jnp.where(lane_head == h, rate[:, h : h + 1], rates)
    row_ids = iota((sz.rows, channels), 0)

    def keep(target, index, value):
        for h in range(sz.heads):
            rows = pl.ds(index, sz.rows, stride=sz.info_sets)
            target[h, rows, :] = value[:, h * dk : (h + 1) * dk]

    def keep_value(index, value):
        shift = index // sz.value_depth
        at = sz.value_at + index % sz.value_depth
        if shift:
            heads = [value[:, h * dk : (h + 1) * dk] for h in range(sz.heads)]
            heads = [pltpu.roll(head, shift * sz.quarter, 1) for head in heads]
            keep(tails.at[shift - 1], at, jnp.concatenate(heads, axis=1))
        else:
            keep(info, at, value)

    for t in range(sz.steps):
        for part in range(2):
            keep(info, t * 2 + part, proj[t, part].astype(F32))
        keep_value(t, proj[t, 2].astype(F32))
        x = decay[t]
        softplus = jnp.maximum(x, 0.0) + jnp.log1p(jnp.exp(-jnp.abs(x)))
        keep(
            info,
            sz.decay_at + t,
            jnp.where(row_ids < live[:, t : t + 1], rates * softplus, 0.0),
        )
    for tap in range(sz.taps):
        for part in range(2):
            keep(info, sz.hist_at + tap * 2 + part, hist[tap, part].astype(F32))
        keep_value(sz.steps + tap, hist[tap, 2].astype(F32))
    lane = iota((sz.heads, dk), 1)
    strengths[...] = jnp.zeros(strengths.shape, F32)
    for r in range(sz.rows):
        strengths[:, : sz.steps] = beta[r]
        lives = jnp.zeros((sz.heads, dk), F32)
        for t in range(sz.steps):
            lives = jnp.where((lane == t) & (r < live[:, t : t + 1]), 1.0, lives)
        strength = lives / (1.0 + jnp.exp(-strengths[...]))
        high = strength.astype(BF16).astype(F32)
        flags = high + pltpu.roll(lives, 16, 1) + pltpu.roll(strength - high, 32, 1)
        for h in range(sz.heads):
            at = r * sz.info_sets + sz.flag_at
            info[h, at : at + 1, :] = flags[h : h + 1]
    wide = [
        r * sz.info_sets + sz.value_at + i for r in range(sz.rows) for i in range(sz.value_depth)
    ]
    masks = {}
    for tile in sorted({at // 8 for at in wide}):
        row = iota((8, dk), 0) + tile * 8
        narrow = functools.reduce(jnp.logical_or, [row == at for at in wide if at // 8 == tile])
        masks[tile] = [
            [narrow & in_block(sz, (8, dk), cut, shift) for shift in range(1, 4)]
            for cut in range(sz.cuts)
        ]
    shared = [
        at for at in range(0, sz.info_rows, 16) if at // 8 not in masks and at // 8 + 1 not in masks
    ]
    held = [[info[h, at : at + 16, :].astype(BF16) for at in shared] for h in range(sz.heads)]
    for copy in copies[count:]:
        copy.wait()
    for h in range(sz.heads):
        across = [states[r, h].T for r in range(sz.rows)]
        for cut in range(sz.cuts):
            p, at = sz.place_of[h * sz.cuts + cut], cut * sz.cols
            own = [a[at : at + sz.cols] for a in across]
            pieces[p, : sz.state_rows, :] = jnp.concatenate(own, axis=0).astype(BF16)
            for at, value in zip(shared, held[h]):
                to = sz.state_rows + at
                pieces[p, to : to + value.shape[0], :] = value
            for at in range(0, sz.info_rows, 16):
                if at in shared:
                    continue
                rest = []
                for tile in range(at // 8, min(at + 16, sz.info_rows) // 8):
                    rows = slice(tile * 8, tile * 8 + 8)
                    value = info[h, rows, :]
                    for shift in range(3 if tile in masks else 0):
                        value = jnp.where(masks[tile][cut][shift], tails[shift, h, rows, :], value)
                    rest.append(value)
                rest = jnp.concatenate(rest, axis=0)
                to = sz.state_rows + at
                pieces[p, to : to + rest.shape[0], :] = rest.astype(BF16)


def route(sz, targets, pick, place, final):
    n, T = sz.slots, sz.steps
    steps = [one_hot(iota((n, n), 0) == targets[t : t + 1, :]) for t in range(T)]
    chain = [steps[0]]
    for t in range(1, T):
        if t % 2:
            pair = dot(steps[t], steps[t - 1]).astype(BF16)
            chain.append(dot(pair, chain[t - 2]).astype(BF16) if t > 1 else pair)
        else:
            chain.append(dot(steps[t], chain[t - 1]).astype(BF16))
    for t in range(T):
        place[t] = chain[t]
        pick[t] = chain[t].astype(F32).T.astype(BF16)
    slot = iota((8, n), 1)
    row, group = mod(slot, sz.rows), quotient(slot, sz.rows)
    head, cut = quotient(group, sz.cuts), mod(group, sz.cuts)
    far = head
    step = 1
    while power_of_two(sz.heads) and step < sz.heads:
        far = far ^ lax.shift_right_logical(far, jnp.int32(step))
        step *= 2
    weights = (cut * sz.heads + far) * sz.rows + row
    places = dot(weights.astype(F32).astype(BF16), chain[T - 1])
    final[...] = (places + 0.5).astype(jnp.int32)


def over_blocks(sz, value):
    step = sz.cols
    while step < sz.dk:
        value = value + pltpu.roll(value, step, 1)
        step *= 2
    return value


def gate_factor(sz, live, gain, gate, factor):
    factor[...] = jnp.zeros(factor.shape, F32)
    row = iota((sz.read_rows, sz.dk), 0)
    alive = row < 0
    for t in range(sz.steps):
        for r in range(sz.rows):
            at = sz.read_at(t, r)
            factor[at : at + 1, :] = gate[t, r : r + 1].astype(F32)
            alive = alive | ((row == at) & (r < live[:, t : t + 1]))
    for h in range(sz.heads):
        lanes = slice(h * sz.dk, (h + 1) * sz.dk)
        gates = gain[...] / (1.0 + jnp.exp(-factor[:, lanes]))
        factor[:, lanes] = jnp.where(alive, gates, 0.0)


def step_kernel(sz, filters, pick, place, came, *refs):
    count = sz.groups
    sources, sent, factor, scratch = refs[:4], refs[4], refs[5], refs[6:]
    scalars, live, gain, gate, info, parked, later, back, sems = scratch
    copies = []
    for i, (source, target) in enumerate(zip(sources, scratch)):
        copies.append(pltpu.make_async_copy(source, target, sems.at[i]))
        copies[-1].start()
    n, dk, T = sz.slots, sz.dk, sz.steps
    mine = lax.axis_index("rep")
    cut = lax.rem(mine, sz.cuts)
    stride = sz.info_rows
    for g in range(count):
        info[g * stride : (g + 1) * stride, :] = came[sz.place_of[g], sz.state_rows :, :].astype(F32)

    def gather(index):
        return info[pl.ds(index, n, stride=sz.info_sets), :]

    def gather_value(index):
        value = gather(sz.value_at + index % sz.value_depth)
        shift = index // sz.value_depth
        return pltpu.roll(value, dk - shift * sz.quarter, 1) if shift else value

    weights = [filters[part] for part in range(sz.parts)]
    flags = gather(sz.flag_at)
    window = [
        [gather(sz.hist_at + tap * 2 + part) for part in range(2)]
        + [gather_value(T + tap)]
        for tap in range(sz.taps)
    ]
    active, retains, strengths = [], [], []
    for t in range(T):
        slots = [gather(t * 2 + part) for part in range(2)]
        slots += [gather_value(t), gather(sz.decay_at + t), flags]
        moved = dot(pick[t], jnp.concatenate(slots, axis=1).astype(BF16))
        inputs = [moved[:, i * dk : (i + 1) * dk] for i in range(sz.parts + 2)]
        moved_flags = inputs[sz.parts + 1]
        strength = moved_flags[:, t : t + 1] + moved_flags[:, 32 + t : 33 + t]
        alive = moved_flags[:, 16 + t : 17 + t] > 0.5
        for part in range(sz.parts):
            frames = [window[tap][part] for tap in range(sz.taps)] + [inputs[part]]
            total = frames[0] * weights[part][:1]
            for j in range(1, sz.taps + 1):
                total = total + frames[j] * weights[part][j : j + 1]
            active.append(total / (1.0 + jnp.exp(-total)))
            for tap in range(sz.taps):
                window[tap][part] = jnp.where(alive, frames[tap + 1], frames[tap])
        retains.append(jnp.exp(-inputs[sz.parts]))
        strengths.append(strength)

    ones = jnp.ones((dk, dk), BF16)

    def summed(products):
        sums = dot(jnp.concatenate([x.astype(BF16) for x in products], axis=0), ones)
        return [sums[i * n : (i + 1) * n] for i in range(len(products))]

    values = active[2 :: sz.parts]
    units = [x for i, x in enumerate(active) if i % sz.parts < 2]
    norms = summed([x * x for x in units])
    units = [x * lax.rsqrt(norm + EPSILON) for x, norm in zip(units, norms)]
    reach = jnp.ones((n, dk), F32)
    keys = []
    from_state, pairs = [], []
    for t in range(T):
        query, key = units[2 * t], units[2 * t + 1]
        reach = reach * retains[t]
        keys = [k * retains[t] for k in keys]
        pairs += [key * k for k in keys]
        keys.append(key)
        pairs += [query * k for k in keys]
        from_state += [reach * key, reach * query]
    mixes = summed(pairs)
    key_mix, read_mix = [], []
    for t in range(T):
        key_mix.append(mixes[:t])
        read_mix.append(mixes[t : 2 * t + 1])
        mixes = mixes[2 * t + 1 :]

    own_lanes = in_block(sz, (n, dk), cut, 0)
    wide = sz.width // dk
    value_cols = []
    for value in values:
        value = over_blocks(sz, jnp.where(own_lanes, value, 0.0))
        value_cols.append(jnp.concatenate([value] * wide, axis=1))
    lane_row = quotient(iota((sz.tile, sz.width), 1), sz.cols)
    own = iota((sz.tile, sz.width), 0) == lane_row
    readouts = [[] for _ in range(T)]

    def widen(value):
        return jnp.concatenate([value] * wide, axis=1)

    for at in range(0, n, sz.tile):
        rows = slice(at, at + sz.tile)
        block = []
        for g in range(at // sz.rows, (at + sz.tile) // sz.rows):
            for r in range(sz.rows):
                if sz.whole_tiles:
                    block.append(came[sz.place_of[g], r * sz.cols : (r + 1) * sz.cols, :])
                else:
                    piece = came[sz.place_of[g], : sz.state_rows, :].astype(F32)
                    block.append(piece[r * sz.cols : (r + 1) * sz.cols])
        seen = dot(
            jnp.concatenate([x[rows] for x in from_state], axis=0).astype(BF16),
            jnp.concatenate(block, axis=0).astype(BF16),
            1,
            1,
        )
        seen = [seen[i * sz.tile : (i + 1) * sz.tile] for i in range(2 * T)]
        writes = []
        for t in range(T):
            target = value_cols[t][rows] - seen[2 * t]
            target = jnp.where(own, target, 0.0)
            for s in range(t):
                target = target - widen(key_mix[t][s][rows]) * writes[s]
            writes.append(strengths[t][rows] * target)
            read = jnp.where(own, seen[2 * t + 1], 0.0)
            for s in range(t + 1):
                read = read + widen(read_mix[t][s][rows]) * writes[s]
            readouts[t].append(read * dk ** (-0.5))
        added = dot(
            jnp.concatenate(writes, axis=0).astype(BF16),
            jnp.concatenate([k[rows] for k in keys], axis=0).astype(BF16),
            0,
            0,
        )
        for i in range(sz.tile):
            part = block[i].astype(F32) * reach[at + i : at + i + 1]
            part = part + added[i * sz.cols : (i + 1) * sz.cols]
            parked[at + i] = part.astype(parked.dtype)
    blocks = [in_block(sz, (n, dk), cut, shift) for shift in range(4)]
    placed = [None] * sz.back_depth
    kept = [None] * sz.back_depth
    for index in range(sz.back_sets):
        shift, slot = index // sz.back_depth, index % sz.back_depth
        if index < T:
            folded = jnp.concatenate(readouts[index], axis=0)
            folded = functools.reduce(
                jnp.add, [folded[:, i * dk : (i + 1) * dk] for i in range(wide)]
            )
            folded = jnp.where(blocks[shift], over_blocks(sz, folded), 0.0)
            value = dot(place[index], folded.astype(BF16))
            placed[slot] = value if placed[slot] is None else placed[slot] + value
        else:
            value = window[(index - T) // sz.parts][(index - T) % sz.parts]
            if shift:
                value = pltpu.roll(value, shift * sz.quarter, 1)
            rest = jnp.zeros((n, dk), F32) if kept[slot] is None else kept[slot]
            kept[slot] = jnp.where(blocks[shift], value, rest)
    kept = [jnp.zeros((n, dk), F32) if value is None else value for value in kept]
    held = dot(place[T - 1], jnp.concatenate(kept, axis=1).astype(BF16))
    for slot in range(sz.back_depth):
        value = held[:, slot * dk : (slot + 1) * dk]
        if placed[slot] is not None:
            value = value + placed[slot]
        back[pl.ds(slot, n, stride=sz.back_depth), :] = value
    for copy in copies:
        copy.wait()
    gate_factor(sz, live, gain, gate, factor)
    for at in range(n):
        to = scalars[0, at]
        if sz.whole_tiles:
            start_row = pl.multiple_of(mod(to, sz.rows) * sz.cols, sz.cols)
            sent[quotient(to, sz.rows), pl.ds(start_row, sz.cols), :] = parked[at]
        else:
            later[pl.ds(pl.multiple_of(to * sz.cols, sz.cols), sz.cols), :] = parked[at]
    for g in range(count):
        p = sz.place_of[g]
        if not sz.whole_tiles:
            sent[p, : sz.state_rows, :] = later[
                p * sz.state_rows : (p + 1) * sz.state_rows, :
            ].astype(BF16)
        sent[p, sz.state_rows :, :] = back[
            g * sz.back_rows : (g + 1) * sz.back_rows, :
        ].astype(BF16)


def unpack(sz, came, h, wanted):
    shape = (sz.back_rows, sz.dk)
    pieces = [
        came[sz.place_of[h * sz.cuts + cut], sz.state_rows :, :].astype(F32)
        for cut in range(sz.cuts)
    ]
    narrow = {}
    for shift in sorted({index // sz.back_depth for index in wanted}):
        value = pieces[0]
        for cut in range(1, sz.cuts):
            value = jnp.where(in_block(sz, shape, cut, shift), pieces[cut], value)
        if shift:
            value = pltpu.roll(value, sz.dk - shift * sz.quarter, 1)
        narrow[shift] = value

    return narrow


def project_kernel(sz, blocks, factor, weight, came, *refs):
    dk = sz.dk
    partials, kept = refs[: blocks - 1], refs[blocks - 1]
    gated = []
    for h in range(sz.heads):
        lanes = slice(h * dk, (h + 1) * dk)
        narrow = unpack(sz, came, h, range(sz.steps))
        total = [narrow[quarter] for quarter in sorted(narrow)]
        spare = sz.read_rows - len(total) * sz.back_rows
        if spare:
            total.append(jnp.zeros((spare, dk), F32))
        total = jnp.concatenate(total, axis=0)
        scaling = lax.rsqrt(jnp.mean(total * total, axis=1, keepdims=True) + EPSILON)
        gated.append(total * scaling * factor[:, lanes])
    gated = jnp.concatenate(gated, axis=1).astype(BF16)
    kept[...] = gated
    for shift in range(1, blocks):
        project(sz, blocks, shift, gated, weight, partials[shift - 1])


def project(sz, blocks, shift, gated, weight, partial):
    columns = weight.shape[1] // blocks
    lanes = slice(None)
    if blocks > 1:
        at = lax.rem(lax.axis_index("head") + shift, blocks) * columns
        lanes = pl.ds(pl.multiple_of(at, LANES), columns)
    result = dot(gated, weight[:, lanes])
    for t in range(sz.steps):
        rows = [result[at : at + 1] for at in (sz.read_at(t, r) for r in range(sz.rows))]
        partial[t] = jnp.concatenate(rows, axis=0).astype(partial.dtype)


def restore_kernel(sz, blocks, gated, weight, came, states, partial, hist):
    project(sz, blocks, 0, gated[...], weight, partial)
    for h in range(sz.heads):
        narrow = unpack(sz, came, h, range(sz.steps, sz.back_sets))
        for tap in range(sz.taps):
            for part in range(sz.parts):
                index = sz.steps + tap * sz.parts + part
                held = narrow[index // sz.back_depth]
                at = index % sz.back_depth
                rows = [held[at + r * sz.back_depth :][:1] for r in range(sz.rows)]
                value = jnp.concatenate(rows, axis=0)
                hist[tap, part, :, h * sz.dk : (h + 1) * sz.dk] = value.astype(BF16)
    kind = BF16 if sz.whole_tiles else F32
    for r in range(sz.rows):
        for h in range(sz.heads):
            cuts = [
                came[sz.place_of[h * sz.cuts + cut], : sz.state_rows, :].astype(kind)[
                    r * sz.cols : (r + 1) * sz.cols
                ]
                for cut in range(sz.cuts)
            ]
            states[r, h] = jnp.concatenate(cuts, axis=0).T.astype(F32)


def vmem():
    return pl.BlockSpec(memory_space=pltpu.VMEM)


def smem():
    return pl.BlockSpec(memory_space=pltpu.SMEM)


def anywhere():
    return pl.BlockSpec(memory_space=pl.ANY)


def in_hbm(value):
    return pltpu.with_memory_space_constraint(value, pltpu.HBM)


def call(body, outs, ins, out_specs, scratch, name):
    return pl.pallas_call(
        body,
        out_shape=outs,
        in_specs=ins,
        out_specs=out_specs,
        scratch_shapes=scratch,
        compiler_params=pltpu.CompilerParams(vmem_limit_bytes=VMEM_LIMIT),
        name=name,
    )


def exchange(sz, pieces):
    return lax.all_to_all(
        pieces, "rep", split_axis=0, concat_axis=0, axis_index_groups=[sz.order], tiled=True
    )


def local(
    group_total,
    head_total,
    states,
    conv_states,
    projected,
    conv_weight,
    decay_input,
    decay_rate,
    beta_logit,
    out_gate,
    norm_gain,
    out_weight,
    destinations,
    live_counts,
):
    sz = Sizes(group_total, states, conv_states, projected)
    n, channels = sz.groups, sz.heads * sz.dk
    shape = jax.ShapeDtypeStruct
    lives = live_counts.T
    arguments = (
        destinations,
        lives,
        decay_rate.reshape(1, sz.heads),
        beta_logit.transpose(1, 2, 0),
        projected.transpose(0, 2, 1, 3),
        conv_states.transpose(1, 2, 0, 3),
        decay_input,
        conv_weight.transpose(1, 0, 2),
        states,
    )
    routes = shape((sz.steps, sz.slots, sz.slots), BF16)
    pieces, pick, place, final, taps = call(
        functools.partial(pack_kernel, sz),
        (
            shape((n, sz.state_rows + sz.info_rows, sz.dk), BF16),
            routes,
            routes,
            shape((8, sz.slots), jnp.int32),
            shape((sz.parts, sz.taps + 1, sz.dk), F32),
        ),
        [anywhere()] * len(arguments),
        (vmem(),) * 5,
        [pltpu.VMEM(x.shape, x.dtype) for x in arguments]
        + [
            pltpu.VMEM((sz.heads, sz.info_rows, sz.dk), F32),
            pltpu.VMEM((3, sz.heads, sz.info_rows, sz.dk), F32),
            pltpu.VMEM((sz.heads, sz.dk), F32),
            pltpu.SemaphoreType.DMA((len(arguments),)),
        ],
        "pack",
    )(*[in_hbm(x) for x in arguments])
    came = exchange(sz, pieces)
    gain = norm_gain.reshape(1, sz.dk)
    stepped, factor = call(
        functools.partial(step_kernel, sz),
        (
            shape((n, sz.state_rows + sz.back_rows, sz.dk), BF16),
            shape((sz.read_rows, channels), F32),
        ),
        [vmem()] * 4 + [anywhere()] * 4,
        (vmem(), vmem()),
        [
            pltpu.SMEM((8, sz.slots), jnp.int32),
            pltpu.VMEM(lives.shape, lives.dtype),
            pltpu.VMEM(gain.shape, F32),
            pltpu.VMEM(out_gate.shape, BF16),
            pltpu.VMEM((n * sz.info_rows, sz.dk), F32),
            pltpu.VMEM((sz.slots, sz.cols, sz.dk), BF16 if sz.whole_tiles else F32),
            pltpu.VMEM((8 if sz.whole_tiles else n * sz.state_rows, sz.dk), F32),
            pltpu.VMEM((n * sz.back_rows, sz.dk), F32),
            pltpu.SemaphoreType.DMA((4,)),
        ],
        "steps",
    )(taps, pick, place, came, final, in_hbm(lives), in_hbm(gain), in_hbm(out_gate))
    back = exchange(sz, stepped)
    width = out_weight.shape[1]
    columns = width // head_total
    blocks = head_total if columns % LANES == 0 else 1
    *partials, gated = call(
        functools.partial(project_kernel, sz, blocks),
        tuple(shape((sz.steps, sz.rows, columns), BF16) for _ in range(1, blocks))
        + (shape((sz.read_rows, channels), BF16),),
        [vmem()] * 3,
        tuple([vmem()] * blocks),
        [],
        "project",
    )(factor, out_weight, back)
    states_out, own, conv_out = call(
        functools.partial(restore_kernel, sz, blocks),
        (
            shape(states.shape, F32),
            shape((sz.steps, sz.rows, width // blocks), F32),
            shape((sz.taps, sz.parts, sz.rows, channels), BF16),
        ),
        [vmem()] * 3,
        (vmem(),) * 3,
        [],
        "restore",
    )(gated, out_weight, back)
    partials = [own, *partials]
    if blocks != head_total:
        mine = lax.axis_index("head")
        partials = [
            lax.dynamic_slice_in_dim(
                partials[0], lax.rem(mine + shift, head_total) * columns, columns, 2
            )
            for shift in range(head_total)
        ]
    total = partials[0]
    for shift in range(1, head_total):
        pairs = [(i, (i + shift) % head_total) for i in range(head_total)]
        passed = lax.ppermute(partials[shift].astype(BF16), "head", pairs)
        total = total + passed.astype(F32)
    return (total.astype(BF16), states_out, conv_out.transpose(2, 0, 1, 3))


def solution(mesh):
    placed = (
        P("rep", "head", None, None),
        P("rep", None, None, "head"),
        P(None, "rep", None, "head"),
        P(None, None, "head"),
        P(None, "rep", "head"),
        P("head"),
        P(None, "rep", "head"),
        P(None, "rep", "head"),
        P(),
        P("head", None),
        P(),
        P(None, "rep"),
    )
    return jax.shard_map(
        functools.partial(local, mesh.shape["rep"], mesh.shape["head"]),
        mesh=mesh,
        in_specs=placed,
        out_specs=(
            P(None, "rep", "head"),
            P("rep", "head", None, None),
            P("rep", None, None, "head"),
        ),
        check_vma=False,
    )
```

```python
import functools

import jax
import jax.numpy as jnp
from jax import lax
from jax.experimental import pallas as pl
from jax.experimental.pallas import tpu as pltpu
from jax.sharding import PartitionSpec as P

EPSILON = 1e-06
LANES = 128
VMEM_LIMIT = 32 * 1024 * 1024
F32 = jnp.float32
BF16 = jnp.bfloat16


def round_up(value, multiple):
    return -(-value // multiple) * multiple


def power_of_two(value):
    return value & (value - 1) == 0


class Sizes:
    def __init__(self, group_total, states, conv_states, projected):
        self.groups = n = group_total
        self.rows, self.heads, self.dk, _ = states.shape
        self.taps, self.parts = conv_states.shape[1:3]
        self.steps = projected.shape[0]
        self.slots = n * self.rows
        self.cuts = n // self.heads
        far = range(self.heads)
        if power_of_two(self.heads):
            far = [h ^ (h >> 1) for h in far]
        self.order = [h * self.cuts + cut for cut in range(self.cuts) for h in far]
        self.place_of = [self.order.index(p) for p in range(n)]
        self.cols = self.dk // self.cuts
        self.state_rows = self.rows * self.cols
        self.quarter = self.dk // 4
        self.decay_at = self.steps * 2
        self.hist_at = self.decay_at + self.steps
        self.value_at = self.hist_at + self.taps * 2
        self.value_depth = -(-(self.steps + self.taps) // 4)
        self.flag_at = self.value_at + self.value_depth
        self.info_sets = self.padded(self.flag_at + 1)
        self.info_rows = self.rows * self.info_sets
        self.back_sets = self.steps + self.taps * self.parts
        self.back_depth = self.padded(-(-self.back_sets // 4))
        self.back_rows = self.rows * self.back_depth
        self.read_rows = round_up(-(-self.steps // self.back_depth) * self.back_rows, 16)
        self.whole_tiles = self.cols % 16 == 0
        self.width = max(LANES, 8 * self.cols)
        self.tile = self.width // self.cols

    def padded(self, sets):
        while sets * self.rows % 8:
            sets += 1
        return sets

    def read_at(self, t, r):
        return t // self.back_depth * self.back_rows + r * self.back_depth + t % self.back_depth


def mod(value, size):
    return value & (size - 1) if size & (size - 1) == 0 else lax.rem(value, size)


def quotient(value, size):
    if size & (size - 1) == 0:
        return lax.shift_right_logical(value, jnp.int32(size.bit_length() - 1))
    return lax.div(value, jnp.int32(size))


def in_block(sz, shape, cut, shift):
    start = cut * sz.cols + shift * sz.quarter
    return mod(iota(shape, len(shape) - 1) + (2 * sz.dk - start), sz.dk) < sz.cols


def iota(shape, dim):
    return lax.broadcasted_iota(jnp.int32, shape, dim)


def one_hot(condition):
    return jnp.where(condition, 1.0, 0.0).astype(BF16)


def dot(lhs, rhs, lhs_dim=1, rhs_dim=0):
    return lax.dot_general(
        lhs, rhs, (((lhs_dim,), (rhs_dim,)), ((), ())), preferred_element_type=F32
    )


def pack_kernel(sz, *refs):
    count = 8
    sources, states_hbm = refs[:count], refs[count]
    pieces, pick, place, final, taps = refs[count + 1 : count + 6]
    scratch = refs[count + 6 :]
    targets, live, rate, beta, proj, hist, decay, filters, states = scratch[: count + 1]
    info, tails, strengths, in_sems = scratch[count + 1 :]
    copies = []

    def start(source, target):
        copies.append(pltpu.make_async_copy(source, target, in_sems.at[len(copies)]))
        copies[-1].start()

    for source, target in zip(sources, scratch):
        start(source, target)
    start(states_hbm, states)
    for copy in copies[:count]:
        copy.wait()
    route(sz, targets, pick, place, final)
    own_head = lax.axis_index("rep") // sz.cuts
    head_lanes = pl.ds(pl.multiple_of(own_head * sz.dk, sz.dk), sz.dk)
    for part in range(sz.parts):
        taps[part] = filters[part, :, head_lanes]
    channels, dk = sz.heads * sz.dk, sz.dk
    lane_head = quotient(iota((1, channels), 1), dk)
    rates = jnp.zeros((1, channels), F32)
    for h in range(sz.heads):
        rates = jnp.where(lane_head == h, rate[:, h : h + 1], rates)
    row_ids = iota((sz.rows, channels), 0)

    def keep(target, index, value):
        for h in range(sz.heads):
            rows = pl.ds(index, sz.rows, stride=sz.info_sets)
            target[h, rows, :] = value[:, h * dk : (h + 1) * dk]

    def keep_value(index, value):
        shift = index // sz.value_depth
        at = sz.value_at + index % sz.value_depth
        if shift:
            heads = [value[:, h * dk : (h + 1) * dk] for h in range(sz.heads)]
            heads = [pltpu.roll(head, shift * sz.quarter, 1) for head in heads]
            keep(tails.at[shift - 1], at, jnp.concatenate(heads, axis=1))
        else:
            keep(info, at, value)

    for t in range(sz.steps):
        for part in range(2):
            keep(info, t * 2 + part, proj[t, part].astype(F32))
        keep_value(t, proj[t, 2].astype(F32))
        x = decay[t]
        softplus = jnp.maximum(x, 0.0) + jnp.log1p(jnp.exp(-jnp.abs(x)))
        keep(
            info,
            sz.decay_at + t,
            jnp.where(row_ids < live[:, t : t + 1], rates * softplus, 0.0),
        )
    for tap in range(sz.taps):
        for part in range(2):
            keep(info, sz.hist_at + tap * 2 + part, hist[tap, part].astype(F32))
        keep_value(sz.steps + tap, hist[tap, 2].astype(F32))
    lane = iota((sz.heads, dk), 1)
    strengths[...] = jnp.zeros(strengths.shape, F32)
    for r in range(sz.rows):
        strengths[:, : sz.steps] = beta[r]
        lives = jnp.zeros((sz.heads, dk), F32)
        for t in range(sz.steps):
            lives = jnp.where((lane == t) & (r < live[:, t : t + 1]), 1.0, lives)
        strength = lives / (1.0 + jnp.exp(-strengths[...]))
        high = strength.astype(BF16).astype(F32)
        flags = high + pltpu.roll(lives, 16, 1) + pltpu.roll(strength - high, 32, 1)
        for h in range(sz.heads):
            at = r * sz.info_sets + sz.flag_at
            info[h, at : at + 1, :] = flags[h : h + 1]
    wide = [
        r * sz.info_sets + sz.value_at + i for r in range(sz.rows) for i in range(sz.value_depth)
    ]
    masks = {}
    for tile in sorted({at // 8 for at in wide}):
        row = iota((8, dk), 0) + tile * 8
        narrow = functools.reduce(jnp.logical_or, [row == at for at in wide if at // 8 == tile])
        masks[tile] = [
            [narrow & in_block(sz, (8, dk), cut, shift) for shift in range(1, 4)]
            for cut in range(sz.cuts)
        ]
    shared = [
        at for at in range(0, sz.info_rows, 16) if at // 8 not in masks and at // 8 + 1 not in masks
    ]
    held = [[info[h, at : at + 16, :].astype(BF16) for at in shared] for h in range(sz.heads)]
    for copy in copies[count:]:
        copy.wait()
    for h in range(sz.heads):
        across = [states[r, h].T for r in range(sz.rows)]
        for cut in range(sz.cuts):
            p, at = sz.place_of[h * sz.cuts + cut], cut * sz.cols
            own = [a[at : at + sz.cols] for a in across]
            pieces[p, : sz.state_rows, :] = jnp.concatenate(own, axis=0).astype(BF16)
            for at, value in zip(shared, held[h]):
                to = sz.state_rows + at
                pieces[p, to : to + value.shape[0], :] = value
            for at in range(0, sz.info_rows, 16):
                if at in shared:
                    continue
                rest = []
                for tile in range(at // 8, min(at + 16, sz.info_rows) // 8):
                    rows = slice(tile * 8, tile * 8 + 8)
                    value = info[h, rows, :]
                    for shift in range(3 if tile in masks else 0):
                        value = jnp.where(masks[tile][cut][shift], tails[shift, h, rows, :], value)
                    rest.append(value)
                rest = jnp.concatenate(rest, axis=0)
                to = sz.state_rows + at
                pieces[p, to : to + rest.shape[0], :] = rest.astype(BF16)


def route(sz, targets, pick, place, final):
    n, T = sz.slots, sz.steps
    steps = [one_hot(iota((n, n), 0) == targets[t : t + 1, :]) for t in range(T)]
    chain = [steps[0]]
    for t in range(1, T):
        if t % 2:
            pair = dot(steps[t], steps[t - 1]).astype(BF16)
            chain.append(dot(pair, chain[t - 2]).astype(BF16) if t > 1 else pair)
        else:
            chain.append(dot(steps[t], chain[t - 1]).astype(BF16))
    for t in range(T):
        place[t] = chain[t]
        pick[t] = chain[t].astype(F32).T.astype(BF16)
    slot = iota((8, n), 1)
    row, group = mod(slot, sz.rows), quotient(slot, sz.rows)
    head, cut = quotient(group, sz.cuts), mod(group, sz.cuts)
    far = head
    step = 1
    while power_of_two(sz.heads) and step < sz.heads:
        far = far ^ lax.shift_right_logical(far, jnp.int32(step))
        step *= 2
    weights = (cut * sz.heads + far) * sz.rows + row
    places = dot(weights.astype(F32).astype(BF16), chain[T - 1])
    final[...] = (places + 0.5).astype(jnp.int32)


def over_blocks(sz, value):
    step = sz.cols
    while step < sz.dk:
        value = value + pltpu.roll(value, step, 1)
        step *= 2
    return value


def gate_factor(sz, live, gain, gate, factor):
    factor[...] = jnp.zeros(factor.shape, F32)
    row = iota((sz.read_rows, sz.dk), 0)
    alive = row < 0
    for t in range(sz.steps):
        for r in range(sz.rows):
            at = sz.read_at(t, r)
            factor[at : at + 1, :] = gate[t, r : r + 1].astype(F32)
            alive = alive | ((row == at) & (r < live[:, t : t + 1]))
    for h in range(sz.heads):
        lanes = slice(h * sz.dk, (h + 1) * sz.dk)
        gates = gain[...] / (1.0 + jnp.exp(-factor[:, lanes]))
        factor[:, lanes] = jnp.where(alive, gates, 0.0)


def step_kernel(sz, filters, pick, place, came, *refs):
    count = sz.groups
    sources, sent, factor, scratch = refs[:4], refs[4], refs[5], refs[6:]
    scalars, live, gain, gate, info, parked, later, back, sems = scratch
    copies = []
    for i, (source, target) in enumerate(zip(sources, scratch)):
        copies.append(pltpu.make_async_copy(source, target, sems.at[i]))
        copies[-1].start()
    n, dk, T = sz.slots, sz.dk, sz.steps
    mine = lax.axis_index("rep")
    cut = lax.rem(mine, sz.cuts)
    stride = sz.info_rows
    for g in range(count):
        info[g * stride : (g + 1) * stride, :] = came[sz.place_of[g], sz.state_rows :, :].astype(F32)

    def gather(index):
        return info[pl.ds(index, n, stride=sz.info_sets), :]

    def gather_value(index):
        value = gather(sz.value_at + index % sz.value_depth)
        shift = index // sz.value_depth
        return pltpu.roll(value, dk - shift * sz.quarter, 1) if shift else value

    weights = [filters[part] for part in range(sz.parts)]
    flags = gather(sz.flag_at)
    window = [
        [gather(sz.hist_at + tap * 2 + part) for part in range(2)]
        + [gather_value(T + tap)]
        for tap in range(sz.taps)
    ]
    active, retains, strengths = [], [], []
    for t in range(T):
        slots = [gather(t * 2 + part) for part in range(2)]
        slots += [gather_value(t), gather(sz.decay_at + t), flags]
        moved = dot(pick[t], jnp.concatenate(slots, axis=1).astype(BF16))
        inputs = [moved[:, i * dk : (i + 1) * dk] for i in range(sz.parts + 2)]
        moved_flags = inputs[sz.parts + 1]
        strength = moved_flags[:, t : t + 1] + moved_flags[:, 32 + t : 33 + t]
        alive = moved_flags[:, 16 + t : 17 + t] > 0.5
        for part in range(sz.parts):
            frames = [window[tap][part] for tap in range(sz.taps)] + [inputs[part]]
            total = frames[0] * weights[part][:1]
            for j in range(1, sz.taps + 1):
                total = total + frames[j] * weights[part][j : j + 1]
            active.append(total / (1.0 + jnp.exp(-total)))
            for tap in range(sz.taps):
                window[tap][part] = jnp.where(alive, frames[tap + 1], frames[tap])
        retains.append(jnp.exp(-inputs[sz.parts]))
        strengths.append(strength)

    ones = jnp.ones((dk, dk), BF16)

    def summed(products):
        sums = dot(jnp.concatenate([x.astype(BF16) for x in products], axis=0), ones)
        return [sums[i * n : (i + 1) * n] for i in range(len(products))]

    values = active[2 :: sz.parts]
    units = [x for i, x in enumerate(active) if i % sz.parts < 2]
    norms = summed([x * x for x in units])
    units = [x * lax.rsqrt(norm + EPSILON) for x, norm in zip(units, norms)]
    reach = jnp.ones((n, dk), F32)
    keys = []
    from_state, pairs = [], []
    for t in range(T):
        query, key = units[2 * t], units[2 * t + 1]
        reach = reach * retains[t]
        keys = [k * retains[t] for k in keys]
        pairs += [key * k for k in keys]
        keys.append(key)
        pairs += [query * k for k in keys]
        from_state += [reach * key, reach * query]
    mixes = summed(pairs)
    key_mix, read_mix = [], []
    for t in range(T):
        key_mix.append(mixes[:t])
        read_mix.append(mixes[t : 2 * t + 1])
        mixes = mixes[2 * t + 1 :]

    own_lanes = in_block(sz, (n, dk), cut, 0)
    wide = sz.width // dk
    value_cols = []
    for value in values:
        value = over_blocks(sz, jnp.where(own_lanes, value, 0.0))
        value_cols.append(jnp.concatenate([value] * wide, axis=1))
    lane_row = quotient(iota((sz.tile, sz.width), 1), sz.cols)
    own = iota((sz.tile, sz.width), 0) == lane_row
    readouts = [[] for _ in range(T)]

    def widen(value):
        return jnp.concatenate([value] * wide, axis=1)

    for at in range(0, n, sz.tile):
        rows = slice(at, at + sz.tile)
        block = []
        for g in range(at // sz.rows, (at + sz.tile) // sz.rows):
            for r in range(sz.rows):
                if sz.whole_tiles:
                    block.append(came[sz.place_of[g], r * sz.cols : (r + 1) * sz.cols, :])
                else:
                    piece = came[sz.place_of[g], : sz.state_rows, :].astype(F32)
                    block.append(piece[r * sz.cols : (r + 1) * sz.cols])
        seen = dot(
            jnp.concatenate([x[rows] for x in from_state], axis=0).astype(BF16),
            jnp.concatenate(block, axis=0).astype(BF16),
            1,
            1,
        )
        seen = [seen[i * sz.tile : (i + 1) * sz.tile] for i in range(2 * T)]
        writes = []
        for t in range(T):
            target = value_cols[t][rows] - seen[2 * t]
            target = jnp.where(own, target, 0.0)
            for s in range(t):
                target = target - widen(key_mix[t][s][rows]) * writes[s]
            writes.append(strengths[t][rows] * target)
            read = jnp.where(own, seen[2 * t + 1], 0.0)
            for s in range(t + 1):
                read = read + widen(read_mix[t][s][rows]) * writes[s]
            readouts[t].append(read * dk ** (-0.5))
        added = dot(
            jnp.concatenate(writes, axis=0).astype(BF16),
            jnp.concatenate([k[rows] for k in keys], axis=0).astype(BF16),
            0,
            0,
        )
        for i in range(sz.tile):
            part = block[i].astype(F32) * reach[at + i : at + i + 1]
            part = part + added[i * sz.cols : (i + 1) * sz.cols]
            parked[at + i] = part.astype(parked.dtype)
    blocks = [in_block(sz, (n, dk), cut, shift) for shift in range(4)]
    placed = [None] * sz.back_depth
    kept = [None] * sz.back_depth
    for index in range(sz.back_sets):
        shift, slot = index // sz.back_depth, index % sz.back_depth
        if index < T:
            folded = jnp.concatenate(readouts[index], axis=0)
            folded = functools.reduce(
                jnp.add, [folded[:, i * dk : (i + 1) * dk] for i in range(wide)]
            )
            folded = jnp.where(blocks[shift], over_blocks(sz, folded), 0.0)
            value = dot(place[index], folded.astype(BF16))
            placed[slot] = value if placed[slot] is None else placed[slot] + value
        else:
            value = window[(index - T) // sz.parts][(index - T) % sz.parts]
            if shift:
                value = pltpu.roll(value, shift * sz.quarter, 1)
            rest = jnp.zeros((n, dk), F32) if kept[slot] is None else kept[slot]
            kept[slot] = jnp.where(blocks[shift], value, rest)
    kept = [jnp.zeros((n, dk), F32) if value is None else value for value in kept]
    held = dot(place[T - 1], jnp.concatenate(kept, axis=1).astype(BF16))
    for slot in range(sz.back_depth):
        value = held[:, slot * dk : (slot + 1) * dk]
        if placed[slot] is not None:
            value = value + placed[slot]
        back[pl.ds(slot, n, stride=sz.back_depth), :] = value
    for copy in copies:
        copy.wait()
    gate_factor(sz, live, gain, gate, factor)
    for at in range(n):
        to = scalars[0, at]
        if sz.whole_tiles:
            start_row = pl.multiple_of(mod(to, sz.rows) * sz.cols, sz.cols)
            sent[quotient(to, sz.rows), pl.ds(start_row, sz.cols), :] = parked[at]
        else:
            later[pl.ds(pl.multiple_of(to * sz.cols, sz.cols), sz.cols), :] = parked[at]
    for g in range(count):
        p = sz.place_of[g]
        if not sz.whole_tiles:
            sent[p, : sz.state_rows, :] = later[
                p * sz.state_rows : (p + 1) * sz.state_rows, :
            ].astype(BF16)
        sent[p, sz.state_rows :, :] = back[
            g * sz.back_rows : (g + 1) * sz.back_rows, :
        ].astype(BF16)


def unpack(sz, came, h, wanted):
    shape = (sz.back_rows, sz.dk)
    pieces = [
        came[sz.place_of[h * sz.cuts + cut], sz.state_rows :, :].astype(F32)
        for cut in range(sz.cuts)
    ]
    narrow = {}
    for shift in sorted({index // sz.back_depth for index in wanted}):
        value = pieces[0]
        for cut in range(1, sz.cuts):
            value = jnp.where(in_block(sz, shape, cut, shift), pieces[cut], value)
        if shift:
            value = pltpu.roll(value, sz.dk - shift * sz.quarter, 1)
        narrow[shift] = value

    return narrow


def project_kernel(sz, blocks, factor, weight, came, *refs):
    dk = sz.dk
    partials, kept = refs[: blocks - 1], refs[blocks - 1]
    gated = []
    for h in range(sz.heads):
        lanes = slice(h * dk, (h + 1) * dk)
        narrow = unpack(sz, came, h, range(sz.steps))
        total = [narrow[quarter] for quarter in sorted(narrow)]
        spare = sz.read_rows - len(total) * sz.back_rows
        if spare:
            total.append(jnp.zeros((spare, dk), F32))
        total = jnp.concatenate(total, axis=0)
        scaling = lax.rsqrt(jnp.mean(total * total, axis=1, keepdims=True) + EPSILON)
        gated.append(total * scaling * factor[:, lanes])
    gated = jnp.concatenate(gated, axis=1).astype(BF16)
    kept[...] = gated
    for shift in range(1, blocks):
        project(sz, blocks, shift, gated, weight, partials[shift - 1])


def project(sz, blocks, shift, gated, weight, partial):
    columns = weight.shape[1] // blocks
    lanes = slice(None)
    if blocks > 1:
        at = lax.rem(lax.axis_index("head") + shift, blocks) * columns
        lanes = pl.ds(pl.multiple_of(at, LANES), columns)
    result = dot(gated, weight[:, lanes])
    for t in range(sz.steps):
        rows = [result[at : at + 1] for at in (sz.read_at(t, r) for r in range(sz.rows))]
        partial[t] = jnp.concatenate(rows, axis=0).astype(partial.dtype)


def restore_kernel(sz, blocks, gated, weight, came, states, partial, hist):
    project(sz, blocks, 0, gated[...], weight, partial)
    for h in range(sz.heads):
        narrow = unpack(sz, came, h, range(sz.steps, sz.back_sets))
        for tap in range(sz.taps):
            for part in range(sz.parts):
                index = sz.steps + tap * sz.parts + part
                held = narrow[index // sz.back_depth]
                at = index % sz.back_depth
                rows = [held[at + r * sz.back_depth :][:1] for r in range(sz.rows)]
                value = jnp.concatenate(rows, axis=0)
                hist[tap, part, :, h * sz.dk : (h + 1) * sz.dk] = value.astype(BF16)
    kind = BF16 if sz.whole_tiles else F32
    for r in range(sz.rows):
        for h in range(sz.heads):
            cuts = [
                came[sz.place_of[h * sz.cuts + cut], : sz.state_rows, :].astype(kind)[
                    r * sz.cols : (r + 1) * sz.cols
                ]
                for cut in range(sz.cuts)
            ]
            states[r, h] = jnp.concatenate(cuts, axis=0).T.astype(F32)


def vmem():
    return pl.BlockSpec(memory_space=pltpu.VMEM)


def smem():
    return pl.BlockSpec(memory_space=pltpu.SMEM)


def anywhere():
    return pl.BlockSpec(memory_space=pl.ANY)


def in_hbm(value):
    return pltpu.with_memory_space_constraint(value, pltpu.HBM)


def call(body, outs, ins, out_specs, scratch, name):
    return pl.pallas_call(
        body,
        out_shape=outs,
        in_specs=ins,
        out_specs=out_specs,
        scratch_shapes=scratch,
        compiler_params=pltpu.CompilerParams(vmem_limit_bytes=VMEM_LIMIT),
        name=name,
    )


def exchange(sz, pieces):
    return lax.all_to_all(
        pieces, "rep", split_axis=0, concat_axis=0, axis_index_groups=[sz.order], tiled=True
    )


def local(
    group_total,
    head_total,
    states,
    conv_states,
    projected,
    conv_weight,
    decay_input,
    decay_rate,
    beta_logit,
    out_gate,
    norm_gain,
    out_weight,
    destinations,
    live_counts,
):
    sz = Sizes(group_total, states, conv_states, projected)
    n, channels = sz.groups, sz.heads * sz.dk
    shape = jax.ShapeDtypeStruct
    spare_info = round_up(sz.info_rows + sz.info_sets, 8)
    lives = live_counts.T
    arguments = (
        destinations,
        lives,
        decay_rate.reshape(1, sz.heads),
        beta_logit.transpose(1, 2, 0),
        projected.transpose(0, 2, 1, 3),
        conv_states.transpose(1, 2, 0, 3),
        decay_input,
        conv_weight.transpose(1, 0, 2),
        states,
    )
    routes = shape((sz.steps, sz.slots, sz.slots), BF16)
    pieces, pick, place, final, taps = call(
        functools.partial(pack_kernel, sz),
        (
            shape((n, sz.state_rows + sz.info_rows, sz.dk), BF16),
            routes,
            routes,
            shape((8, sz.slots), jnp.int32),
            shape((sz.parts, sz.taps + 1, sz.dk), F32),
        ),
        [anywhere()] * len(arguments),
        (vmem(),) * 5,
        [pltpu.VMEM(x.shape, x.dtype) for x in arguments]
        + [
            pltpu.VMEM((sz.heads, spare_info, sz.dk), F32),
            pltpu.VMEM((3, sz.heads, spare_info, sz.dk), F32),
            pltpu.VMEM((sz.heads, sz.dk), F32),
            pltpu.SemaphoreType.DMA((len(arguments),)),
        ],
        "pack",
    )(*[in_hbm(x) for x in arguments])
    came = exchange(sz, pieces)
    gain = norm_gain.reshape(1, sz.dk)
    stepped, factor = call(
        functools.partial(step_kernel, sz),
        (
            shape((n, sz.state_rows + sz.back_rows, sz.dk), BF16),
            shape((sz.read_rows, channels), F32),
        ),
        [vmem()] * 4 + [anywhere()] * 4,
        (vmem(), vmem()),
        [
            pltpu.SMEM((8, sz.slots), jnp.int32),
            pltpu.VMEM(lives.shape, lives.dtype),
            pltpu.VMEM(gain.shape, F32),
            pltpu.VMEM(out_gate.shape, BF16),
            pltpu.VMEM((round_up(n * sz.info_rows + sz.info_sets, 8), sz.dk), F32),
            pltpu.VMEM((sz.slots, sz.cols, sz.dk), BF16 if sz.whole_tiles else F32),
            pltpu.VMEM((8 if sz.whole_tiles else n * sz.state_rows, sz.dk), F32),
            pltpu.VMEM((round_up(n * sz.back_rows + sz.back_depth, 8), sz.dk), F32),
            pltpu.SemaphoreType.DMA((4,)),
        ],
        "steps",
    )(taps, pick, place, came, final, in_hbm(lives), in_hbm(gain), in_hbm(out_gate))
    back = exchange(sz, stepped)
    width = out_weight.shape[1]
    columns = width // head_total
    blocks = head_total if columns % LANES == 0 else 1
    *partials, gated = call(
        functools.partial(project_kernel, sz, blocks),
        tuple(shape((sz.steps, sz.rows, columns), BF16) for _ in range(1, blocks))
        + (shape((sz.read_rows, channels), BF16),),
        [vmem()] * 3,
        tuple([vmem()] * blocks),
        [],
        "project",
    )(factor, out_weight, back)
    states_out, own, conv_out = call(
        functools.partial(restore_kernel, sz, blocks),
        (
            shape(states.shape, F32),
            shape((sz.steps, sz.rows, width // blocks), F32),
            shape((sz.taps, sz.parts, sz.rows, channels), BF16),
        ),
        [vmem()] * 3,
        (vmem(),) * 3,
        [],
        "restore",
    )(gated, out_weight, back)
    partials = [own, *partials]
    if blocks != head_total:
        mine = lax.axis_index("head")
        partials = [
            lax.dynamic_slice_in_dim(
                partials[0], lax.rem(mine + shift, head_total) * columns, columns, 2
            )
            for shift in range(head_total)
        ]
    total = partials[0]
    for shift in range(1, head_total):
        pairs = [(i, (i + shift) % head_total) for i in range(head_total)]
        passed = lax.ppermute(partials[shift].astype(BF16), "head", pairs)
        total = total + passed.astype(F32)
    return (total.astype(BF16), states_out, conv_out.transpose(2, 0, 1, 3))


def solution(mesh):
    placed = (
        P("rep", "head", None, None),
        P("rep", None, None, "head"),
        P(None, "rep", None, "head"),
        P(None, None, "head"),
        P(None, "rep", "head"),
        P("head"),
        P(None, "rep", "head"),
        P(None, "rep", "head"),
        P(),
        P("head", None),
        P(),
        P(None, "rep"),
    )
    return jax.shard_map(
        functools.partial(local, mesh.shape["rep"], mesh.shape["head"]),
        mesh=mesh,
        in_specs=placed,
        out_specs=(
            P(None, "rep", "head"),
            P("rep", "head", None, None),
            P("rep", None, None, "head"),
        ),
        check_vma=False,
    )
```
